32 devices in a mesh: rep: 2 (over y), tensor: 4 (over z), req: 4 (over x, core).
Axes of the slice: x: 2, y: 2, z: 4, core: 2. Of those that a mesh axis runs over, the one named last changes fastest.
Arguments:
- hidden: bfloat16 [1024, 29568], P(('rep', 'req'), 'tensor'), parts along dimension 0, may hold values from -6 to 6
- down_projection_weight: bfloat16 [29568, 8192], P('tensor', 'req'), may hold values from -0.03125 to 0.03125
- adapter_shrink_weight: bfloat16 [29568, 8, 64], P('tensor'), may hold values from -0.03125 to 0.03125
- adapter_expand_weight: bfloat16 [8, 64, 8192], P(None, None, 'req'), may hold values from -0.75 to 0.75
- adapter_index_per_row: int32 [1024], P(('rep', 'req')), parts along dimension 0, may hold values from 0 to 7, as said below
Outputs:
- projected: bfloat16 [1024, 8192], P(('rep', 'tensor'), 'req'), parts along dimension 0
The draws below stay inside these ranges and needn't reach their ends.
There are 2 independent parts, one for each index of `rep`. The reference program is written for one: setup_inputs(seed, part) draws one part's arguments, and reference() takes and returns one part's arrays. A program takes and returns all parts, laid end to end along the dimension named above; an argument that names none is the same for every part. Nothing has to cross between parts.
Inputs may be any that keep to these rules, and one draw needn't show every extreme that they name: `adapter_index_per_row`: within each aligned block of 128 rows the ids never fall; some row names 0 and some row names 7.
All inputs are finite; a program needn't handle non-finite values.
Results may differ from the reference program's by a relative error of at most 0.012.
Values may be sent and summed in bfloat16 or wider, within the bound.
No kernel may reach another device: no remote copies, remote signals or barrier semaphores. Data moves between devices by JAX's collectives and lax.ppermute only.
A program may use at most 128 MiB of HBM per device.

```python
import jax
import jax.numpy as jnp
from jax import lax

MODEL_WIDTH = 8192
HIDDEN_UNITS = 29568
ADAPTER_RANK = 64
ADAPTER_COUNT = 8
R_DEV = 128
ROWS = 512
N_TENSOR = 4


def draw_adapter_index_per_row(key, part):
    key = jax.random.fold_in(key, 7)
    picked = jax.random.randint(key, (ROWS,), 0, ADAPTER_COUNT, dtype=jnp.int32)
    picked = picked.at[0].set(ADAPTER_COUNT - 1).at[1].set(0)
    return jnp.sort(picked.reshape(-1, R_DEV), axis=1).reshape(-1)


def level_of(key, dims, cuts, low, high):
    level, own = 1.0, jax.random.fold_in(key, 6)
    for axis_at, blocks in cuts:
        heights = jnp.exp(jax.random.uniform(jax.random.fold_in(own, axis_at), (blocks,), jnp.float32, low / len(cuts), high / len(cuts)))
        level = level * jnp.repeat(heights, dims[axis_at] // blocks).reshape([-1 if axis == axis_at else 1 for axis in range(len(dims))])
    return level


def noise(rng, dims, scale, limit, cuts=(), held_as=jnp.bfloat16):
    loudness = level_of(rng, dims, cuts, -0.22, 0.18) if cuts else 1.0
    result = jax.random.normal(rng, dims, jnp.float32) * scale * loudness
    return jnp.minimum(jnp.maximum(result, -limit), limit).astype(held_as)


def setup_inputs(seed: int = 0, part: int = 0) -> dict:
    streams_of = jax.random.split(jax.random.key(seed), 6)
    own_keys = jax.random.split(jax.random.fold_in(streams_of[5], part), 6)
    hidden = noise(own_keys[0], (ROWS, HIDDEN_UNITS), 1.0, 6.0, ((0, 4), (1, 4)))
    down_projection_weight = noise(streams_of[1], (HIDDEN_UNITS, MODEL_WIDTH), HIDDEN_UNITS ** -0.5, 0.03125, ((0, 4), (1, 4)))
    adapter_shrink_weight = noise(streams_of[2], (HIDDEN_UNITS, ADAPTER_COUNT, ADAPTER_RANK), HIDDEN_UNITS ** -0.5, 0.03125, ((0, 4),))
    adapter_expand_weight = noise(streams_of[3], (ADAPTER_COUNT, ADAPTER_RANK, MODEL_WIDTH), ADAPTER_RANK ** -0.5, 0.75, ((2, 4),))
    adapter_index_per_row = draw_adapter_index_per_row(jax.random.fold_in(jax.random.fold_in(streams_of[5], part), 71), part)
    return {"hidden": hidden, "down_projection_weight": down_projection_weight, "adapter_shrink_weight": adapter_shrink_weight, "adapter_expand_weight": adapter_expand_weight, "adapter_index_per_row": adapter_index_per_row}


def reference(hidden, down_projection_weight, adapter_shrink_weight, adapter_expand_weight, adapter_index_per_row):
    block_slice = HIDDEN_UNITS // N_TENSOR
    onehot = (adapter_index_per_row[:, None] == jnp.arange(ADAPTER_COUNT, dtype=jnp.int32)[None, :]).astype(jnp.float32)
    nrows = hidden.shape[0]

    def add_block(carry, index):
        base_acc, shrink_acc = carry
        block_start = (index * block_slice).astype(jnp.int32)
        piece = lax.dynamic_slice_in_dim(hidden, block_start, block_slice, 1)
        weight_rows = lax.dynamic_slice_in_dim(down_projection_weight, block_start, block_slice, 0)
        shrink_matrix_rows = lax.dynamic_slice_in_dim(adapter_shrink_weight, block_start, block_slice, 0).reshape(block_slice, ADAPTER_COUNT * ADAPTER_RANK)
        part_base = jnp.dot(piece, weight_rows, preferred_element_type=jnp.float32).astype(jnp.bfloat16)
        every = jnp.dot(piece, shrink_matrix_rows, preferred_element_type=jnp.float32).reshape(nrows, ADAPTER_COUNT, ADAPTER_RANK)
        part_shrink = jnp.sum(every * onehot[:, :, None], axis=1).astype(jnp.bfloat16)
        part_base, part_shrink = lax.optimization_barrier((part_base, part_shrink))
        return (base_acc + part_base.astype(jnp.float32), shrink_acc + part_shrink.astype(jnp.float32)), None

    start_carry = (jnp.zeros((nrows, MODEL_WIDTH), jnp.float32), jnp.zeros((nrows, ADAPTER_RANK), jnp.float32))
    (base_output, shrink_acc), _ = lax.scan(add_block, start_carry, jnp.arange(N_TENSOR, dtype=jnp.int32))
    shrink = shrink_acc.astype(jnp.bfloat16)
    placed_rows = (shrink[:, None, :] * onehot[:, :, None].astype(jnp.bfloat16)).reshape(-1, ADAPTER_COUNT * ADAPTER_RANK)
    adapter_output = jnp.dot(placed_rows, adapter_expand_weight.reshape(ADAPTER_COUNT * ADAPTER_RANK, MODEL_WIDTH), preferred_element_type=jnp.float32)
    return (base_output + adapter_output).astype(jnp.bfloat16)
```

```python
import functools

import jax
import jax.numpy as jnp
from jax import lax
from jax.experimental import pallas as pl
from jax.experimental.pallas import tpu as pltpu
from jax.sharding import PartitionSpec as P

LANES = 128
DEPTH = 1024
SLOTS = 3
MIB = 1 << 20


def in_vmem():
    return pl.BlockSpec(memory_space=pltpu.VMEM)


def in_hbm():
    return pl.BlockSpec(memory_space=pl.ANY)


def padded(units):
    return (units // LANES + 1) * LANES


def turn_kernel(starts, hidden_ref, ids_ref, whole_ref, *chunk_refs):
    units, rows = hidden_ref.shape
    full = units // LANES
    for block in range(full + 1):
        if block < full:
            tile = hidden_ref[block * LANES : (block + 1) * LANES, :]
        else:
            ids = jnp.broadcast_to(
                ids_ref[...].astype(jnp.float32).astype(jnp.bfloat16),
                ((full + 1) * LANES - units, rows),
            )
            tile = jnp.concatenate([hidden_ref[full * LANES :, :], ids], axis=0)
        turned = tile.T
        at = slice(block * LANES, (block + 1) * LANES)
        whole_ref[:, at] = turned
        for (first, count), chunk_ref in zip(starts, chunk_refs):
            chunk_ref[:, at] = turned[first : first + count]


def emit(acc_ref, ids, keep_first, send_ref, keep_ref, width, adapters):
    rows = send_ref.shape[0]
    wide = acc_ref.shape[1] - width
    rank = wide // adapters
    column = lax.broadcasted_iota(jnp.int32, (2 * rows, wide), 1) // rank
    picked = jnp.where(column.astype(jnp.float32) == ids, acc_ref[:, width:], 0.0)
    tile = picked[:, :LANES]
    for at in range(LANES, wide, LANES):
        tile = tile + picked[:, at : at + LANES]
    tile = tile + pltpu.roll(tile, rank, 1)
    lane = lax.broadcasted_iota(jnp.int32, tile.shape, 1)
    tile = jnp.where(lane < rank, tile, ids).astype(jnp.bfloat16)
    first, second = tile[:rows], tile[rows:]
    send_ref[:, width:] = jnp.where(keep_first, second, first)
    keep_ref[:, width:] = jnp.where(keep_first, first, second)
    for at in range(0, width, 512):
        cols = slice(at, at + 512)
        first = acc_ref[:rows, cols].astype(jnp.bfloat16)
        second = acc_ref[rows:, cols].astype(jnp.bfloat16)
        send_ref[:, cols] = jnp.where(keep_first, second, first)
        keep_ref[:, cols] = jnp.where(keep_first, first, second)


def keeps_first():
    return lax.rem(lax.axis_index("req"), 2) == lax.rem(lax.axis_index("tensor"), 2)


def row_ids(refs, units):
    ids = jnp.concatenate([ref[:, units : units + 1] for ref in refs], axis=0)
    return ids.astype(jnp.float32)


def add_depth(refs, at, count, both_ref, acc_ref):
    rows = jnp.concatenate([ref[:, pl.ds(at, count)] for ref in refs], axis=0)
    acc_ref[...] += jnp.dot(
        rows, both_ref[pl.ds(at, count), :], preferred_element_type=jnp.float32
    )


def first_kernel(
    adapters,
    own_ref,
    other_ref,
    w_hbm,
    s_hbm,
    send_ref,
    keep_ref,
    both_ref,
    acc_ref,
    s_ref,
    s_tail,
    w_sems,
    s_sems,
):
    units, width = w_hbm.shape
    steps = units // DEPTH
    tail = units - steps * DEPTH
    slots = s_ref.shape[0]
    refs = (own_ref, other_ref)

    def w_copy(step, count=DEPTH):
        rows = pl.ds(step * DEPTH, count)
        return pltpu.make_async_copy(
            w_hbm.at[rows], both_ref.at[rows, pl.ds(0, width)], w_sems.at[step]
        )

    def s_copy(step):
        slot = lax.rem(step, slots)
        return pltpu.make_async_copy(
            s_hbm.at[:, pl.ds(step * DEPTH, DEPTH)], s_ref.at[slot], s_sems.at[slot]
        )

    s_tail_copy = pltpu.make_async_copy(
        s_hbm.at[:, pl.ds(steps * DEPTH, tail)], s_tail, s_sems.at[slots]
    )
    for step in range(steps):
        w_copy(step).start()
        if step < slots:
            s_copy(step).start()
    w_copy(steps, tail).start()
    s_tail_copy.start()
    acc_ref[...] = jnp.zeros_like(acc_ref)

    def take(step, carry):
        at = pl.multiple_of(step * DEPTH, DEPTH)
        s_copy(step).wait()
        both_ref[pl.ds(at, DEPTH), width:] = s_ref[lax.rem(step, slots)].T

        @pl.when(step + slots < steps)
        def _():
            s_copy(step + slots).start()

        w_copy(step).wait()
        add_depth(refs, at, DEPTH, both_ref, acc_ref)
        return carry

    lax.fori_loop(0, steps, take, 0)
    s_tail_copy.wait()
    both_ref[pl.ds(steps * DEPTH, tail), width:] = s_tail[...].T
    w_copy(steps, tail).wait()
    add_depth(refs, steps * DEPTH, tail, both_ref, acc_ref)
    emit(acc_ref, row_ids(refs, units), keeps_first(), send_ref, keep_ref, width, adapters)


def later_kernel(adapters, width, own_ref, other_ref, both_ref, send_ref, keep_ref, acc_ref):
    units = both_ref.shape[0]
    steps = units // DEPTH
    tail = units - steps * DEPTH
    refs = (own_ref, other_ref)
    acc_ref[...] = jnp.zeros_like(acc_ref)

    def step_of(step, carry):
        add_depth(refs, pl.multiple_of(step * DEPTH, DEPTH), DEPTH, both_ref, acc_ref)
        return carry

    lax.fori_loop(0, steps, step_of, 0)
    if tail:
        add_depth(refs, steps * DEPTH, tail, both_ref, acc_ref)
    emit(acc_ref, row_ids(refs, units), keeps_first(), send_ref, keep_ref, width, adapters)


def last_kernel(n_tensor, adapters, far, expand_ref, *refs):
    out_ref = refs[-1]
    near_sum, near_got = refs[0], refs[1]
    far_sums, far_gots = refs[2 : 2 + far], refs[2 + far : 2 + 2 * far]
    wide, width = expand_ref.shape
    rank = wide // adapters
    is_near = lax.axis_index("tensor") // 2 == lax.axis_index("req") // 2

    def total(first, count, far_at, cols):
        rows = slice(first, first + count)
        near = near_sum[rows, cols].astype(jnp.float32) + near_got[rows, cols].astype(jnp.float32)
        away = far_sums[far_at][:, cols].astype(jnp.float32) + far_gots[far_at][:, cols].astype(
            jnp.float32
        )
        return jnp.where(is_near, near, away)

    def whole(cols):
        parts, first = [], 0
        for at, ref in enumerate(far_sums):
            parts.append(total(first, ref.shape[0], at, cols))
            first += ref.shape[0]
        return jnp.concatenate(parts, axis=0)

    small = whole(slice(width, width + LANES))
    ids = small[:, rank : rank + 1] * (1.0 / n_tensor)
    lane = lax.broadcasted_iota(jnp.int32, small.shape, 1)
    shrink = jnp.where(lane < rank, small, 0.0)
    shrink = shrink + pltpu.roll(shrink, rank, 1)
    spread = jnp.concatenate([shrink] * (wide // LANES), axis=1)
    column = lax.broadcasted_iota(jnp.int32, spread.shape, 1) // rank
    placed = jnp.where(column.astype(jnp.float32) == ids, spread, 0.0).astype(jnp.bfloat16)
    for at in range(0, width, 512):
        cols = slice(at, at + 512)
        adapter = jnp.dot(placed, expand_ref[:, cols], preferred_element_type=jnp.float32)
        out_ref[:, cols] = (whole(cols) + adapter).astype(out_ref.dtype)


def paired(n_tensor, n_req, parts, hidden, weight, shrink, expand, ids):
    rows, units = hidden.shape
    width = weight.shape[1]
    adapters, rank = shrink.shape[1:]
    wide = adapters * rank
    room = padded(units)
    payload = width + LANES
    chunk = rows // parts
    bf16 = jnp.bfloat16

    def params(mib):
        return pltpu.CompilerParams(vmem_limit_bytes=mib * MIB)

    quick = pl.CostEstimate(flops=1, bytes_accessed=1, transcendentals=0)

    starts = [(at * chunk, chunk) for at in range(parts)]
    turned = pl.pallas_call(
        functools.partial(turn_kernel, starts),
        out_shape=[jax.ShapeDtypeStruct((rows, room), bf16)]
        + [jax.ShapeDtypeStruct((chunk, room), bf16)] * parts,
        in_specs=[in_vmem(), in_vmem()],
        out_specs=[in_vmem()] * (1 + parts),
        compiler_params=params(2),
        name="turn",
    )(hidden.T, ids.reshape(1, rows))
    own, chunks = turned[0], turned[1:]

    def left(array):
        return pltpu.with_memory_space_constraint(array, pltpu.HBM)

    across = [(i, i ^ 2) for i in range(n_req)]
    beside = [(i, i ^ 1) for i in range(n_req)]
    next_z = [(i, i ^ 1) for i in range(n_tensor)]
    to_near, to_far = [], []
    for t in range(n_tensor):
        for r in range(n_req):
            hop = (t * n_req + r, (t ^ 2) * n_req + r)
            (to_far if t // 2 == r // 2 else to_near).append(hop)

    direct = [lax.ppermute(part, "req", across) for part in chunks]
    other = lax.ppermute(own, "req", beside)

    shrink_rows = shrink.transpose(1, 2, 0).reshape(wide, units)
    near_send, near_keep, both = pl.pallas_call(
        functools.partial(first_kernel, adapters),
        out_shape=[
            jax.ShapeDtypeStruct((rows, payload), bf16),
            jax.ShapeDtypeStruct((rows, payload), bf16),
            pltpu.VMEM((units, width + wide), bf16),
        ],
        in_specs=[in_vmem(), in_vmem(), in_hbm(), in_hbm()],
        out_specs=[in_vmem()] * 3,
        scratch_shapes=[
            pltpu.VMEM((2 * rows, width + wide), jnp.float32),
            pltpu.VMEM((SLOTS, wide, DEPTH), bf16),
            pltpu.VMEM((wide, units % DEPTH), bf16),
            pltpu.SemaphoreType.DMA((units // DEPTH + 1,)),
            pltpu.SemaphoreType.DMA((SLOTS + 1,)),
        ],
        compiler_params=params(8),
        cost_estimate=quick,
        name="first",
    )(own, other, left(weight), left(shrink_rows))

    def halve(send, keep, hops):
        got = lax.ppermute(send, "tensor", next_z)
        total = (keep.astype(jnp.float32) + got.astype(jnp.float32)).astype(bf16)
        return total, lax.ppermute(total, ("tensor", "req"), hops)

    direct[0], near_send = lax.optimization_barrier((direct[0], near_send))
    near_sum, near_got = halve(near_send, near_keep, to_near)

    far_sums, far_gots = [], []
    for at in range(parts):
        part = direct[at]
        passed = lax.ppermute(part, "req", beside)
        send, keep = pl.pallas_call(
            functools.partial(later_kernel, adapters, width),
            out_shape=[jax.ShapeDtypeStruct((chunk, payload), bf16)] * 2,
            in_specs=[in_vmem()] * 3,
            out_specs=[in_vmem()] * 2,
            scratch_shapes=[pltpu.VMEM((2 * chunk, width + wide), jnp.float32)],
            compiler_params=params(3),
            cost_estimate=quick,
            name="later",
        )(part, passed, both)
        if at + 1 < parts:
            direct[at + 1], send = lax.optimization_barrier((direct[at + 1], send))
        total, got = halve(send, keep, to_far)
        far_sums.append(total)
        far_gots.append(got)

    return pl.pallas_call(
        functools.partial(last_kernel, n_tensor, adapters, parts),
        out_shape=jax.ShapeDtypeStruct((rows, width), bf16),
        in_specs=[in_vmem()] * (3 + 2 * parts),
        out_specs=in_vmem(),
        compiler_params=params(8),
        name="last",
    )(expand.reshape(wide, width), near_sum, near_got, *far_sums, *far_gots)


def gathered(hidden, weight, shrink, expand, ids):
    rows, units = hidden.shape
    adapters, rank = shrink.shape[1:]
    width = weight.shape[1]
    columns = jnp.arange(adapters, dtype=jnp.int32)[None, :]
    onehot = (ids[:, None] == columns).astype(jnp.float32)
    every = jnp.dot(
        hidden, shrink.reshape(units, adapters * rank), preferred_element_type=jnp.float32
    )
    part = jnp.sum(every.reshape(rows, adapters, rank) * onehot[:, :, None], axis=1)
    all_ids = lax.all_gather(ids, "req", axis=0, tiled=True)
    base = jnp.dot(
        lax.all_gather(hidden, "req", axis=0, tiled=True),
        weight,
        preferred_element_type=jnp.float32,
    )
    base = lax.psum_scatter(
        base.astype(jnp.bfloat16), "tensor", scatter_dimension=0, tiled=True
    ).astype(jnp.float32)
    shrunk = lax.all_gather(
        lax.psum(part.astype(jnp.bfloat16), "tensor"), "req", axis=0, tiled=True
    )
    mine = base.shape[0]
    first = lax.axis_index("tensor") * mine
    shrunk = lax.dynamic_slice_in_dim(shrunk, first, mine, 0)
    mask = lax.dynamic_slice_in_dim(all_ids, first, mine, 0)[:, None] == columns
    placed = (shrunk[:, None, :] * mask.astype(jnp.bfloat16)[:, :, None]).reshape(
        mine, adapters * rank
    )
    adapter = jnp.dot(
        placed, expand.reshape(adapters * rank, width), preferred_element_type=jnp.float32
    )
    return (base + adapter).astype(jnp.bfloat16)


def solution(mesh):
    n_tensor, n_req = mesh.shape["tensor"], mesh.shape["req"]
    if n_tensor == 4 and n_req == 4:
        on_device = functools.partial(paired, n_tensor, n_req, 4)
    else:
        on_device = gathered
    placed = (
        P(("rep", "req"), "tensor"),
        P("tensor", "req"),
        P("tensor", None, None),
        P(None, None, "req"),
        P(("rep", "req")),
    )
    return jax.shard_map(
        on_device,
        mesh=mesh,
        in_specs=placed,
        out_specs=P(("rep", "tensor"), "req"),
        check_vma=False,
    )
```

```python
import functools

import jax
import jax.numpy as jnp
from jax import lax
from jax.experimental import pallas as pl
from jax.experimental.pallas import tpu as pltpu
from jax.sharding import PartitionSpec as P

LANES = 128
PANEL = 512
DEPTH = 1024
MIB = 1 << 20


def in_vmem():
    return pl.BlockSpec(memory_space=pltpu.VMEM)


def in_hbm():
    return pl.BlockSpec(memory_space=pltpu.HBM)


def left(array):
    return pltpu.with_memory_space_constraint(array, pltpu.HBM)


def turn_kernel(starts, hidden_ref, ids_ref, *chunk_refs):
    units, rows = hidden_ref.shape
    full = units // LANES
    for block in range(full + 1):
        if block < full:
            tile = hidden_ref[block * LANES : (block + 1) * LANES, :]
        else:
            ids = jnp.broadcast_to(
                ids_ref[...].astype(jnp.float32).astype(jnp.bfloat16),
                ((full + 1) * LANES - units, rows),
            )
            tile = jnp.concatenate([hidden_ref[full * LANES :, :], ids], axis=0)
        turned = tile.T
        at = slice(block * LANES, (block + 1) * LANES)
        for first, chunk_ref in zip(starts, chunk_refs):
            chunk_ref[:, at] = turned[first : first + chunk_ref.shape[0]]


def keeps_first():
    return lax.rem(lax.axis_index("req"), 2) == lax.rem(lax.axis_index("tensor"), 2)


def part_rows(value, keep_first, cols, send_ref, keep_ref):
    rows = send_ref.shape[0]
    value = value.astype(send_ref.dtype)
    first, second = value[:rows], value[rows:]
    send_ref[:, cols] = jnp.where(keep_first, second, first)
    keep_ref[:, cols] = jnp.where(keep_first, first, second)


def base_panel(panel, refs, panel_ref, send_ref, keep_ref):
    cols = slice(panel * PANEL, (panel + 1) * PANEL)
    rows = jnp.concatenate([ref[...] for ref in refs], axis=0)
    value = jnp.dot(rows, panel_ref[...], preferred_element_type=jnp.float32)
    part_rows(value, keeps_first(), cols, send_ref, keep_ref)


def shrink_panel(adapters, units, refs, panel_ref, send_ref, keep_ref):
    width = send_ref.shape[1] - LANES
    wide = panel_ref.shape[1]
    rank = wide // adapters
    rows = jnp.concatenate([ref[...] for ref in refs], axis=0)
    every = jnp.dot(rows, panel_ref[...], preferred_element_type=jnp.float32)
    ids = jnp.concatenate([ref[:, units : units + 1] for ref in refs], axis=0)
    ids = ids.astype(jnp.float32)
    column = lax.broadcasted_iota(jnp.int32, every.shape, 1) // rank
    picked = jnp.where(column.astype(jnp.float32) == ids, every, 0.0)
    tile = picked[:, :LANES]
    for at in range(LANES, wide, LANES):
        tile = tile + picked[:, at : at + LANES]
    tile = tile + pltpu.roll(tile, rank, 1)
    lane = lax.broadcasted_iota(jnp.int32, tile.shape, 1)
    tile = jnp.where(lane < rank, tile, ids)
    part_rows(tile, keeps_first(), slice(width, width + LANES), send_ref, keep_ref)


def first_kernel(adapters, own_ref, other_ref, w_hbm, s_hbm, send_ref, keep_ref, *refs):
    *panel_refs, spread_ref, s_ref, w_sems, s_sem = refs
    units = w_hbm.shape[0]
    rows = (own_ref, other_ref)
    copies = [
        pltpu.make_async_copy(
            w_hbm.at[:, pl.ds(panel * PANEL, PANEL)],
            panel_ref.at[pl.ds(0, units), :],
            w_sems.at[panel],
        )
        for panel, panel_ref in enumerate(panel_refs)
    ]
    s_copy = pltpu.make_async_copy(s_hbm, s_ref, s_sem)
    s_copy.start()
    for copy in copies:
        copy.start()
    for ref in (spread_ref, *panel_refs):
        ref[units:, :] = jnp.zeros_like(ref[units:, :])
    s_copy.wait()
    for at in range(0, units, DEPTH):
        to = min(at + DEPTH, units)
        spread_ref[at:to, :] = s_ref[:, at:to].T
    shrink_panel(adapters, units, rows, spread_ref, send_ref, keep_ref)
    for panel, panel_ref in enumerate(panel_refs):
        copies[panel].wait()
        base_panel(panel, rows, panel_ref, send_ref, keep_ref)


def later_kernel(adapters, units, own_ref, other_ref, *refs):
    *panel_refs, spread_ref, send_ref, keep_ref = refs
    rows = (own_ref, other_ref)
    shrink_panel(adapters, units, rows, spread_ref, send_ref, keep_ref)
    for panel, panel_ref in enumerate(panel_refs):
        base_panel(panel, rows, panel_ref, send_ref, keep_ref)


def add_kernel(first_ref, second_ref, out_ref):
    total = first_ref[...].astype(jnp.float32) + second_ref[...].astype(jnp.float32)
    out_ref[...] = total.astype(out_ref.dtype)


def last_kernel(n_tensor, adapters, near, far, expand_ref, *refs):
    out_ref = refs[-1]
    near_sums, near_gots = refs[:near], refs[near : 2 * near]
    far_sums, far_gots = refs[2 * near : 2 * near + far], refs[2 * near + far : -1]
    wide, width = expand_ref.shape
    rank = wide // adapters
    is_near = lax.axis_index("tensor") // 2 == lax.axis_index("req") // 2

    def total(sums, gots, cols):
        parts = [
            kept[:, cols].astype(jnp.float32) + got[:, cols].astype(jnp.float32)
            for kept, got in zip(sums, gots)
        ]
        return jnp.concatenate(parts, axis=0)

    def whole(cols):
        return jnp.where(
            is_near, total(near_sums, near_gots, cols), total(far_sums, far_gots, cols)
        )

    small = whole(slice(width, width + LANES))
    ids = small[:, rank : rank + 1] * (1.0 / n_tensor)
    lane = lax.broadcasted_iota(jnp.int32, small.shape, 1)
    shrink = jnp.where(lane < rank, small, 0.0)
    shrink = shrink + pltpu.roll(shrink, rank, 1)
    spread = jnp.concatenate([shrink] * (wide // LANES), axis=1)
    column = lax.broadcasted_iota(jnp.int32, spread.shape, 1) // rank
    placed = jnp.where(column.astype(jnp.float32) == ids, spread, 0.0).astype(jnp.bfloat16)
    for at in range(0, width, PANEL):
        cols = slice(at, at + PANEL)
        adapter = jnp.dot(placed, expand_ref[:, cols], preferred_element_type=jnp.float32)
        out_ref[:, cols] = (whole(cols) + adapter).astype(out_ref.dtype)


def paired(n_tensor, n_req, hidden, weight, shrink, expand, ids):
    rows, units = hidden.shape
    width = weight.shape[1]
    adapters, rank = shrink.shape[1:]
    wide = adapters * rank
    room = (units // LANES + 1) * LANES
    payload = width + LANES
    bf16 = jnp.bfloat16
    half, quarter = rows // 2, rows // 4
    quick = pl.CostEstimate(flops=1, bytes_accessed=1, transcendentals=0)

    def params(mib):
        return pltpu.CompilerParams(vmem_limit_bytes=mib * MIB)

    starts, counts = (0, half, half, half + quarter), (half, half, quarter, quarter)
    own_a, own_b, own_c, own_d = pl.pallas_call(
        functools.partial(turn_kernel, starts),
        out_shape=[jax.ShapeDtypeStruct((count, room), bf16) for count in counts],
        in_specs=[in_vmem(), in_vmem()],
        out_specs=[in_vmem()] * 4,
        compiler_params=params(2),
        name="turn",
    )(hidden.T, ids.reshape(1, rows))

    across = [(i, i ^ 2) for i in range(n_req)]
    beside = [(i, i ^ 1) for i in range(n_req)]
    next_z = [(i, i ^ 1) for i in range(n_tensor)]
    to_near, to_far = [], []
    for t in range(n_tensor):
        for r in range(n_req):
            hop = (t * n_req + r, (t ^ 2) * n_req + r)
            (to_far if t // 2 == r // 2 else to_near).append(hop)

    def over_x(part):
        return lax.ppermute(part, "req", across)

    def over_core(part):
        return lax.ppermute(part, "req", beside)

    def first_hop(send, keep):
        got = lax.ppermute(send, "tensor", next_z)
        return pl.pallas_call(
            add_kernel,
            out_shape=jax.ShapeDtypeStruct(keep.shape, bf16),
            in_specs=[in_vmem()] * 2,
            out_specs=in_vmem(),
            compiler_params=params(10),
            cost_estimate=quick,
            name="add",
        )(keep, got)

    def second_hop(total, hops):
        return lax.ppermute(total, ("tensor", "req"), hops)

    def product(own, other, both):
        count = own.shape[0]
        return pl.pallas_call(
            functools.partial(later_kernel, adapters, units),
            out_shape=[jax.ShapeDtypeStruct((count, payload), bf16)] * 2,
            in_specs=[in_vmem()] * (2 + len(both)),
            out_specs=[in_vmem()] * 2,
            compiler_params=params(10),
            cost_estimate=quick,
            name="later",
        )(own, other, *both)

    other_a = over_core(own_a)
    direct_a = over_x(own_a)
    other_b = over_core(own_b)

    shrink_rows = shrink.transpose(1, 2, 0).reshape(wide, units)
    send_a, keep_a, *both = pl.pallas_call(
        functools.partial(first_kernel, adapters),
        out_shape=[
            jax.ShapeDtypeStruct((half, payload), bf16),
            jax.ShapeDtypeStruct((half, payload), bf16),
            *[pltpu.VMEM((room, PANEL), bf16)] * (width // PANEL),
            pltpu.VMEM((room, wide), bf16),
        ],
        in_specs=[in_vmem(), in_vmem(), in_hbm(), in_hbm()],
        out_specs=[in_vmem()] * (3 + width // PANEL),
        scratch_shapes=[
            pltpu.VMEM((wide, units), bf16),
            pltpu.SemaphoreType.DMA((width // PANEL,)),
            pltpu.SemaphoreType.DMA,
        ],
        compiler_params=params(10),
        cost_estimate=quick,
        name="first",
    )(own_a, other_a, left(weight), left(shrink_rows))
    send_b, keep_b = product(own_b, other_b, both)

    direct_a, own_c, send_b = lax.optimization_barrier((direct_a, own_c, send_b))
    direct_c = over_x(own_c)
    sent_a, kept_a = product(direct_a, over_core(direct_a), both)

    near = [first_hop(send_a, keep_a), first_hop(send_b, keep_b)]
    direct_c, own_d, near, sent_a = lax.optimization_barrier((direct_c, own_d, near, sent_a))
    direct_d = over_x(own_d)
    passed_c = over_core(direct_c)
    far = [first_hop(sent_a, kept_a)]
    direct_c, far[0] = lax.optimization_barrier((direct_c, far[0]))
    sent_c, kept_c = product(direct_c, passed_c, both)

    direct_d, sent_c = lax.optimization_barrier((direct_d, sent_c))
    passed_d = over_core(direct_d)
    far.append(first_hop(sent_c, kept_c))
    direct_d, far[1] = lax.optimization_barrier((direct_d, far[1]))
    sent_d, kept_d = product(direct_d, passed_d, both)
    far.append(first_hop(sent_d, kept_d))

    near = [(total, second_hop(total, to_near)) for total in near]
    far = [(total, second_hop(total, to_far)) for total in far]
    pieces = [total for total, _ in near] + [got for _, got in near]
    pieces += [total for total, _ in far] + [got for _, got in far]
    return pl.pallas_call(
        functools.partial(last_kernel, n_tensor, adapters, len(near), len(far)),
        out_shape=jax.ShapeDtypeStruct((rows, width), bf16),
        in_specs=[in_vmem()] * (1 + len(pieces)),
        out_specs=in_vmem(),
        compiler_params=params(8),
        name="last",
    )(expand.reshape(wide, width), *pieces)


def gathered(hidden, weight, shrink, expand, ids):
    rows, units = hidden.shape
    adapters, rank = shrink.shape[1:]
    width = weight.shape[1]
    columns = jnp.arange(adapters, dtype=jnp.int32)[None, :]
    onehot = (ids[:, None] == columns).astype(jnp.float32)
    every = jnp.dot(
        hidden, shrink.reshape(units, adapters * rank), preferred_element_type=jnp.float32
    )
    part = jnp.sum(every.reshape(rows, adapters, rank) * onehot[:, :, None], axis=1)
    all_ids = lax.all_gather(ids, "req", axis=0, tiled=True)
    base = jnp.dot(
        lax.all_gather(hidden, "req", axis=0, tiled=True),
        weight,
        preferred_element_type=jnp.float32,
    )
    base = lax.psum_scatter(
        base.astype(jnp.bfloat16), "tensor", scatter_dimension=0, tiled=True
    ).astype(jnp.float32)
    shrunk = lax.all_gather(
        lax.psum(part.astype(jnp.bfloat16), "tensor"), "req", axis=0, tiled=True
    )
    mine = base.shape[0]
    first = lax.axis_index("tensor") * mine
    shrunk = lax.dynamic_slice_in_dim(shrunk, first, mine, 0)
    mask = lax.dynamic_slice_in_dim(all_ids, first, mine, 0)[:, None] == columns
    placed = (shrunk[:, None, :] * mask.astype(jnp.bfloat16)[:, :, None]).reshape(
        mine, adapters * rank
    )
    adapter = jnp.dot(
        placed, expand.reshape(adapters * rank, width), preferred_element_type=jnp.float32
    )
    return (base + adapter).astype(jnp.bfloat16)


def solution(mesh):
    n_tensor, n_req = mesh.shape["tensor"], mesh.shape["req"]
    if n_tensor == 4 and n_req == 4:
        on_device = functools.partial(paired, n_tensor, n_req)
    else:
        on_device = gathered
    placed = (
        P(("rep", "req"), "tensor"),
        P("tensor", "req"),
        P("tensor", None, None),
        P(None, None, "req"),
        P(("rep", "req")),
    )
    return jax.shard_map(
        on_device,
        mesh=mesh,
        in_specs=placed,
        out_specs=P(("rep", "tensor"), "req"),
        check_vma=False,
    )
```

```python
import functools

import jax
import jax.numpy as jnp
from jax import lax
from jax.experimental import pallas as pl
from jax.experimental.pallas import tpu as pltpu
from jax.sharding import PartitionSpec as P

LANES = 128
PANEL = 512
DEPTH = 1024
TURN = 15
PIECES = (32, 32, 32, 32)
MIB = 1 << 20


def in_vmem():
    return pl.BlockSpec(memory_space=pltpu.VMEM)


def in_hbm():
    return pl.BlockSpec(memory_space=pltpu.HBM)


def left(array):
    return pltpu.with_memory_space_constraint(array, pltpu.HBM)


def turn_kernel(starts, hidden_hbm, ids_hbm, own_ref, *refs):
    *piece_refs, hidden_ref, ids_ref, sems = refs
    units, rows = hidden_hbm.shape
    full = units // LANES
    stops = [at * LANES for at in range(0, full, TURN)] + [units]
    copies = [
        pltpu.make_async_copy(
            hidden_hbm.at[pl.ds(at, to - at)], hidden_ref.at[pl.ds(at, to - at)], sems.at[step]
        )
        for step, (at, to) in enumerate(zip(stops, stops[1:]))
    ]
    ids_copy = pltpu.make_async_copy(ids_hbm, ids_ref, sems.at[len(copies)])
    for copy in copies:
        copy.start()
    ids_copy.start()
    for step, copy in enumerate(copies):
        copy.wait()
        last = step == len(copies) - 1
        if last:
            ids_copy.wait()
        for block in range(stops[step] // LANES, full + 1 if last else stops[step + 1] // LANES):
            if block < full:
                tile = hidden_ref[block * LANES : (block + 1) * LANES, :]
            else:
                ids = jnp.broadcast_to(
                    ids_ref[...].astype(jnp.float32).astype(jnp.bfloat16),
                    ((full + 1) * LANES - units, rows),
                )
                tile = jnp.concatenate([hidden_ref[full * LANES :, :], ids], axis=0)
            turned = tile.T
            at = slice(block * LANES, (block + 1) * LANES)
            own_ref[:, at] = turned
            for first, piece_ref in zip(starts, piece_refs):
                piece_ref[:, at] = turned[first : first + piece_ref.shape[0]]


def load_kernel(w_hbm, s_hbm, token_ref, *refs):
    *panel_refs, spread_ref, s_ref, w_sems, s_sem = refs
    units = w_hbm.shape[0]
    copies = [
        pltpu.make_async_copy(
            w_hbm.at[:, pl.ds(panel * PANEL, PANEL)],
            panel_ref.at[pl.ds(0, units), :],
            w_sems.at[panel],
        )
        for panel, panel_ref in enumerate(panel_refs)
    ]
    s_copy = pltpu.make_async_copy(s_hbm, s_ref, s_sem)
    s_copy.start()
    for copy in copies:
        copy.start()
    token_ref[...] = jnp.zeros_like(token_ref)
    for ref in (spread_ref, *panel_refs):
        ref[units:, :] = jnp.zeros_like(ref[units:, :])
    s_copy.wait()
    for at in range(0, units, DEPTH):
        to = min(at + DEPTH, units)
        spread_ref[at:to, :] = s_ref[:, at:to].T
    for copy in copies:
        copy.wait()


def part_rows(value, cols, send_ref, keep_ref):
    rows = send_ref.shape[0] // 2
    keep_first = lax.rem(lax.axis_index("req"), 2) == lax.rem(lax.axis_index("tensor"), 2)
    value = value.astype(send_ref.dtype)
    for half in range(2):
        first = value[(2 * half) * rows : (2 * half + 1) * rows]
        second = value[(2 * half + 1) * rows : (2 * half + 2) * rows]
        at = slice(half * rows, (half + 1) * rows)
        send_ref[at, cols] = jnp.where(keep_first, second, first)
        keep_ref[at, cols] = jnp.where(keep_first, first, second)


def product_kernel(
    adapters, units, at, _, own_ref, other_ref, direct_ref, passed_ref, *refs
):
    *panel_refs, spread_ref, send_ref, keep_ref = refs
    rows = direct_ref.shape[0]
    width = send_ref.shape[1] - LANES
    wide = spread_ref.shape[1]
    rank = wide // adapters

    def pieces(cols):
        near = [ref[at : at + rows, cols] for ref in (own_ref, other_ref)]
        far = [ref[:, cols] for ref in (direct_ref, passed_ref)]
        return jnp.concatenate(near + far, axis=0)

    every = jnp.dot(pieces(slice(None)), spread_ref[...], preferred_element_type=jnp.float32)
    ids = pieces(slice(units, units + 1)).astype(jnp.float32)
    column = lax.broadcasted_iota(jnp.int32, every.shape, 1) // rank
    picked = jnp.where(column.astype(jnp.float32) == ids, every, 0.0)
    tile = picked[:, :LANES]
    for lane in range(LANES, wide, LANES):
        tile = tile + picked[:, lane : lane + LANES]
    tile = tile + pltpu.roll(tile, rank, 1)
    lane = lax.broadcasted_iota(jnp.int32, tile.shape, 1)
    tile = jnp.where(lane < rank, tile, ids)
    part_rows(tile, slice(width, width + LANES), send_ref, keep_ref)

    for panel, panel_ref in enumerate(panel_refs):
        value = jnp.dot(
            pieces(slice(None)), panel_ref[...], preferred_element_type=jnp.float32
        )
        part_rows(value, slice(panel * PANEL, (panel + 1) * PANEL), send_ref, keep_ref)


def add_kernel(first_ref, second_ref, send_ref, keep_ref):
    rows = send_ref.shape[0]
    keep_near = lax.axis_index("tensor") // 2 == lax.axis_index("req") // 2

    def total(at):
        cut = slice(at, at + rows)
        value = first_ref[cut].astype(jnp.float32) + second_ref[cut].astype(jnp.float32)
        return value.astype(send_ref.dtype)

    near, far = total(0), total(rows)
    send_ref[...] = jnp.where(keep_near, far, near)
    keep_ref[...] = jnp.where(keep_near, near, far)


def last_kernel(n_tensor, adapters, expand_ref, *refs):
    out_ref = refs[-1]
    count = (len(refs) - 1) // 2
    kept, got = refs[:count], refs[count:-1]
    wide, width = expand_ref.shape
    rank = wide // adapters

    def whole(cols):
        parts = [
            first[:, cols].astype(jnp.float32) + second[:, cols].astype(jnp.float32)
            for first, second in zip(kept, got)
        ]
        return jnp.concatenate(parts, axis=0)

    small = whole(slice(width, width + LANES))
    ids = small[:, rank : rank + 1] * (1.0 / n_tensor)
    lane = lax.broadcasted_iota(jnp.int32, small.shape, 1)
    shrink = jnp.where(lane < rank, small, 0.0)
    shrink = shrink + pltpu.roll(shrink, rank, 1)
    spread = jnp.concatenate([shrink] * (wide // LANES), axis=1)
    column = lax.broadcasted_iota(jnp.int32, spread.shape, 1) // rank
    placed = jnp.where(column.astype(jnp.float32) == ids, spread, 0.0).astype(jnp.bfloat16)
    for at in range(0, width, PANEL):
        cols = slice(at, at + PANEL)
        adapter = jnp.dot(placed, expand_ref[:, cols], preferred_element_type=jnp.float32)
        out_ref[:, cols] = (whole(cols) + adapter).astype(out_ref.dtype)


def paired(n_tensor, n_req, hidden, weight, shrink, expand, ids):
    rows, units = hidden.shape
    width = weight.shape[1]
    adapters, rank = shrink.shape[1:]
    wide = adapters * rank
    room = (units // LANES + 1) * LANES
    payload = width + LANES
    bf16 = jnp.bfloat16
    counts = [rows * part // 128 for part in PIECES]
    starts = [sum(counts[:at]) for at in range(len(counts))]
    quick = pl.CostEstimate(flops=1, bytes_accessed=1, transcendentals=0)

    def params(mib):
        return pltpu.CompilerParams(vmem_limit_bytes=mib * MIB)

    def struct(count, lanes):
        return jax.ShapeDtypeStruct((count, lanes), bf16)

    own, *pieces = pl.pallas_call(
        functools.partial(turn_kernel, starts),
        out_shape=[struct(rows, room)] + [struct(count, room) for count in counts],
        in_specs=[in_hbm(), in_hbm()],
        out_specs=[in_vmem()] * (1 + len(counts)),
        scratch_shapes=[
            pltpu.VMEM((units, rows), bf16),
            pltpu.VMEM((1, rows), jnp.int32),
            pltpu.SemaphoreType.DMA((units // LANES // TURN + 2,)),
        ],
        compiler_params=params(4),
        name="turn",
    )(left(hidden.T), left(ids.reshape(1, rows)))

    across = [(i, i ^ 2) for i in range(n_req)]
    beside = [(i, i ^ 1) for i in range(n_req)]
    next_z = [(i, i ^ 1) for i in range(n_tensor)]
    far_z = [(i, i ^ 2) for i in range(n_tensor)]

    direct = [lax.ppermute(pieces[0], "req", across)]
    other = lax.ppermute(own, "req", beside)

    shrink_rows = shrink.transpose(1, 2, 0).reshape(wide, units)
    token, *both = pl.pallas_call(
        load_kernel,
        out_shape=[jax.ShapeDtypeStruct((8, LANES), jnp.float32)]
        + [pltpu.VMEM((room, PANEL), bf16)] * (width // PANEL)
        + [pltpu.VMEM((room, wide), bf16)],
        in_specs=[in_hbm(), in_hbm()],
        out_specs=[in_vmem()] * (2 + width // PANEL),
        scratch_shapes=[
            pltpu.VMEM((wide, units), bf16),
            pltpu.SemaphoreType.DMA((width // PANEL,)),
            pltpu.SemaphoreType.DMA,
        ],
        compiler_params=params(10),
        cost_estimate=quick,
        name="load",
    )(left(weight), left(shrink_rows))

    def product(step, passed, token):
        return pl.pallas_call(
            functools.partial(product_kernel, adapters, units, starts[step]),
            out_shape=[struct(2 * counts[step], payload)] * 2,
            in_specs=[in_vmem()] * (5 + len(both)),
            out_specs=[in_vmem()] * 2,
            compiler_params=params(4),
            cost_estimate=quick,
            name="product",
        )(token, own, other, direct[step], passed, *both)

    def add(step, keep, got):
        return pl.pallas_call(
            add_kernel,
            out_shape=[struct(counts[step], payload)] * 2,
            in_specs=[in_vmem()] * 2,
            out_specs=[in_vmem()] * 2,
            compiler_params=params(4),
            cost_estimate=quick,
            name="add",
        )(keep, got)

    after = lax.optimization_barrier
    steps = len(counts)
    pieces[1], direct[0], token = after((pieces[1], direct[0], token))
    parts, kept, gots = [], [], []

    def add_part(step):
        keep, got = parts[step]
        send, keep = add(step, keep, got)
        kept.append(keep)
        return send

    for step in range(steps):
        if step + 1 < steps:
            direct.append(lax.ppermute(pieces[step + 1], "req", across))
        passed = lax.ppermute(direct[step], "req", beside)
        if step > 1:
            send = add_part(step - 2)
            passed, send = after((passed, send))
            gots.append(lax.ppermute(send, "tensor", far_z))
        send, keep = product(step, passed, token)
        if step + 1 < steps:
            later = pieces[step + 2 : step + 3]
            earlier = parts[step - 1 : step] if step else []
            direct[step + 1], send, later, earlier = after(
                (direct[step + 1], send, later, earlier)
            )
            pieces[step + 2 : step + 3] = later
            if step:
                parts[step - 1] = earlier[0]
        parts.append((keep, lax.ppermute(send, "tensor", next_z)))
    for step in range(steps - 2, steps):
        gots.append(lax.ppermute(add_part(step), "tensor", far_z))

    return pl.pallas_call(
        functools.partial(last_kernel, n_tensor, adapters),
        out_shape=struct(rows, width),
        in_specs=[in_vmem()] * (1 + 2 * steps),
        out_specs=in_vmem(),
        compiler_params=params(8),
        name="last",
    )(expand.reshape(wide, width), *kept, *gots)


def gathered(hidden, weight, shrink, expand, ids):
    rows, units = hidden.shape
    adapters, rank = shrink.shape[1:]
    width = weight.shape[1]
    columns = jnp.arange(adapters, dtype=jnp.int32)[None, :]
    onehot = (ids[:, None] == columns).astype(jnp.float32)
    every = jnp.dot(
        hidden, shrink.reshape(units, adapters * rank), preferred_element_type=jnp.float32
    )
    part = jnp.sum(every.reshape(rows, adapters, rank) * onehot[:, :, None], axis=1)
    all_ids = lax.all_gather(ids, "req", axis=0, tiled=True)
    base = jnp.dot(
        lax.all_gather(hidden, "req", axis=0, tiled=True),
        weight,
        preferred_element_type=jnp.float32,
    )
    base = lax.psum_scatter(
        base.astype(jnp.bfloat16), "tensor", scatter_dimension=0, tiled=True
    ).astype(jnp.float32)
    shrunk = lax.all_gather(
        lax.psum(part.astype(jnp.bfloat16), "tensor"), "req", axis=0, tiled=True
    )
    mine = base.shape[0]
    first = lax.axis_index("tensor") * mine
    shrunk = lax.dynamic_slice_in_dim(shrunk, first, mine, 0)
    mask = lax.dynamic_slice_in_dim(all_ids, first, mine, 0)[:, None] == columns
    placed = (shrunk[:, None, :] * mask.astype(jnp.bfloat16)[:, :, None]).reshape(
        mine, adapters * rank
    )
    adapter = jnp.dot(
        placed, expand.reshape(adapters * rank, width), preferred_element_type=jnp.float32
    )
    return (base + adapter).astype(jnp.bfloat16)


def solution(mesh):
    n_tensor, n_req = mesh.shape["tensor"], mesh.shape["req"]
    if n_tensor == 4 and n_req == 4:
        on_device = functools.partial(paired, n_tensor, n_req)
    else:
        on_device = gathered
    placed = (
        P(("rep", "req"), "tensor"),
        P("tensor", "req"),
        P("tensor", None, None),
        P(None, None, "req"),
        P(("rep", "req")),
    )
    return jax.shard_map(
        on_device,
        mesh=mesh,
        in_specs=placed,
        out_specs=P(("rep", "tensor"), "req"),
        check_vma=False,
    )
```

```python
import functools

import jax
import jax.numpy as jnp
from jax import lax
from jax.experimental import pallas as pl
from jax.experimental.pallas import tpu as pltpu
from jax.sharding import PartitionSpec as P

LANES = 128
PANEL = 512
DEPTH = 1024
TURN = 15
PIECES = (32, 32, 32, 32)
MIB = 1 << 20


def in_vmem():
    return pl.BlockSpec(memory_space=pltpu.VMEM)


def in_hbm():
    return pl.BlockSpec(memory_space=pltpu.HBM)


def left(array):
    return pltpu.with_memory_space_constraint(array, pltpu.HBM)


def turn_kernel(starts, hidden_hbm, ids_hbm, own_ref, *refs):
    *piece_refs, hidden_ref, ids_ref, sems = refs
    units, rows = hidden_hbm.shape
    full = units // LANES
    stops = [at * LANES for at in range(0, full, TURN)] + [units]
    copies = [
        pltpu.make_async_copy(
            hidden_hbm.at[pl.ds(at, to - at)], hidden_ref.at[pl.ds(at, to - at)], sems.at[step]
        )
        for step, (at, to) in enumerate(zip(stops, stops[1:]))
    ]
    ids_copy = pltpu.make_async_copy(ids_hbm, ids_ref, sems.at[len(copies)])
    for copy in copies:
        copy.start()
    ids_copy.start()
    for step, copy in enumerate(copies):
        copy.wait()
        last = step == len(copies) - 1
        if last:
            ids_copy.wait()
        for block in range(stops[step] // LANES, full + 1 if last else stops[step + 1] // LANES):
            if block < full:
                tile = hidden_ref[block * LANES : (block + 1) * LANES, :]
            else:
                ids = jnp.broadcast_to(
                    ids_ref[...].astype(jnp.float32).astype(jnp.bfloat16),
                    ((full + 1) * LANES - units, rows),
                )
                tile = jnp.concatenate([hidden_ref[full * LANES :, :], ids], axis=0)
            turned = tile.T
            at = slice(block * LANES, (block + 1) * LANES)
            own_ref[:, at] = turned
            for first, piece_ref in zip(starts, piece_refs):
                piece_ref[:, at] = turned[first : first + piece_ref.shape[0]]


def load_kernel(w_hbm, s_hbm, token_ref, *refs):
    *panel_refs, spread_ref, s_ref, w_sems, s_sem = refs
    units = w_hbm.shape[0]
    copies = [
        pltpu.make_async_copy(
            w_hbm.at[:, pl.ds(panel * PANEL, PANEL)],
            panel_ref.at[pl.ds(0, units), :],
            w_sems.at[panel],
        )
        for panel, panel_ref in enumerate(panel_refs)
    ]
    s_copy = pltpu.make_async_copy(s_hbm, s_ref, s_sem)
    s_copy.start()
    for copy in copies:
        copy.start()
    token_ref[...] = jnp.zeros_like(token_ref)
    for ref in (spread_ref, *panel_refs):
        ref[units:, :] = jnp.zeros_like(ref[units:, :])
    s_copy.wait()
    for at in range(0, units, DEPTH):
        to = min(at + DEPTH, units)
        spread_ref[at:to, :] = s_ref[:, at:to].T
    for copy in copies:
        copy.wait()


def part_rows(value, cols, send_ref, keep_ref):
    rows = send_ref.shape[0] // 2
    keep_first = lax.rem(lax.axis_index("req"), 2) == lax.rem(lax.axis_index("tensor"), 2)
    value = value.astype(send_ref.dtype)
    for half in range(2):
        first = value[(2 * half) * rows : (2 * half + 1) * rows]
        second = value[(2 * half + 1) * rows : (2 * half + 2) * rows]
        at = slice(half * rows, (half + 1) * rows)
        send_ref[at, cols] = jnp.where(keep_first, second, first)
        keep_ref[at, cols] = jnp.where(keep_first, first, second)


def product_kernel(
    adapters, units, at, _, own_ref, other_ref, direct_ref, passed_a, passed_b, *refs
):
    *panel_refs, spread_ref, send_ref, keep_ref = refs
    rows = direct_ref.shape[0]
    width = send_ref.shape[1] - LANES
    wide = spread_ref.shape[1]
    rank = wide // adapters

    def pieces(cols):
        near = [ref[at : at + rows, cols] for ref in (own_ref, other_ref)]
        far = [ref[:, cols] for ref in (direct_ref, passed_a, passed_b)]
        return jnp.concatenate(near + far, axis=0)

    every = jnp.dot(pieces(slice(None)), spread_ref[...], preferred_element_type=jnp.float32)
    ids = pieces(slice(units, units + 1)).astype(jnp.float32)
    column = lax.broadcasted_iota(jnp.int32, every.shape, 1) // rank
    picked = jnp.where(column.astype(jnp.float32) == ids, every, 0.0)
    tile = picked[:, :LANES]
    for lane in range(LANES, wide, LANES):
        tile = tile + picked[:, lane : lane + LANES]
    tile = tile + pltpu.roll(tile, rank, 1)
    lane = lax.broadcasted_iota(jnp.int32, tile.shape, 1)
    tile = jnp.where(lane < rank, tile, ids)
    part_rows(tile, slice(width, width + LANES), send_ref, keep_ref)

    for panel, panel_ref in enumerate(panel_refs):
        value = jnp.dot(
            pieces(slice(None)), panel_ref[...], preferred_element_type=jnp.float32
        )
        part_rows(value, slice(panel * PANEL, (panel + 1) * PANEL), send_ref, keep_ref)


def add_kernel(first_ref, second_ref, send_ref, keep_ref):
    rows = send_ref.shape[0]
    keep_near = lax.axis_index("tensor") // 2 == lax.axis_index("req") // 2

    def total(at):
        cut = slice(at, at + rows)
        value = first_ref[cut].astype(jnp.float32) + second_ref[cut].astype(jnp.float32)
        return value.astype(send_ref.dtype)

    near, far = total(0), total(rows)
    send_ref[...] = jnp.where(keep_near, far, near)
    keep_ref[...] = jnp.where(keep_near, near, far)


def last_kernel(n_tensor, adapters, expand_ref, *refs):
    out_ref = refs[-1]
    count = (len(refs) - 1) // 2
    kept, got = refs[:count], refs[count:-1]
    wide, width = expand_ref.shape
    rank = wide // adapters

    def whole(cols):
        parts = [
            first[:, cols].astype(jnp.float32) + second[:, cols].astype(jnp.float32)
            for first, second in zip(kept, got)
        ]
        return jnp.concatenate(parts, axis=0)

    small = whole(slice(width, width + LANES))
    ids = small[:, rank : rank + 1] * (1.0 / n_tensor)
    lane = lax.broadcasted_iota(jnp.int32, small.shape, 1)
    shrink = jnp.where(lane < rank, small, 0.0)
    shrink = shrink + pltpu.roll(shrink, rank, 1)
    spread = jnp.concatenate([shrink] * (wide // LANES), axis=1)
    column = lax.broadcasted_iota(jnp.int32, spread.shape, 1) // rank
    placed = jnp.where(column.astype(jnp.float32) == ids, spread, 0.0).astype(jnp.bfloat16)
    for at in range(0, width, PANEL):
        cols = slice(at, at + PANEL)
        adapter = jnp.dot(placed, expand_ref[:, cols], preferred_element_type=jnp.float32)
        out_ref[:, cols] = (whole(cols) + adapter).astype(out_ref.dtype)


def paired(n_tensor, n_req, hidden, weight, shrink, expand, ids):
    rows, units = hidden.shape
    width = weight.shape[1]
    adapters, rank = shrink.shape[1:]
    wide = adapters * rank
    room = (units // LANES + 1) * LANES
    payload = width + LANES
    bf16 = jnp.bfloat16
    counts = [rows * part // 128 for part in PIECES]
    starts = [sum(counts[:at]) for at in range(len(counts))]
    quick = pl.CostEstimate(flops=1, bytes_accessed=1, transcendentals=0)

    def params(mib):
        return pltpu.CompilerParams(vmem_limit_bytes=mib * MIB)

    def struct(count, lanes):
        return jax.ShapeDtypeStruct((count, lanes), bf16)

    own, *pieces = pl.pallas_call(
        functools.partial(turn_kernel, starts),
        out_shape=[struct(rows, room)] + [struct(count, room) for count in counts],
        in_specs=[in_hbm(), in_hbm()],
        out_specs=[in_vmem()] * (1 + len(counts)),
        scratch_shapes=[
            pltpu.VMEM((units, rows), bf16),
            pltpu.VMEM((1, rows), jnp.int32),
            pltpu.SemaphoreType.DMA((units // LANES // TURN + 2,)),
        ],
        compiler_params=params(4),
        name="turn",
    )(left(hidden.T), left(ids.reshape(1, rows)))

    across = [(i, i ^ 2) for i in range(n_req)]
    beside = [(i, i ^ 1) for i in range(n_req)]
    next_z = [(i, i ^ 1) for i in range(n_tensor)]
    far_z = [(i, i ^ 2) for i in range(n_tensor)]

    direct = [lax.ppermute(pieces[0], "req", across)]
    other = lax.ppermute(own, "req", beside)

    shrink_rows = shrink.transpose(1, 2, 0).reshape(wide, units)
    token, *both = pl.pallas_call(
        load_kernel,
        out_shape=[jax.ShapeDtypeStruct((8, LANES), jnp.float32)]
        + [pltpu.VMEM((room, PANEL), bf16)] * (width // PANEL)
        + [pltpu.VMEM((room, wide), bf16)],
        in_specs=[in_hbm(), in_hbm()],
        out_specs=[in_vmem()] * (2 + width // PANEL),
        scratch_shapes=[
            pltpu.VMEM((wide, units), bf16),
            pltpu.SemaphoreType.DMA((width // PANEL,)),
            pltpu.SemaphoreType.DMA,
        ],
        compiler_params=params(10),
        cost_estimate=quick,
        name="load",
    )(left(weight), left(shrink_rows))

    def product(step, passed, token):
        return pl.pallas_call(
            functools.partial(product_kernel, adapters, units, starts[step]),
            out_shape=[struct(2 * counts[step], payload)] * 2,
            in_specs=[in_vmem()] * (6 + len(both)),
            out_specs=[in_vmem()] * 2,
            compiler_params=params(4),
            cost_estimate=quick,
            name="product",
        )(token, own, other, direct[step], *passed, *both)

    def add(step, keep, got):
        return pl.pallas_call(
            add_kernel,
            out_shape=[struct(counts[step], payload)] * 2,
            in_specs=[in_vmem()] * 2,
            out_specs=[in_vmem()] * 2,
            compiler_params=params(4),
            cost_estimate=quick,
            name="add",
        )(keep, got)

    def over_core(part):
        half = part.shape[0] // 2
        return [lax.ppermute(cut, "req", beside) for cut in (part[:half], part[half:])]

    after = lax.optimization_barrier
    steps = len(counts)
    direct[0], token = after((direct[0], token))
    parts, kept, gots = [], [], []

    def add_part(step):
        keep, got = parts[step]
        send, keep = add(step, keep, got)
        kept.append(keep)
        return send

    for step in range(steps):
        passed = over_core(direct[step])
        if step + 1 < steps:
            direct.append(lax.ppermute(pieces[step + 1], "req", across))
        if step > 1:
            send = add_part(step - 2)
            passed, send = after((passed, send))
            gots.append(lax.ppermute(send, "tensor", far_z))
        send, keep = product(step, passed, token)
        if step + 1 < steps:
            if step + 2 < steps:
                send, pieces[step + 2] = after((send, pieces[step + 2]))
            earlier = parts[step - 1 : step] if step else []
            direct[step + 1], send, earlier, done = after(
                (direct[step + 1], send, earlier, gots[step - 2 : step - 1] if step > 1 else [])
            )
            if step:
                parts[step - 1] = earlier[0]
            if done:
                gots[step - 2] = done[0]
        parts.append((keep, lax.ppermute(send, "tensor", next_z)))
    for step in range(steps - 2, steps):
        gots.append(lax.ppermute(add_part(step), "tensor", far_z))

    return pl.pallas_call(
        functools.partial(last_kernel, n_tensor, adapters),
        out_shape=struct(rows, width),
        in_specs=[in_vmem()] * (1 + 2 * steps),
        out_specs=in_vmem(),
        compiler_params=params(8),
        name="last",
    )(expand.reshape(wide, width), *kept, *gots)


def gathered(hidden, weight, shrink, expand, ids):
    rows, units = hidden.shape
    adapters, rank = shrink.shape[1:]
    width = weight.shape[1]
    columns = jnp.arange(adapters, dtype=jnp.int32)[None, :]
    onehot = (ids[:, None] == columns).astype(jnp.float32)
    every = jnp.dot(
        hidden, shrink.reshape(units, adapters * rank), preferred_element_type=jnp.float32
    )
    part = jnp.sum(every.reshape(rows, adapters, rank) * onehot[:, :, None], axis=1)
    all_ids = lax.all_gather(ids, "req", axis=0, tiled=True)
    base = jnp.dot(
        lax.all_gather(hidden, "req", axis=0, tiled=True),
        weight,
        preferred_element_type=jnp.float32,
    )
    base = lax.psum_scatter(
        base.astype(jnp.bfloat16), "tensor", scatter_dimension=0, tiled=True
    ).astype(jnp.float32)
    shrunk = lax.all_gather(
        lax.psum(part.astype(jnp.bfloat16), "tensor"), "req", axis=0, tiled=True
    )
    mine = base.shape[0]
    first = lax.axis_index("tensor") * mine
    shrunk = lax.dynamic_slice_in_dim(shrunk, first, mine, 0)
    mask = lax.dynamic_slice_in_dim(all_ids, first, mine, 0)[:, None] == columns
    placed = (shrunk[:, None, :] * mask.astype(jnp.bfloat16)[:, :, None]).reshape(
        mine, adapters * rank
    )
    adapter = jnp.dot(
        placed, expand.reshape(adapters * rank, width), preferred_element_type=jnp.float32
    )
    return (base + adapter).astype(jnp.bfloat16)


def solution(mesh):
    n_tensor, n_req = mesh.shape["tensor"], mesh.shape["req"]
    if n_tensor == 4 and n_req == 4:
        on_device = functools.partial(paired, n_tensor, n_req)
    else:
        on_device = gathered
    placed = (
        P(("rep", "req"), "tensor"),
        P("tensor", "req"),
        P("tensor", None, None),
        P(None, None, "req"),
        P(("rep", "req")),
    )
    return jax.shard_map(
        on_device,
        mesh=mesh,
        in_specs=placed,
        out_specs=P(("rep", "tensor"), "req"),
        check_vma=False,
    )
```

```python
import functools

import jax
import jax.numpy as jnp
from jax import lax
from jax.experimental import pallas as pl
from jax.experimental.pallas import tpu as pltpu
from jax.sharding import PartitionSpec as P

LANES = 128
PANEL = 512
DEPTH = 1024
TURN = 15
PIECES = (32, 32, 32, 32)
MIB = 1 << 20


def in_vmem():
    return pl.BlockSpec(memory_space=pltpu.VMEM)


def in_hbm():
    return pl.BlockSpec(memory_space=pltpu.HBM)


def left(array):
    return pltpu.with_memory_space_constraint(array, pltpu.HBM)


def turn_kernel(starts, hidden_hbm, ids_hbm, own_ref, *refs):
    *piece_refs, hidden_ref, ids_ref, sems = refs
    units, rows = hidden_hbm.shape
    full = units // LANES
    stops = [at * LANES for at in range(0, full, TURN)] + [units]
    copies = [
        pltpu.make_async_copy(
            hidden_hbm.at[pl.ds(at, to - at)], hidden_ref.at[pl.ds(at, to - at)], sems.at[step]
        )
        for step, (at, to) in enumerate(zip(stops, stops[1:]))
    ]
    ids_copy = pltpu.make_async_copy(ids_hbm, ids_ref, sems.at[len(copies)])
    for copy in copies:
        copy.start()
    ids_copy.start()
    for step, copy in enumerate(copies):
        copy.wait()
        last = step == len(copies) - 1
        if last:
            ids_copy.wait()
        for block in range(stops[step] // LANES, full + 1 if last else stops[step + 1] // LANES):
            if block < full:
                tile = hidden_ref[block * LANES : (block + 1) * LANES, :]
            else:
                ids = jnp.broadcast_to(
                    ids_ref[...].astype(jnp.float32).astype(jnp.bfloat16),
                    ((full + 1) * LANES - units, rows),
                )
                tile = jnp.concatenate([hidden_ref[full * LANES :, :], ids], axis=0)
            turned = tile.T
            at = slice(block * LANES, (block + 1) * LANES)
            own_ref[:, at] = turned
            for first, piece_ref in zip(starts, piece_refs):
                piece_ref[:, at] = turned[first : first + piece_ref.shape[0]]


def load_kernel(w_hbm, s_hbm, token_ref, *refs):
    *panel_refs, spread_ref, s_ref, w_sems, s_sem = refs
    units = w_hbm.shape[0]
    copies = [
        pltpu.make_async_copy(
            w_hbm.at[:, pl.ds(panel * PANEL, PANEL)],
            panel_ref.at[pl.ds(0, units), :],
            w_sems.at[panel],
        )
        for panel, panel_ref in enumerate(panel_refs)
    ]
    s_copy = pltpu.make_async_copy(s_hbm, s_ref, s_sem)
    s_copy.start()
    for copy in copies:
        copy.start()
    token_ref[...] = jnp.zeros_like(token_ref)
    for ref in (spread_ref, *panel_refs):
        ref[units:, :] = jnp.zeros_like(ref[units:, :])
    s_copy.wait()
    for at in range(0, units, DEPTH):
        to = min(at + DEPTH, units)
        spread_ref[at:to, :] = s_ref[:, at:to].T
    for copy in copies:
        copy.wait()


def part_rows(value, cols, send_ref, keep_ref):
    rows = send_ref.shape[0] // 2
    keep_first = lax.rem(lax.axis_index("req"), 2) == lax.rem(lax.axis_index("tensor"), 2)
    value = value.astype(send_ref.dtype)
    for half in range(2):
        first = value[(2 * half) * rows : (2 * half + 1) * rows]
        second = value[(2 * half + 1) * rows : (2 * half + 2) * rows]
        at = slice(half * rows, (half + 1) * rows)
        send_ref[at, cols] = jnp.where(keep_first, second, first)
        keep_ref[at, cols] = jnp.where(keep_first, first, second)


def product_kernel(
    adapters, units, at, _, own_ref, other_ref, direct_ref, passed_a, passed_b, *refs
):
    *panel_refs, spread_ref, send_ref, keep_ref = refs
    rows = direct_ref.shape[0]
    width = send_ref.shape[1] - LANES
    wide = spread_ref.shape[1]
    rank = wide // adapters

    def pieces(cols):
        near = [ref[at : at + rows, cols] for ref in (own_ref, other_ref)]
        far = [ref[:, cols] for ref in (direct_ref, passed_a, passed_b)]
        return jnp.concatenate(near + far, axis=0)

    every = jnp.dot(pieces(slice(None)), spread_ref[...], preferred_element_type=jnp.float32)
    ids = pieces(slice(units, units + 1)).astype(jnp.float32)
    column = lax.broadcasted_iota(jnp.int32, every.shape, 1) // rank
    picked = jnp.where(column.astype(jnp.float32) == ids, every, 0.0)
    tile = picked[:, :LANES]
    for lane in range(LANES, wide, LANES):
        tile = tile + picked[:, lane : lane + LANES]
    tile = tile + pltpu.roll(tile, rank, 1)
    lane = lax.broadcasted_iota(jnp.int32, tile.shape, 1)
    tile = jnp.where(lane < rank, tile, ids)
    part_rows(tile, slice(width, width + LANES), send_ref, keep_ref)

    for panel, panel_ref in enumerate(panel_refs):
        value = jnp.dot(
            pieces(slice(None)), panel_ref[...], preferred_element_type=jnp.float32
        )
        part_rows(value, slice(panel * PANEL, (panel + 1) * PANEL), send_ref, keep_ref)


def add_kernel(first_ref, second_ref, send_ref, keep_ref):
    rows = send_ref.shape[0]
    keep_near = lax.axis_index("tensor") // 2 == lax.axis_index("req") // 2

    def total(at):
        cut = slice(at, at + rows)
        value = first_ref[cut].astype(jnp.float32) + second_ref[cut].astype(jnp.float32)
        return value.astype(send_ref.dtype)

    near, far = total(0), total(rows)
    send_ref[...] = jnp.where(keep_near, far, near)
    keep_ref[...] = jnp.where(keep_near, near, far)


def last_kernel(n_tensor, adapters, expand_ref, *refs):
    out_ref = refs[-1]
    count = (len(refs) - 1) // 2
    kept, got = refs[:count], refs[count:-1]
    wide, width = expand_ref.shape
    rank = wide // adapters

    def whole(cols):
        parts = [
            first[:, cols].astype(jnp.float32) + second[:, cols].astype(jnp.float32)
            for first, second in zip(kept, got)
        ]
        return jnp.concatenate(parts, axis=0)

    small = whole(slice(width, width + LANES))
    ids = small[:, rank : rank + 1] * (1.0 / n_tensor)
    lane = lax.broadcasted_iota(jnp.int32, small.shape, 1)
    shrink = jnp.where(lane < rank, small, 0.0)
    shrink = shrink + pltpu.roll(shrink, rank, 1)
    spread = jnp.concatenate([shrink] * (wide // LANES), axis=1)
    column = lax.broadcasted_iota(jnp.int32, spread.shape, 1) // rank
    placed = jnp.where(column.astype(jnp.float32) == ids, spread, 0.0).astype(jnp.bfloat16)
    for at in range(0, width, PANEL):
        cols = slice(at, at + PANEL)
        adapter = jnp.dot(placed, expand_ref[:, cols], preferred_element_type=jnp.float32)
        out_ref[:, cols] = (whole(cols) + adapter).astype(out_ref.dtype)


def paired(n_tensor, n_req, hidden, weight, shrink, expand, ids):
    rows, units = hidden.shape
    width = weight.shape[1]
    adapters, rank = shrink.shape[1:]
    wide = adapters * rank
    room = (units // LANES + 1) * LANES
    payload = width + LANES
    bf16 = jnp.bfloat16
    counts = [rows * part // 128 for part in PIECES]
    starts = [sum(counts[:at]) for at in range(len(counts))]
    quick = pl.CostEstimate(flops=1, bytes_accessed=1, transcendentals=0)

    def params(mib):
        return pltpu.CompilerParams(vmem_limit_bytes=mib * MIB)

    def struct(count, lanes):
        return jax.ShapeDtypeStruct((count, lanes), bf16)

    own, *pieces = pl.pallas_call(
        functools.partial(turn_kernel, starts),
        out_shape=[struct(rows, room)] + [struct(count, room) for count in counts],
        in_specs=[in_hbm(), in_hbm()],
        out_specs=[in_vmem()] * (1 + len(counts)),
        scratch_shapes=[
            pltpu.VMEM((units, rows), bf16),
            pltpu.VMEM((1, rows), jnp.int32),
            pltpu.SemaphoreType.DMA((units // LANES // TURN + 2,)),
        ],
        compiler_params=params(4),
        name="turn",
    )(left(hidden.T), left(ids.reshape(1, rows)))

    across = [(i, i ^ 2) for i in range(n_req)]
    beside = [(i, i ^ 1) for i in range(n_req)]
    next_z = [(i, i ^ 1) for i in range(n_tensor)]
    far_z = [(i, i ^ 2) for i in range(n_tensor)]

    direct = [lax.ppermute(pieces[0], "req", across)]
    other = lax.ppermute(own, "req", beside)

    shrink_rows = shrink.transpose(1, 2, 0).reshape(wide, units)
    token, *both = pl.pallas_call(
        load_kernel,
        out_shape=[jax.ShapeDtypeStruct((8, LANES), jnp.float32)]
        + [pltpu.VMEM((room, PANEL), bf16)] * (width // PANEL)
        + [pltpu.VMEM((room, wide), bf16)],
        in_specs=[in_hbm(), in_hbm()],
        out_specs=[in_vmem()] * (2 + width // PANEL),
        scratch_shapes=[
            pltpu.VMEM((wide, units), bf16),
            pltpu.SemaphoreType.DMA((width // PANEL,)),
            pltpu.SemaphoreType.DMA,
        ],
        compiler_params=params(10),
        cost_estimate=quick,
        name="load",
    )(left(weight), left(shrink_rows))

    def product(step, passed, token):
        return pl.pallas_call(
            functools.partial(product_kernel, adapters, units, starts[step]),
            out_shape=[struct(2 * counts[step], payload)] * 2,
            in_specs=[in_vmem()] * (6 + len(both)),
            out_specs=[in_vmem()] * 2,
            compiler_params=params(4),
            cost_estimate=quick,
            name="product",
        )(token, own, other, direct[step], *passed, *both)

    def add(step, keep, got):
        return pl.pallas_call(
            add_kernel,
            out_shape=[struct(counts[step], payload)] * 2,
            in_specs=[in_vmem()] * 2,
            out_specs=[in_vmem()] * 2,
            compiler_params=params(4),
            cost_estimate=quick,
            name="add",
        )(keep, got)

    def over_core(part):
        half = part.shape[0] // 2
        return [lax.ppermute(cut, "req", beside) for cut in (part[:half], part[half:])]

    after = lax.optimization_barrier
    steps = len(counts)
    direct[0], token = after((direct[0], token))
    parts, kept, gots = [], [], []

    def add_part(step):
        keep, got = parts[step]
        send, keep = add(step, keep, got)
        kept.append(keep)
        return send

    for step in range(steps):
        passed = over_core(direct[step])
        if step + 1 < steps:
            direct.append(lax.ppermute(pieces[step + 1], "req", across))
        if step > 1:
            send = add_part(step - 2)
            passed, send = after((passed, send))
            gots.append(lax.ppermute(send, "tensor", far_z))
        send, keep = product(step, passed, token)
        near = slice(step - 2, step - 1) if step > 1 else slice(0, 0)
        send, gots[near] = after((send, gots[near]))
        if step + 1 < steps:
            earlier = parts[step - 1 : step] if step else []
            direct[step + 1], send, earlier = after((direct[step + 1], send, earlier))
            if step:
                parts[step - 1] = earlier[0]
        parts.append((keep, lax.ppermute(send, "tensor", next_z)))
    for step in range(steps - 2, steps):
        gots.append(lax.ppermute(add_part(step), "tensor", far_z))

    return pl.pallas_call(
        functools.partial(last_kernel, n_tensor, adapters),
        out_shape=struct(rows, width),
        in_specs=[in_vmem()] * (1 + 2 * steps),
        out_specs=in_vmem(),
        compiler_params=params(8),
        name="last",
    )(expand.reshape(wide, width), *kept, *gots)


def gathered(hidden, weight, shrink, expand, ids):
    rows, units = hidden.shape
    adapters, rank = shrink.shape[1:]
    width = weight.shape[1]
    columns = jnp.arange(adapters, dtype=jnp.int32)[None, :]
    onehot = (ids[:, None] == columns).astype(jnp.float32)
    every = jnp.dot(
        hidden, shrink.reshape(units, adapters * rank), preferred_element_type=jnp.float32
    )
    part = jnp.sum(every.reshape(rows, adapters, rank) * onehot[:, :, None], axis=1)
    all_ids = lax.all_gather(ids, "req", axis=0, tiled=True)
    base = jnp.dot(
        lax.all_gather(hidden, "req", axis=0, tiled=True),
        weight,
        preferred_element_type=jnp.float32,
    )
    base = lax.psum_scatter(
        base.astype(jnp.bfloat16), "tensor", scatter_dimension=0, tiled=True
    ).astype(jnp.float32)
    shrunk = lax.all_gather(
        lax.psum(part.astype(jnp.bfloat16), "tensor"), "req", axis=0, tiled=True
    )
    mine = base.shape[0]
    first = lax.axis_index("tensor") * mine
    shrunk = lax.dynamic_slice_in_dim(shrunk, first, mine, 0)
    mask = lax.dynamic_slice_in_dim(all_ids, first, mine, 0)[:, None] == columns
    placed = (shrunk[:, None, :] * mask.astype(jnp.bfloat16)[:, :, None]).reshape(
        mine, adapters * rank
    )
    adapter = jnp.dot(
        placed, expand.reshape(adapters * rank, width), preferred_element_type=jnp.float32
    )
    return (base + adapter).astype(jnp.bfloat16)


def solution(mesh):
    n_tensor, n_req = mesh.shape["tensor"], mesh.shape["req"]
    if n_tensor == 4 and n_req == 4:
        on_device = functools.partial(paired, n_tensor, n_req)
    else:
        on_device = gathered
    placed = (
        P(("rep", "req"), "tensor"),
        P("tensor", "req"),
        P("tensor", None, None),
        P(None, None, "req"),
        P(("rep", "req")),
    )
    return jax.shard_map(
        on_device,
        mesh=mesh,
        in_specs=placed,
        out_specs=P(("rep", "tensor"), "req"),
        check_vma=False,
    )
```

```python
import functools

import jax
import jax.numpy as jnp
from jax import lax
from jax.experimental import pallas as pl
from jax.experimental.pallas import tpu as pltpu
from jax.sharding import PartitionSpec as P

LANES = 128
PANEL = 512
DEPTH = 1024
TURN = 15
PIECES = (32, 32, 32, 32)
CUTS = 4
MIB = 1 << 20


def in_vmem():
    return pl.BlockSpec(memory_space=pltpu.VMEM)


def in_hbm():
    return pl.BlockSpec(memory_space=pltpu.HBM)


def left(array):
    return pltpu.with_memory_space_constraint(array, pltpu.HBM)


def turn_kernel(starts, hidden_hbm, ids_hbm, own_ref, *refs):
    *piece_refs, hidden_ref, ids_ref, sems = refs
    units, rows = hidden_hbm.shape
    full = units // LANES
    stops = [at * LANES for at in range(0, full, TURN)] + [units]
    copies = [
        pltpu.make_async_copy(
            hidden_hbm.at[pl.ds(at, to - at)], hidden_ref.at[pl.ds(at, to - at)], sems.at[step]
        )
        for step, (at, to) in enumerate(zip(stops, stops[1:]))
    ]
    ids_copy = pltpu.make_async_copy(ids_hbm, ids_ref, sems.at[len(copies)])
    for copy in copies:
        copy.start()
    ids_copy.start()
    for step, copy in enumerate(copies):
        copy.wait()
        last = step == len(copies) - 1
        if last:
            ids_copy.wait()
        for block in range(stops[step] // LANES, full + 1 if last else stops[step + 1] // LANES):
            if block < full:
                tile = hidden_ref[block * LANES : (block + 1) * LANES, :]
            else:
                ids = jnp.broadcast_to(
                    ids_ref[...].astype(jnp.float32).astype(jnp.bfloat16),
                    ((full + 1) * LANES - units, rows),
                )
                tile = jnp.concatenate([hidden_ref[full * LANES :, :], ids], axis=0)
            turned = tile.T
            at = slice(block * LANES, (block + 1) * LANES)
            own_ref[:, at] = turned
            for first, piece_ref in zip(starts, piece_refs):
                piece_ref[:, at] = turned[first : first + piece_ref.shape[0]]


def load_kernel(w_hbm, s_hbm, token_ref, *refs):
    *panel_refs, spread_ref, s_ref, w_sems, s_sem = refs
    units = w_hbm.shape[0]
    copies = [
        pltpu.make_async_copy(
            w_hbm.at[:, pl.ds(panel * PANEL, PANEL)],
            panel_ref.at[pl.ds(0, units), :],
            w_sems.at[panel],
        )
        for panel, panel_ref in enumerate(panel_refs)
    ]
    s_copy = pltpu.make_async_copy(s_hbm, s_ref, s_sem)
    s_copy.start()
    for copy in copies:
        copy.start()
    token_ref[...] = jnp.zeros_like(token_ref)
    for ref in (spread_ref, *panel_refs):
        ref[units:, :] = jnp.zeros_like(ref[units:, :])
    s_copy.wait()
    for at in range(0, units, DEPTH):
        to = min(at + DEPTH, units)
        spread_ref[at:to, :] = s_ref[:, at:to].T
    for copy in copies:
        copy.wait()


def part_rows(value, cols, send_ref, keep_ref):
    rows = send_ref.shape[0] // 2
    keep_first = lax.rem(lax.axis_index("req"), 2) == lax.rem(lax.axis_index("tensor"), 2)
    value = value.astype(send_ref.dtype)
    for half in range(2):
        first = value[(2 * half) * rows : (2 * half + 1) * rows]
        second = value[(2 * half + 1) * rows : (2 * half + 2) * rows]
        at = slice(half * rows, (half + 1) * rows)
        send_ref[at, cols] = jnp.where(keep_first, second, first)
        keep_ref[at, cols] = jnp.where(keep_first, first, second)


def product_kernel(adapters, units, at, _, own_ref, other_ref, direct_ref, *refs):
    passed_refs, refs = refs[:CUTS], refs[CUTS:]
    *panel_refs, spread_ref, send_ref, keep_ref = refs
    rows = direct_ref.shape[0]
    width = send_ref.shape[1] - LANES
    wide = spread_ref.shape[1]
    rank = wide // adapters

    def piece():
        near = [own_ref[at : at + rows, :], other_ref[at : at + rows, :]]
        passed = jnp.concatenate([ref[...] for ref in passed_refs], axis=1)
        return jnp.concatenate([*near, direct_ref[...], passed], axis=0)

    every = jnp.dot(piece(), spread_ref[...], preferred_element_type=jnp.float32)
    ids = piece()[:, units : units + 1].astype(jnp.float32)
    column = lax.broadcasted_iota(jnp.int32, every.shape, 1) // rank
    picked = jnp.where(column.astype(jnp.float32) == ids, every, 0.0)
    tile = picked[:, :LANES]
    for lane in range(LANES, wide, LANES):
        tile = tile + picked[:, lane : lane + LANES]
    tile = tile + pltpu.roll(tile, rank, 1)
    lane = lax.broadcasted_iota(jnp.int32, tile.shape, 1)
    tile = jnp.where(lane < rank, tile, ids)
    part_rows(tile, slice(width, width + LANES), send_ref, keep_ref)

    for panel, panel_ref in enumerate(panel_refs):
        value = jnp.dot(
            piece(), panel_ref[...], preferred_element_type=jnp.float32
        )
        part_rows(value, slice(panel * PANEL, (panel + 1) * PANEL), send_ref, keep_ref)


def add_kernel(first_ref, second_ref, send_ref, keep_ref):
    rows = send_ref.shape[0]
    keep_near = lax.axis_index("tensor") // 2 == lax.axis_index("req") // 2

    def total(at):
        cut = slice(at, at + rows)
        value = first_ref[cut].astype(jnp.float32) + second_ref[cut].astype(jnp.float32)
        return value.astype(send_ref.dtype)

    near, far = total(0), total(rows)
    send_ref[...] = jnp.where(keep_near, far, near)
    keep_ref[...] = jnp.where(keep_near, near, far)


def last_kernel(n_tensor, adapters, expand_ref, *refs):
    out_ref = refs[-1]
    count = (len(refs) - 1) // 2
    kept, got = refs[:count], refs[count:-1]
    wide, width = expand_ref.shape
    rank = wide // adapters

    def whole(cols):
        parts = [
            first[:, cols].astype(jnp.float32) + second[:, cols].astype(jnp.float32)
            for first, second in zip(kept, got)
        ]
        return jnp.concatenate(parts, axis=0)

    small = whole(slice(width, width + LANES))
    ids = small[:, rank : rank + 1] * (1.0 / n_tensor)
    lane = lax.broadcasted_iota(jnp.int32, small.shape, 1)
    shrink = jnp.where(lane < rank, small, 0.0)
    shrink = shrink + pltpu.roll(shrink, rank, 1)
    spread = jnp.concatenate([shrink] * (wide // LANES), axis=1)
    column = lax.broadcasted_iota(jnp.int32, spread.shape, 1) // rank
    placed = jnp.where(column.astype(jnp.float32) == ids, spread, 0.0).astype(jnp.bfloat16)
    for at in range(0, width, PANEL):
        cols = slice(at, at + PANEL)
        adapter = jnp.dot(placed, expand_ref[:, cols], preferred_element_type=jnp.float32)
        out_ref[:, cols] = (whole(cols) + adapter).astype(out_ref.dtype)


def paired(n_tensor, n_req, hidden, weight, shrink, expand, ids):
    rows, units = hidden.shape
    width = weight.shape[1]
    adapters, rank = shrink.shape[1:]
    wide = adapters * rank
    room = (units // LANES + 1) * LANES
    payload = width + LANES
    bf16 = jnp.bfloat16
    counts = [rows * part // 128 for part in PIECES]
    starts = [sum(counts[:at]) for at in range(len(counts))]
    quick = pl.CostEstimate(flops=1, bytes_accessed=1, transcendentals=0)

    def params(mib):
        return pltpu.CompilerParams(vmem_limit_bytes=mib * MIB)

    def struct(count, lanes):
        return jax.ShapeDtypeStruct((count, lanes), bf16)

    own, *pieces = pl.pallas_call(
        functools.partial(turn_kernel, starts),
        out_shape=[struct(rows, room)] + [struct(count, room) for count in counts],
        in_specs=[in_hbm(), in_hbm()],
        out_specs=[in_vmem()] * (1 + len(counts)),
        scratch_shapes=[
            pltpu.VMEM((units, rows), bf16),
            pltpu.VMEM((1, rows), jnp.int32),
            pltpu.SemaphoreType.DMA((units // LANES // TURN + 2,)),
        ],
        compiler_params=params(4),
        name="turn",
    )(left(hidden.T), left(ids.reshape(1, rows)))

    across = [(i, i ^ 2) for i in range(n_req)]
    beside = [(i, i ^ 1) for i in range(n_req)]
    next_z = [(i, i ^ 1) for i in range(n_tensor)]
    far_z = [(i, i ^ 2) for i in range(n_tensor)]

    direct = [lax.ppermute(pieces[0], "req", across)]
    other = lax.ppermute(own, "req", beside)

    shrink_rows = shrink.transpose(1, 2, 0).reshape(wide, units)
    token, *both = pl.pallas_call(
        load_kernel,
        out_shape=[jax.ShapeDtypeStruct((8, LANES), jnp.float32)]
        + [pltpu.VMEM((room, PANEL), bf16)] * (width // PANEL)
        + [pltpu.VMEM((room, wide), bf16)],
        in_specs=[in_hbm(), in_hbm()],
        out_specs=[in_vmem()] * (2 + width // PANEL),
        scratch_shapes=[
            pltpu.VMEM((wide, units), bf16),
            pltpu.SemaphoreType.DMA((width // PANEL,)),
            pltpu.SemaphoreType.DMA,
        ],
        compiler_params=params(10),
        cost_estimate=quick,
        name="load",
    )(left(weight), left(shrink_rows))

    def product(step, passed, token):
        return pl.pallas_call(
            functools.partial(product_kernel, adapters, units, starts[step]),
            out_shape=[struct(2 * counts[step], payload)] * 2,
            in_specs=[in_vmem()] * (4 + CUTS + len(both)),
            out_specs=[in_vmem()] * 2,
            compiler_params=params(4),
            cost_estimate=quick,
            name="product",
        )(token, own, other, direct[step], *passed, *both)

    def add(step, keep, got):
        return pl.pallas_call(
            add_kernel,
            out_shape=[struct(counts[step], payload)] * 2,
            in_specs=[in_vmem()] * 2,
            out_specs=[in_vmem()] * 2,
            compiler_params=params(4),
            cost_estimate=quick,
            name="add",
        )(keep, got)

    def over_core(part):
        tiles = room // LANES
        ends = [tiles * cut // CUTS * LANES for cut in range(CUTS + 1)]
        return [
            lax.ppermute(part[:, at:to], "req", beside) for at, to in zip(ends, ends[1:])
        ]

    after = lax.optimization_barrier
    steps = len(counts)
    direct[0], token = after((direct[0], token))
    parts, kept, gots = [], [], []

    def add_part(step):
        keep, got = parts[step]
        send, keep = add(step, keep, got)
        kept.append(keep)
        return send

    for step in range(steps):
        passed = over_core(direct[step])
        if step + 1 < steps:
            direct.append(lax.ppermute(pieces[step + 1], "req", across))
        if step > 1:
            send = add_part(step - 2)
            passed, send = after((passed, send))
            gots.append(lax.ppermute(send, "tensor", far_z))
        send, keep = product(step, passed, token)
        prior, before = slice(max(step - 1, 0), step), slice(max(step - 2, 0), max(step - 1, 0))
        if step + 1 < steps:
            got = lax.ppermute(send, "tensor", next_z)
            direct[step + 1], keep, parts[prior], gots[before] = after(
                (direct[step + 1], keep, parts[prior], gots[before])
            )
        else:
            send, parts[prior], gots[before] = after((send, parts[prior], gots[before]))
            got = lax.ppermute(send, "tensor", next_z)
        parts.append((keep, got))
    for step in range(steps - 2, steps):
        gots.append(lax.ppermute(add_part(step), "tensor", far_z))

    return pl.pallas_call(
        functools.partial(last_kernel, n_tensor, adapters),
        out_shape=struct(rows, width),
        in_specs=[in_vmem()] * (1 + 2 * steps),
        out_specs=in_vmem(),
        compiler_params=params(8),
        name="last",
    )(expand.reshape(wide, width), *kept, *gots)


def gathered(hidden, weight, shrink, expand, ids):
    rows, units = hidden.shape
    adapters, rank = shrink.shape[1:]
    width = weight.shape[1]
    columns = jnp.arange(adapters, dtype=jnp.int32)[None, :]
    onehot = (ids[:, None] == columns).astype(jnp.float32)
    every = jnp.dot(
        hidden, shrink.reshape(units, adapters * rank), preferred_element_type=jnp.float32
    )
    part = jnp.sum(every.reshape(rows, adapters, rank) * onehot[:, :, None], axis=1)
    all_ids = lax.all_gather(ids, "req", axis=0, tiled=True)
    base = jnp.dot(
        lax.all_gather(hidden, "req", axis=0, tiled=True),
        weight,
        preferred_element_type=jnp.float32,
    )
    base = lax.psum_scatter(
        base.astype(jnp.bfloat16), "tensor", scatter_dimension=0, tiled=True
    ).astype(jnp.float32)
    shrunk = lax.all_gather(
        lax.psum(part.astype(jnp.bfloat16), "tensor"), "req", axis=0, tiled=True
    )
    mine = base.shape[0]
    first = lax.axis_index("tensor") * mine
    shrunk = lax.dynamic_slice_in_dim(shrunk, first, mine, 0)
    mask = lax.dynamic_slice_in_dim(all_ids, first, mine, 0)[:, None] == columns
    placed = (shrunk[:, None, :] * mask.astype(jnp.bfloat16)[:, :, None]).reshape(
        mine, adapters * rank
    )
    adapter = jnp.dot(
        placed, expand.reshape(adapters * rank, width), preferred_element_type=jnp.float32
    )
    return (base + adapter).astype(jnp.bfloat16)


def solution(mesh):
    n_tensor, n_req = mesh.shape["tensor"], mesh.shape["req"]
    if n_tensor == 4 and n_req == 4:
        on_device = functools.partial(paired, n_tensor, n_req)
    else:
        on_device = gathered
    placed = (
        P(("rep", "req"), "tensor"),
        P("tensor", "req"),
        P("tensor", None, None),
        P(None, None, "req"),
        P(("rep", "req")),
    )
    return jax.shard_map(
        on_device,
        mesh=mesh,
        in_specs=placed,
        out_specs=P(("rep", "tensor"), "req"),
        check_vma=False,
    )
```

```python
import functools

import jax
import jax.numpy as jnp
from jax import lax
from jax.experimental import pallas as pl
from jax.experimental.pallas import tpu as pltpu
from jax.sharding import PartitionSpec as P

LANES = 128
PANEL = 512
DEPTH = 1024
TURN = 15
PIECES = (32, 32, 32, 32)
CUTS = 2
MIB = 1 << 20


def in_vmem():
    return pl.BlockSpec(memory_space=pltpu.VMEM)


def in_hbm():
    return pl.BlockSpec(memory_space=pltpu.HBM)


def left(array):
    return pltpu.with_memory_space_constraint(array, pltpu.HBM)


def turn_kernel(starts, hidden_hbm, ids_hbm, own_ref, *refs):
    *piece_refs, hidden_ref, ids_ref, sems = refs
    units, rows = hidden_hbm.shape
    full = units // LANES
    stops = [at * LANES for at in range(0, full, TURN)] + [units]
    copies = [
        pltpu.make_async_copy(
            hidden_hbm.at[pl.ds(at, to - at)], hidden_ref.at[pl.ds(at, to - at)], sems.at[step]
        )
        for step, (at, to) in enumerate(zip(stops, stops[1:]))
    ]
    ids_copy = pltpu.make_async_copy(ids_hbm, ids_ref, sems.at[len(copies)])
    for copy in copies:
        copy.start()
    ids_copy.start()
    for step, copy in enumerate(copies):
        copy.wait()
        last = step == len(copies) - 1
        if last:
            ids_copy.wait()
        for block in range(stops[step] // LANES, full + 1 if last else stops[step + 1] // LANES):
            if block < full:
                tile = hidden_ref[block * LANES : (block + 1) * LANES, :]
            else:
                ids = jnp.broadcast_to(
                    ids_ref[...].astype(jnp.float32).astype(jnp.bfloat16),
                    ((full + 1) * LANES - units, rows),
                )
                tile = jnp.concatenate([hidden_ref[full * LANES :, :], ids], axis=0)
            turned = tile.T
            at = slice(block * LANES, (block + 1) * LANES)
            own_ref[:, at] = turned
            for first, piece_ref in zip(starts, piece_refs):
                piece_ref[:, at] = turned[first : first + piece_ref.shape[0]]


def load_kernel(w_hbm, s_hbm, token_ref, *refs):
    *panel_refs, spread_ref, s_ref, w_sems, s_sem = refs
    units = w_hbm.shape[0]
    copies = [
        pltpu.make_async_copy(
            w_hbm.at[:, pl.ds(panel * PANEL, PANEL)],
            panel_ref.at[pl.ds(0, units), :],
            w_sems.at[panel],
        )
        for panel, panel_ref in enumerate(panel_refs)
    ]
    s_copy = pltpu.make_async_copy(s_hbm, s_ref, s_sem)
    s_copy.start()
    for copy in copies:
        copy.start()
    token_ref[...] = jnp.zeros_like(token_ref)
    for ref in (spread_ref, *panel_refs):
        ref[units:, :] = jnp.zeros_like(ref[units:, :])
    s_copy.wait()
    for at in range(0, units, DEPTH):
        to = min(at + DEPTH, units)
        spread_ref[at:to, :] = s_ref[:, at:to].T
    for copy in copies:
        copy.wait()


def part_rows(value, cols, send_ref, keep_ref):
    rows = send_ref.shape[0] // 2
    keep_first = lax.rem(lax.axis_index("req"), 2) == lax.rem(lax.axis_index("tensor"), 2)
    value = value.astype(send_ref.dtype)
    for half in range(2):
        first = value[(2 * half) * rows : (2 * half + 1) * rows]
        second = value[(2 * half + 1) * rows : (2 * half + 2) * rows]
        at = slice(half * rows, (half + 1) * rows)
        send_ref[at, cols] = jnp.where(keep_first, second, first)
        keep_ref[at, cols] = jnp.where(keep_first, first, second)


def product_kernel(adapters, units, at, _, own_ref, other_ref, direct_ref, *refs):
    passed_refs, refs = refs[:CUTS], refs[CUTS:]
    *panel_refs, spread_ref, send_ref, keep_ref = refs
    rows = direct_ref.shape[0]
    width = send_ref.shape[1] - LANES
    wide = spread_ref.shape[1]
    rank = wide // adapters

    def piece():
        near = [own_ref[at : at + rows, :], other_ref[at : at + rows, :]]
        passed = jnp.concatenate([ref[...] for ref in passed_refs], axis=1)
        return jnp.concatenate([*near, direct_ref[...], passed], axis=0)

    every = jnp.dot(piece(), spread_ref[...], preferred_element_type=jnp.float32)
    ids = piece()[:, units : units + 1].astype(jnp.float32)
    column = lax.broadcasted_iota(jnp.int32, every.shape, 1) // rank
    picked = jnp.where(column.astype(jnp.float32) == ids, every, 0.0)
    tile = picked[:, :LANES]
    for lane in range(LANES, wide, LANES):
        tile = tile + picked[:, lane : lane + LANES]
    tile = tile + pltpu.roll(tile, rank, 1)
    lane = lax.broadcasted_iota(jnp.int32, tile.shape, 1)
    tile = jnp.where(lane < rank, tile, ids)
    part_rows(tile, slice(width, width + LANES), send_ref, keep_ref)

    for panel, panel_ref in enumerate(panel_refs):
        value = jnp.dot(
            piece(), panel_ref[...], preferred_element_type=jnp.float32
        )
        part_rows(value, slice(panel * PANEL, (panel + 1) * PANEL), send_ref, keep_ref)


def add_kernel(first_ref, second_ref, send_ref, keep_ref):
    rows = send_ref.shape[0]
    keep_near = lax.axis_index("tensor") // 2 == lax.axis_index("req") // 2

    def total(at):
        cut = slice(at, at + rows)
        value = first_ref[cut].astype(jnp.float32) + second_ref[cut].astype(jnp.float32)
        return value.astype(send_ref.dtype)

    near, far = total(0), total(rows)
    send_ref[...] = jnp.where(keep_near, far, near)
    keep_ref[...] = jnp.where(keep_near, near, far)


def last_kernel(n_tensor, adapters, expand_ref, *refs):
    out_ref = refs[-1]
    count = (len(refs) - 1) // 2
    kept, got = refs[:count], refs[count:-1]
    wide, width = expand_ref.shape
    rank = wide // adapters

    def whole(cols):
        parts = [
            first[:, cols].astype(jnp.float32) + second[:, cols].astype(jnp.float32)
            for first, second in zip(kept, got)
        ]
        return jnp.concatenate(parts, axis=0)

    small = whole(slice(width, width + LANES))
    ids = small[:, rank : rank + 1] * (1.0 / n_tensor)
    lane = lax.broadcasted_iota(jnp.int32, small.shape, 1)
    shrink = jnp.where(lane < rank, small, 0.0)
    shrink = shrink + pltpu.roll(shrink, rank, 1)
    spread = jnp.concatenate([shrink] * (wide // LANES), axis=1)
    column = lax.broadcasted_iota(jnp.int32, spread.shape, 1) // rank
    placed = jnp.where(column.astype(jnp.float32) == ids, spread, 0.0).astype(jnp.bfloat16)
    for at in range(0, width, PANEL):
        cols = slice(at, at + PANEL)
        adapter = jnp.dot(placed, expand_ref[:, cols], preferred_element_type=jnp.float32)
        out_ref[:, cols] = (whole(cols) + adapter).astype(out_ref.dtype)


def paired(n_tensor, n_req, hidden, weight, shrink, expand, ids):
    rows, units = hidden.shape
    width = weight.shape[1]
    adapters, rank = shrink.shape[1:]
    wide = adapters * rank
    room = (units // LANES + 1) * LANES
    payload = width + LANES
    bf16 = jnp.bfloat16
    counts = [rows * part // 128 for part in PIECES]
    starts = [sum(counts[:at]) for at in range(len(counts))]
    quick = pl.CostEstimate(flops=1, bytes_accessed=1, transcendentals=0)

    def params(mib):
        return pltpu.CompilerParams(vmem_limit_bytes=mib * MIB)

    def struct(count, lanes):
        return jax.ShapeDtypeStruct((count, lanes), bf16)

    own, *pieces = pl.pallas_call(
        functools.partial(turn_kernel, starts),
        out_shape=[struct(rows, room)] + [struct(count, room) for count in counts],
        in_specs=[in_hbm(), in_hbm()],
        out_specs=[in_vmem()] * (1 + len(counts)),
        scratch_shapes=[
            pltpu.VMEM((units, rows), bf16),
            pltpu.VMEM((1, rows), jnp.int32),
            pltpu.SemaphoreType.DMA((units // LANES // TURN + 2,)),
        ],
        compiler_params=params(4),
        name="turn",
    )(left(hidden.T), left(ids.reshape(1, rows)))

    across = [(i, i ^ 2) for i in range(n_req)]
    beside = [(i, i ^ 1) for i in range(n_req)]
    next_z = [(i, i ^ 1) for i in range(n_tensor)]
    far_z = [(i, i ^ 2) for i in range(n_tensor)]

    direct = [lax.ppermute(pieces[0], "req", across)]
    other = lax.ppermute(own, "req", beside)

    shrink_rows = shrink.transpose(1, 2, 0).reshape(wide, units)
    token, *both = pl.pallas_call(
        load_kernel,
        out_shape=[jax.ShapeDtypeStruct((8, LANES), jnp.float32)]
        + [pltpu.VMEM((room, PANEL), bf16)] * (width // PANEL)
        + [pltpu.VMEM((room, wide), bf16)],
        in_specs=[in_hbm(), in_hbm()],
        out_specs=[in_vmem()] * (2 + width // PANEL),
        scratch_shapes=[
            pltpu.VMEM((wide, units), bf16),
            pltpu.SemaphoreType.DMA((width // PANEL,)),
            pltpu.SemaphoreType.DMA,
        ],
        compiler_params=params(10),
        cost_estimate=quick,
        name="load",
    )(left(weight), left(shrink_rows))

    def product(step, passed, token):
        return pl.pallas_call(
            functools.partial(product_kernel, adapters, units, starts[step]),
            out_shape=[struct(2 * counts[step], payload)] * 2,
            in_specs=[in_vmem()] * (4 + CUTS + len(both)),
            out_specs=[in_vmem()] * 2,
            compiler_params=params(4),
            cost_estimate=quick,
            name="product",
        )(token, own, other, direct[step], *passed, *both)

    def add(step, keep, got):
        return pl.pallas_call(
            add_kernel,
            out_shape=[struct(counts[step], payload)] * 2,
            in_specs=[in_vmem()] * 2,
            out_specs=[in_vmem()] * 2,
            compiler_params=params(4),
            cost_estimate=quick,
            name="add",
        )(keep, got)

    def over_core(part):
        tiles = room // LANES
        ends = [tiles * cut // CUTS * LANES for cut in range(CUTS + 1)]
        return [
            lax.ppermute(part[:, at:to], "req", beside) for at, to in zip(ends, ends[1:])
        ]

    after = lax.optimization_barrier
    steps = len(counts)
    direct[0], token = after((direct[0], token))
    parts, kept, gots = [], [], []

    def add_part(step):
        keep, got = parts[step]
        send, keep = add(step, keep, got)
        kept.append(keep)
        return send

    for step in range(steps):
        passed = over_core(direct[step])
        if step + 1 < steps:
            direct.append(lax.ppermute(pieces[step + 1], "req", across))
        send, keep = product(step, passed, token)
        hop = gots[step - 2 :] if step > 1 else []
        if step + 1 < steps:
            got = lax.ppermute(send, "tensor", next_z)
            direct[step + 1], keep, parts, hop = after((direct[step + 1], keep, parts, hop))
        else:
            send, parts, hop = after((send, parts, hop))
            got = lax.ppermute(send, "tensor", next_z)
        if step > 1:
            gots[step - 2 :] = hop
        if step > 0:
            send = add_part(step - 1)
            if step + 1 < steps:
                direct[step + 1], kept[-1] = after((direct[step + 1], kept[-1]))
            gots.append(lax.ppermute(send, "tensor", far_z))
        parts.append((keep, got))
    gots.append(lax.ppermute(add_part(steps - 1), "tensor", far_z))

    return pl.pallas_call(
        functools.partial(last_kernel, n_tensor, adapters),
        out_shape=struct(rows, width),
        in_specs=[in_vmem()] * (1 + 2 * steps),
        out_specs=in_vmem(),
        compiler_params=params(8),
        name="last",
    )(expand.reshape(wide, width), *kept, *gots)


def gathered(hidden, weight, shrink, expand, ids):
    rows, units = hidden.shape
    adapters, rank = shrink.shape[1:]
    width = weight.shape[1]
    columns = jnp.arange(adapters, dtype=jnp.int32)[None, :]
    onehot = (ids[:, None] == columns).astype(jnp.float32)
    every = jnp.dot(
        hidden, shrink.reshape(units, adapters * rank), preferred_element_type=jnp.float32
    )
    part = jnp.sum(every.reshape(rows, adapters, rank) * onehot[:, :, None], axis=1)
    all_ids = lax.all_gather(ids, "req", axis=0, tiled=True)
    base = jnp.dot(
        lax.all_gather(hidden, "req", axis=0, tiled=True),
        weight,
        preferred_element_type=jnp.float32,
    )
    base = lax.psum_scatter(
        base.astype(jnp.bfloat16), "tensor", scatter_dimension=0, tiled=True
    ).astype(jnp.float32)
    shrunk = lax.all_gather(
        lax.psum(part.astype(jnp.bfloat16), "tensor"), "req", axis=0, tiled=True
    )
    mine = base.shape[0]
    first = lax.axis_index("tensor") * mine
    shrunk = lax.dynamic_slice_in_dim(shrunk, first, mine, 0)
    mask = lax.dynamic_slice_in_dim(all_ids, first, mine, 0)[:, None] == columns
    placed = (shrunk[:, None, :] * mask.astype(jnp.bfloat16)[:, :, None]).reshape(
        mine, adapters * rank
    )
    adapter = jnp.dot(
        placed, expand.reshape(adapters * rank, width), preferred_element_type=jnp.float32
    )
    return (base + adapter).astype(jnp.bfloat16)


def solution(mesh):
    n_tensor, n_req = mesh.shape["tensor"], mesh.shape["req"]
    if n_tensor == 4 and n_req == 4:
        on_device = functools.partial(paired, n_tensor, n_req)
    else:
        on_device = gathered
    placed = (
        P(("rep", "req"), "tensor"),
        P("tensor", "req"),
        P("tensor", None, None),
        P(None, None, "req"),
        P(("rep", "req")),
    )
    return jax.shard_map(
        on_device,
        mesh=mesh,
        in_specs=placed,
        out_specs=P(("rep", "tensor"), "req"),
        check_vma=False,
    )
```

```python
import functools

import jax
import jax.numpy as jnp
from jax import lax
from jax.experimental import pallas as pl
from jax.experimental.pallas import tpu as pltpu
from jax.sharding import PartitionSpec as P

LANES = 128
PANEL = 512
DEPTH = 1024
TURN = 15
PIECES = (48, 32, 32, 16)
CUTS = 2
FULL = 128
MIB = 1 << 20


def in_vmem():
    return pl.BlockSpec(memory_space=pltpu.VMEM)


def in_hbm():
    return pl.BlockSpec(memory_space=pltpu.HBM)


def left(array):
    return pltpu.with_memory_space_constraint(array, pltpu.HBM)


def turn_kernel(starts, hidden_hbm, ids_hbm, own_ref, *refs):
    *piece_refs, hidden_ref, ids_ref, sems = refs
    units, rows = hidden_hbm.shape
    full = units // LANES
    stops = [at * LANES for at in range(0, full, TURN)] + [units]
    copies = [
        pltpu.make_async_copy(
            hidden_hbm.at[pl.ds(at, to - at)], hidden_ref.at[pl.ds(at, to - at)], sems.at[step]
        )
        for step, (at, to) in enumerate(zip(stops, stops[1:]))
    ]
    ids_copy = pltpu.make_async_copy(ids_hbm, ids_ref, sems.at[len(copies)])
    for copy in copies:
        copy.start()
    ids_copy.start()
    for step, copy in enumerate(copies):
        copy.wait()
        last = step == len(copies) - 1
        if last:
            ids_copy.wait()
        for block in range(stops[step] // LANES, full + 1 if last else stops[step + 1] // LANES):
            if block < full:
                tile = hidden_ref[block * LANES : (block + 1) * LANES, :]
            else:
                ids = jnp.broadcast_to(
                    ids_ref[...].astype(jnp.float32).astype(jnp.bfloat16),
                    ((full + 1) * LANES - units, rows),
                )
                tile = jnp.concatenate([hidden_ref[full * LANES :, :], ids], axis=0)
            turned = tile.T
            at = slice(block * LANES, (block + 1) * LANES)
            own_ref[:, at] = turned
            for first, piece_ref in zip(starts, piece_refs):
                piece_ref[:, at] = turned[first : first + piece_ref.shape[0]]


def load_kernel(w_hbm, s_hbm, token_ref, *refs):
    *panel_refs, spread_ref, s_ref, w_sems, s_sem = refs
    units = w_hbm.shape[0]
    copies = [
        pltpu.make_async_copy(
            w_hbm.at[:, pl.ds(panel * PANEL, PANEL)],
            panel_ref.at[pl.ds(0, units), :],
            w_sems.at[panel],
        )
        for panel, panel_ref in enumerate(panel_refs)
    ]
    s_copy = pltpu.make_async_copy(s_hbm, s_ref, s_sem)
    s_copy.start()
    for copy in copies:
        copy.start()
    token_ref[...] = jnp.zeros_like(token_ref)
    for ref in (spread_ref, *panel_refs):
        ref[units:, :] = jnp.zeros_like(ref[units:, :])
    s_copy.wait()
    for at in range(0, units, DEPTH):
        to = min(at + DEPTH, units)
        spread_ref[at:to, :] = s_ref[:, at:to].T
    for copy in copies:
        copy.wait()


def part_rows(value, cols, send_ref, keep_ref):
    rows = send_ref.shape[0] // 2
    keep_first = lax.rem(lax.axis_index("req"), 2) == lax.rem(lax.axis_index("tensor"), 2)
    value = value.astype(send_ref.dtype)
    for half in range(2):
        first = value[(2 * half) * rows : (2 * half + 1) * rows]
        second = value[(2 * half + 1) * rows : (2 * half + 2) * rows]
        at = slice(half * rows, (half + 1) * rows)
        send_ref[at, cols] = jnp.where(keep_first, second, first)
        keep_ref[at, cols] = jnp.where(keep_first, first, second)


def product_kernel(adapters, units, at, _, own_ref, other_ref, direct_ref, *refs):
    passed_refs, refs = refs[:CUTS], refs[CUTS:]
    *panel_refs, spread_ref, send_ref, keep_ref = refs
    rows = direct_ref.shape[0]
    width = send_ref.shape[1] - LANES
    wide = spread_ref.shape[1]
    rank = wide // adapters

    def piece():
        near = [own_ref[at : at + rows, :], other_ref[at : at + rows, :]]
        passed = jnp.concatenate([ref[...] for ref in passed_refs], axis=1)
        whole = [*near, direct_ref[...], passed]
        return jnp.concatenate(whole * max(1, FULL // (4 * rows)), axis=0)

    every = jnp.dot(piece(), spread_ref[...], preferred_element_type=jnp.float32)
    ids = piece()[:, units : units + 1].astype(jnp.float32)
    column = lax.broadcasted_iota(jnp.int32, every.shape, 1) // rank
    picked = jnp.where(column.astype(jnp.float32) == ids, every, 0.0)
    tile = picked[:, :LANES]
    for lane in range(LANES, wide, LANES):
        tile = tile + picked[:, lane : lane + LANES]
    tile = tile + pltpu.roll(tile, rank, 1)
    lane = lax.broadcasted_iota(jnp.int32, tile.shape, 1)
    tile = jnp.where(lane < rank, tile, ids)
    part_rows(tile, slice(width, width + LANES), send_ref, keep_ref)

    for panel, panel_ref in enumerate(panel_refs):
        value = jnp.dot(
            piece(), panel_ref[...], preferred_element_type=jnp.float32
        )
        part_rows(value, slice(panel * PANEL, (panel + 1) * PANEL), send_ref, keep_ref)


def add_kernel(first_ref, second_ref, send_ref, keep_ref):
    rows = send_ref.shape[0]
    keep_near = lax.axis_index("tensor") // 2 == lax.axis_index("req") // 2

    def total(at):
        cut = slice(at, at + rows)
        value = first_ref[cut].astype(jnp.float32) + second_ref[cut].astype(jnp.float32)
        return value.astype(send_ref.dtype)

    near, far = total(0), total(rows)
    send_ref[...] = jnp.where(keep_near, far, near)
    keep_ref[...] = jnp.where(keep_near, near, far)


def last_kernel(n_tensor, adapters, expand_ref, *refs):
    out_ref = refs[-1]
    count = (len(refs) - 1) // 2
    kept, got = refs[:count], refs[count:-1]
    wide, width = expand_ref.shape
    rank = wide // adapters

    def whole(cols):
        parts = [
            first[:, cols].astype(jnp.float32) + second[:, cols].astype(jnp.float32)
            for first, second in zip(kept, got)
        ]
        return jnp.concatenate(parts, axis=0)

    small = whole(slice(width, width + LANES))
    ids = small[:, rank : rank + 1] * (1.0 / n_tensor)
    lane = lax.broadcasted_iota(jnp.int32, small.shape, 1)
    shrink = jnp.where(lane < rank, small, 0.0)
    shrink = shrink + pltpu.roll(shrink, rank, 1)
    spread = jnp.concatenate([shrink] * (wide // LANES), axis=1)
    column = lax.broadcasted_iota(jnp.int32, spread.shape, 1) // rank
    placed = jnp.where(column.astype(jnp.float32) == ids, spread, 0.0).astype(jnp.bfloat16)
    for at in range(0, width, PANEL):
        cols = slice(at, at + PANEL)
        adapter = jnp.dot(placed, expand_ref[:, cols], preferred_element_type=jnp.float32)
        out_ref[:, cols] = (whole(cols) + adapter).astype(out_ref.dtype)


def paired(n_tensor, n_req, hidden, weight, shrink, expand, ids):
    rows, units = hidden.shape
    width = weight.shape[1]
    adapters, rank = shrink.shape[1:]
    wide = adapters * rank
    room = (units // LANES + 1) * LANES
    payload = width + LANES
    bf16 = jnp.bfloat16
    counts = [rows * part // 128 for part in PIECES]
    starts = [sum(counts[:at]) for at in range(len(counts))]
    quick = pl.CostEstimate(flops=1, bytes_accessed=1, transcendentals=0)

    def params(mib):
        return pltpu.CompilerParams(vmem_limit_bytes=mib * MIB)

    def struct(count, lanes):
        return jax.ShapeDtypeStruct((count, lanes), bf16)

    own, *pieces = pl.pallas_call(
        functools.partial(turn_kernel, starts),
        out_shape=[struct(rows, room)] + [struct(count, room) for count in counts],
        in_specs=[in_hbm(), in_hbm()],
        out_specs=[in_vmem()] * (1 + len(counts)),
        scratch_shapes=[
            pltpu.VMEM((units, rows), bf16),
            pltpu.VMEM((1, rows), jnp.int32),
            pltpu.SemaphoreType.DMA((units // LANES // TURN + 2,)),
        ],
        compiler_params=params(4),
        name="turn",
    )(left(hidden.T), left(ids.reshape(1, rows)))

    across = [(i, i ^ 2) for i in range(n_req)]
    beside = [(i, i ^ 1) for i in range(n_req)]
    next_z = [(i, i ^ 1) for i in range(n_tensor)]
    far_z = [(i, i ^ 2) for i in range(n_tensor)]

    direct = [lax.ppermute(pieces[0], "req", across)]
    other = lax.ppermute(own, "req", beside)

    shrink_rows = shrink.transpose(1, 2, 0).reshape(wide, units)
    token, *both = pl.pallas_call(
        load_kernel,
        out_shape=[jax.ShapeDtypeStruct((8, LANES), jnp.float32)]
        + [pltpu.VMEM((room, PANEL), bf16)] * (width // PANEL)
        + [pltpu.VMEM((room, wide), bf16)],
        in_specs=[in_hbm(), in_hbm()],
        out_specs=[in_vmem()] * (2 + width // PANEL),
        scratch_shapes=[
            pltpu.VMEM((wide, units), bf16),
            pltpu.SemaphoreType.DMA((width // PANEL,)),
            pltpu.SemaphoreType.DMA,
        ],
        compiler_params=params(10),
        cost_estimate=quick,
        name="load",
    )(left(weight), left(shrink_rows))

    def product(step, passed, token):
        return pl.pallas_call(
            functools.partial(product_kernel, adapters, units, starts[step]),
            out_shape=[struct(2 * counts[step], payload)] * 2,
            in_specs=[in_vmem()] * (4 + CUTS + len(both)),
            out_specs=[in_vmem()] * 2,
            compiler_params=params(4),
            cost_estimate=quick,
            name="product",
        )(token, own, other, direct[step], *passed, *both)

    def add(step, keep, got):
        return pl.pallas_call(
            add_kernel,
            out_shape=[struct(counts[step], payload)] * 2,
            in_specs=[in_vmem()] * 2,
            out_specs=[in_vmem()] * 2,
            compiler_params=params(4),
            cost_estimate=quick,
            name="add",
        )(keep, got)

    def over_core(part):
        tiles = room // LANES
        ends = [tiles * cut // CUTS * LANES for cut in range(CUTS + 1)]
        return [
            lax.ppermute(part[:, at:to], "req", beside) for at, to in zip(ends, ends[1:])
        ]

    after = lax.optimization_barrier
    steps = len(counts)
    direct[0], token = after((direct[0], token))
    parts, kept, gots = [], [], []

    def add_part(step):
        keep, got = parts[step]
        send, keep = add(step, keep, got)
        kept.append(keep)
        return send

    for step in range(steps):
        passed = over_core(direct[step])
        if step + 1 < steps:
            direct.append(lax.ppermute(pieces[step + 1], "req", across))
        send, keep = product(step, passed, token)
        late = step + 1 == steps
        hop = gots if late else []
        if step + 1 < steps:
            got = lax.ppermute(send, "tensor", next_z)
            direct[step + 1], keep, parts, hop = after((direct[step + 1], keep, parts, hop))
        else:
            got = lax.ppermute(send, "tensor", next_z)
            parts, hop = after((parts, hop))
        if late:
            gots = hop
        if step > 0:
            send = add_part(step - 1)
            if step + 1 < steps:
                direct[step + 1], kept[-1] = after((direct[step + 1], kept[-1]))
            gots.append(lax.ppermute(send, "tensor", far_z))
        parts.append((keep, got))
    gots.append(lax.ppermute(add_part(steps - 1), "tensor", far_z))

    return pl.pallas_call(
        functools.partial(last_kernel, n_tensor, adapters),
        out_shape=struct(rows, width),
        in_specs=[in_vmem()] * (1 + 2 * steps),
        out_specs=in_vmem(),
        compiler_params=params(8),
        name="last",
    )(expand.reshape(wide, width), *kept, *gots)


def gathered(hidden, weight, shrink, expand, ids):
    rows, units = hidden.shape
    adapters, rank = shrink.shape[1:]
    width = weight.shape[1]
    columns = jnp.arange(adapters, dtype=jnp.int32)[None, :]
    onehot = (ids[:, None] == columns).astype(jnp.float32)
    every = jnp.dot(
        hidden, shrink.reshape(units, adapters * rank), preferred_element_type=jnp.float32
    )
    part = jnp.sum(every.reshape(rows, adapters, rank) * onehot[:, :, None], axis=1)
    all_ids = lax.all_gather(ids, "req", axis=0, tiled=True)
    base = jnp.dot(
        lax.all_gather(hidden, "req", axis=0, tiled=True),
        weight,
        preferred_element_type=jnp.float32,
    )
    base = lax.psum_scatter(
        base.astype(jnp.bfloat16), "tensor", scatter_dimension=0, tiled=True
    ).astype(jnp.float32)
    shrunk = lax.all_gather(
        lax.psum(part.astype(jnp.bfloat16), "tensor"), "req", axis=0, tiled=True
    )
    mine = base.shape[0]
    first = lax.axis_index("tensor") * mine
    shrunk = lax.dynamic_slice_in_dim(shrunk, first, mine, 0)
    mask = lax.dynamic_slice_in_dim(all_ids, first, mine, 0)[:, None] == columns
    placed = (shrunk[:, None, :] * mask.astype(jnp.bfloat16)[:, :, None]).reshape(
        mine, adapters * rank
    )
    adapter = jnp.dot(
        placed, expand.reshape(adapters * rank, width), preferred_element_type=jnp.float32
    )
    return (base + adapter).astype(jnp.bfloat16)


def solution(mesh):
    n_tensor, n_req = mesh.shape["tensor"], mesh.shape["req"]
    if n_tensor == 4 and n_req == 4:
        on_device = functools.partial(paired, n_tensor, n_req)
    else:
        on_device = gathered
    placed = (
        P(("rep", "req"), "tensor"),
        P("tensor", "req"),
        P("tensor", None, None),
        P(None, None, "req"),
        P(("rep", "req")),
    )
    return jax.shard_map(
        on_device,
        mesh=mesh,
        in_specs=placed,
        out_specs=P(("rep", "tensor"), "req"),
        check_vma=False,
    )
```

```python
import functools

import jax
import jax.numpy as jnp
from jax import lax
from jax.experimental import pallas as pl
from jax.experimental.pallas import tpu as pltpu
from jax.sharding import PartitionSpec as P

LANES = 128
PANEL = 512
DEPTH = 1024
TURN = 15
PIECES = (32, 32, 32, 32)
CUTS = (2, 2, 2, 2)
HALVES = (1, 1, 1, 2)
MIB = 1 << 20


def in_vmem():
    return pl.BlockSpec(memory_space=pltpu.VMEM)


def in_hbm():
    return pl.BlockSpec(memory_space=pltpu.HBM)


def left(array):
    return pltpu.with_memory_space_constraint(array, pltpu.HBM)


def turn_kernel(starts, hidden_hbm, ids_hbm, own_ref, *refs):
    *piece_refs, hidden_ref, ids_ref, sems = refs
    units, rows = hidden_hbm.shape
    full = units // LANES
    stops = [at * LANES for at in range(0, full, TURN)] + [units]
    copies = [
        pltpu.make_async_copy(
            hidden_hbm.at[pl.ds(at, to - at)], hidden_ref.at[pl.ds(at, to - at)], sems.at[step]
        )
        for step, (at, to) in enumerate(zip(stops, stops[1:]))
    ]
    ids_copy = pltpu.make_async_copy(ids_hbm, ids_ref, sems.at[len(copies)])
    for copy in copies:
        copy.start()
    ids_copy.start()
    for step, copy in enumerate(copies):
        copy.wait()
        last = step == len(copies) - 1
        if last:
            ids_copy.wait()
        for block in range(stops[step] // LANES, full + 1 if last else stops[step + 1] // LANES):
            if block < full:
                tile = hidden_ref[block * LANES : (block + 1) * LANES, :]
            else:
                ids = jnp.broadcast_to(
                    ids_ref[...].astype(jnp.float32).astype(jnp.bfloat16),
                    ((full + 1) * LANES - units, rows),
                )
                tile = jnp.concatenate([hidden_ref[full * LANES :, :], ids], axis=0)
            turned = tile.T
            at = slice(block * LANES, (block + 1) * LANES)
            own_ref[:, at] = turned
            for first, piece_ref in zip(starts, piece_refs):
                piece_ref[:, at] = turned[first : first + piece_ref.shape[0]]


def load_kernel(w_hbm, s_hbm, token_ref, *refs):
    *panel_refs, spread_ref, s_ref, w_sems, s_sem = refs
    units = w_hbm.shape[0]
    copies = [
        pltpu.make_async_copy(
            w_hbm.at[:, pl.ds(panel * PANEL, PANEL)],
            panel_ref.at[pl.ds(0, units), :],
            w_sems.at[panel],
        )
        for panel, panel_ref in enumerate(panel_refs)
    ]
    s_copy = pltpu.make_async_copy(s_hbm, s_ref, s_sem)
    s_copy.start()
    for copy in copies:
        copy.start()
    token_ref[...] = jnp.zeros_like(token_ref)
    for ref in (spread_ref, *panel_refs):
        ref[units:, :] = jnp.zeros_like(ref[units:, :])
    s_copy.wait()
    for at in range(0, units, DEPTH):
        to = min(at + DEPTH, units)
        spread_ref[at:to, :] = s_ref[:, at:to].T
    for copy in copies:
        copy.wait()


def part_rows(value, cols, send_ref, keep_ref):
    rows = send_ref.shape[0] // 2
    keep_first = lax.rem(lax.axis_index("req"), 2) == lax.rem(lax.axis_index("tensor"), 2)
    value = value.astype(send_ref.dtype)
    for half in range(2):
        first = value[(2 * half) * rows : (2 * half + 1) * rows]
        second = value[(2 * half + 1) * rows : (2 * half + 2) * rows]
        at = slice(half * rows, (half + 1) * rows)
        send_ref[at, cols] = jnp.where(keep_first, second, first)
        keep_ref[at, cols] = jnp.where(keep_first, first, second)


def product_kernel(
    adapters, units, at, cuts, half, halves, _, own_ref, other_ref, direct_ref, *refs
):
    passed_refs, refs = refs[:cuts], refs[cuts:]
    *panel_refs, spread_ref, send_ref, keep_ref = refs
    count = len(panel_refs) // halves
    panel_refs = panel_refs[half * count : (half + 1) * count]
    rows = direct_ref.shape[0]

    def piece():
        near = [own_ref[at : at + rows, :], other_ref[at : at + rows, :]]
        passed = jnp.concatenate([ref[...] for ref in passed_refs], axis=1)
        return jnp.concatenate([*near, direct_ref[...], passed], axis=0)

    if half == 0:
        width = send_ref.shape[1] - LANES
        wide = spread_ref.shape[1]
        rank = wide // adapters
        every = jnp.dot(piece(), spread_ref[...], preferred_element_type=jnp.float32)
        ids = piece()[:, units : units + 1].astype(jnp.float32)
        column = lax.broadcasted_iota(jnp.int32, every.shape, 1) // rank
        picked = jnp.where(column.astype(jnp.float32) == ids, every, 0.0)
        tile = picked[:, :LANES]
        for lane in range(LANES, wide, LANES):
            tile = tile + picked[:, lane : lane + LANES]
        tile = tile + pltpu.roll(tile, rank, 1)
        lane = lax.broadcasted_iota(jnp.int32, tile.shape, 1)
        tile = jnp.where(lane < rank, tile, ids)
        part_rows(tile, slice(width, width + LANES), send_ref, keep_ref)

    for panel, panel_ref in enumerate(panel_refs):
        value = jnp.dot(piece(), panel_ref[...], preferred_element_type=jnp.float32)
        part_rows(value, slice(panel * PANEL, (panel + 1) * PANEL), send_ref, keep_ref)


def add_kernel(first_ref, second_ref, send_ref, keep_ref):
    rows = send_ref.shape[0]
    keep_near = lax.axis_index("tensor") // 2 == lax.axis_index("req") // 2

    def total(at):
        cut = slice(at, at + rows)
        value = first_ref[cut].astype(jnp.float32) + second_ref[cut].astype(jnp.float32)
        return value.astype(send_ref.dtype)

    near, far = total(0), total(rows)
    send_ref[...] = jnp.where(keep_near, far, near)
    keep_ref[...] = jnp.where(keep_near, near, far)


def last_kernel(n_tensor, adapters, halves, expand_ref, *refs):
    *sums, out_ref = refs
    wide, width = expand_ref.shape
    rank = wide // adapters
    pieces, at = [], 0
    for count in halves:
        pieces.append(sums[at : at + 2 * count])
        at += 2 * count

    def whole(first, lanes):
        parts = []
        for piece in pieces:
            step = 2 * width // len(piece)
            half = 0 if first == width else first // step
            start = step if first == width else first % step
            kept, got = piece[2 * half : 2 * half + 2]
            cols = slice(start, start + lanes)
            parts.append(kept[:, cols].astype(jnp.float32) + got[:, cols].astype(jnp.float32))
        return jnp.concatenate(parts, axis=0)

    small = whole(width, LANES)
    ids = small[:, rank : rank + 1] * (1.0 / n_tensor)
    lane = lax.broadcasted_iota(jnp.int32, small.shape, 1)
    shrink = jnp.where(lane < rank, small, 0.0)
    shrink = shrink + pltpu.roll(shrink, rank, 1)
    spread = jnp.concatenate([shrink] * (wide // LANES), axis=1)
    column = lax.broadcasted_iota(jnp.int32, spread.shape, 1) // rank
    placed = jnp.where(column.astype(jnp.float32) == ids, spread, 0.0).astype(jnp.bfloat16)
    for at in range(0, width, PANEL):
        cols = slice(at, at + PANEL)
        adapter = jnp.dot(placed, expand_ref[:, cols], preferred_element_type=jnp.float32)
        out_ref[:, cols] = (whole(at, PANEL) + adapter).astype(out_ref.dtype)


def paired(n_tensor, n_req, hidden, weight, shrink, expand, ids):
    rows, units = hidden.shape
    width = weight.shape[1]
    adapters, rank = shrink.shape[1:]
    wide = adapters * rank
    room = (units // LANES + 1) * LANES
    payload = width + LANES
    bf16 = jnp.bfloat16
    counts = [rows * part // 128 for part in PIECES]
    starts = [sum(counts[:at]) for at in range(len(counts))]
    quick = pl.CostEstimate(flops=1, bytes_accessed=1, transcendentals=0)

    def params(mib):
        return pltpu.CompilerParams(vmem_limit_bytes=mib * MIB)

    def struct(count, lanes):
        return jax.ShapeDtypeStruct((count, lanes), bf16)

    own, *pieces = pl.pallas_call(
        functools.partial(turn_kernel, starts),
        out_shape=[struct(rows, room)] + [struct(count, room) for count in counts],
        in_specs=[in_hbm(), in_hbm()],
        out_specs=[in_vmem()] * (1 + len(counts)),
        scratch_shapes=[
            pltpu.VMEM((units, rows), bf16),
            pltpu.VMEM((1, rows), jnp.int32),
            pltpu.SemaphoreType.DMA((units // LANES // TURN + 2,)),
        ],
        compiler_params=params(4),
        name="turn",
    )(left(hidden.T), left(ids.reshape(1, rows)))

    across = [(i, i ^ 2) for i in range(n_req)]
    beside = [(i, i ^ 1) for i in range(n_req)]
    next_z = [(i, i ^ 1) for i in range(n_tensor)]
    far_z = [(i, i ^ 2) for i in range(n_tensor)]

    direct = [lax.ppermute(pieces[0], "req", across)]
    other = lax.ppermute(own, "req", beside)

    shrink_rows = shrink.transpose(1, 2, 0).reshape(wide, units)
    token, *both = pl.pallas_call(
        load_kernel,
        out_shape=[jax.ShapeDtypeStruct((8, LANES), jnp.float32)]
        + [pltpu.VMEM((room, PANEL), bf16)] * (width // PANEL)
        + [pltpu.VMEM((room, wide), bf16)],
        in_specs=[in_hbm(), in_hbm()],
        out_specs=[in_vmem()] * (2 + width // PANEL),
        scratch_shapes=[
            pltpu.VMEM((wide, units), bf16),
            pltpu.SemaphoreType.DMA((width // PANEL,)),
            pltpu.SemaphoreType.DMA,
        ],
        compiler_params=params(10),
        cost_estimate=quick,
        name="load",
    )(left(weight), left(shrink_rows))

    def product(step, half, passed, token):
        count = width // PANEL // HALVES[step]
        lanes = count * PANEL + (LANES if half == 0 else 0)
        return pl.pallas_call(
            functools.partial(
                product_kernel, adapters, units, starts[step], len(passed), half, HALVES[step]
            ),
            out_shape=[struct(2 * counts[step], lanes)] * 2,
            in_specs=[in_vmem()] * (4 + len(passed) + len(both)),
            out_specs=[in_vmem()] * 2,
            compiler_params=params(4),
            cost_estimate=quick,
            name="product",
        )(token, own, other, direct[step], *passed, *both)

    def add(keep, got):
        half = (keep.shape[0] // 2, keep.shape[1])
        return pl.pallas_call(
            add_kernel,
            out_shape=[struct(*half)] * 2,
            in_specs=[in_vmem()] * 2,
            out_specs=[in_vmem()] * 2,
            compiler_params=params(4),
            cost_estimate=quick,
            name="add",
        )(keep, got)

    def over_core(part, cuts):
        tiles = room // LANES
        ends = [tiles * cut // cuts * LANES for cut in range(cuts + 1)]
        return [
            lax.ppermute(part[:, at:to], "req", beside) for at, to in zip(ends, ends[1:])
        ]

    def hop_next(send):
        return lax.ppermute(send, "tensor", next_z)

    def hop_far(send):
        return lax.ppermute(send, "tensor", far_z)

    after = lax.optimization_barrier
    steps = len(counts)
    direct[0], token = after((direct[0], token))
    parts, kept, gots = [], [], []
    for step in range(steps - 1):
        passed = over_core(direct[step], CUTS[step])
        direct.append(lax.ppermute(pieces[step + 1], "req", across))
        send, keep = product(step, 0, passed, token)
        got = hop_next(send)
        hops = gots[step - 2 :] if step > 1 else []
        keep, parts, hops = after((keep, parts, hops))
        if step > 1:
            gots[step - 2 :] = hops
        if step > 0:
            send, stays = add(*parts[step - 1])
            kept.append(stays)
            gots.append(hop_far(send))
        else:
            stays = keep
        direct[step + 1], stays = after((direct[step + 1], stays))
        if step > 0:
            kept[-1] = stays
        else:
            keep = stays
        parts.append((keep, got))

    passed = over_core(direct[-1], CUTS[-1])
    for half in range(HALVES[-1]):
        send, keep = product(steps - 1, half, passed, token)
        if half == 0:
            send, parts = after((send, parts))
        passed, keep, gots = after((passed, keep, gots))
        parts.append((keep, hop_next(send)))
    for keep, got in parts[steps - 2 :]:
        send, stays = add(keep, got)
        kept.append(stays)
        gots.append(hop_far(send))
    sums = [array for pair in zip(kept, gots) for array in pair]

    return pl.pallas_call(
        functools.partial(last_kernel, n_tensor, adapters, HALVES),
        out_shape=struct(rows, width),
        in_specs=[in_vmem()] * (1 + len(sums)),
        out_specs=in_vmem(),
        compiler_params=params(8),
        name="last",
    )(expand.reshape(wide, width), *sums)


def gathered(hidden, weight, shrink, expand, ids):
    rows, units = hidden.shape
    adapters, rank = shrink.shape[1:]
    width = weight.shape[1]
    columns = jnp.arange(adapters, dtype=jnp.int32)[None, :]
    onehot = (ids[:, None] == columns).astype(jnp.float32)
    every = jnp.dot(
        hidden, shrink.reshape(units, adapters * rank), preferred_element_type=jnp.float32
    )
    part = jnp.sum(every.reshape(rows, adapters, rank) * onehot[:, :, None], axis=1)
    all_ids = lax.all_gather(ids, "req", axis=0, tiled=True)
    base = jnp.dot(
        lax.all_gather(hidden, "req", axis=0, tiled=True),
        weight,
        preferred_element_type=jnp.float32,
    )
    base = lax.psum_scatter(
        base.astype(jnp.bfloat16), "tensor", scatter_dimension=0, tiled=True
    ).astype(jnp.float32)
    shrunk = lax.all_gather(
        lax.psum(part.astype(jnp.bfloat16), "tensor"), "req", axis=0, tiled=True
    )
    mine = base.shape[0]
    first = lax.axis_index("tensor") * mine
    shrunk = lax.dynamic_slice_in_dim(shrunk, first, mine, 0)
    mask = lax.dynamic_slice_in_dim(all_ids, first, mine, 0)[:, None] == columns
    placed = (shrunk[:, None, :] * mask.astype(jnp.bfloat16)[:, :, None]).reshape(
        mine, adapters * rank
    )
    adapter = jnp.dot(
        placed, expand.reshape(adapters * rank, width), preferred_element_type=jnp.float32
    )
    return (base + adapter).astype(jnp.bfloat16)


def solution(mesh):
    n_tensor, n_req = mesh.shape["tensor"], mesh.shape["req"]
    if n_tensor == 4 and n_req == 4:
        on_device = functools.partial(paired, n_tensor, n_req)
    else:
        on_device = gathered
    placed = (
        P(("rep", "req"), "tensor"),
        P("tensor", "req"),
        P("tensor", None, None),
        P(None, None, "req"),
        P(("rep", "req")),
    )
    return jax.shard_map(
        on_device,
        mesh=mesh,
        in_specs=placed,
        out_specs=P(("rep", "tensor"), "req"),
        check_vma=False,
    )
```

```python
import functools

import jax
import jax.numpy as jnp
from jax import lax
from jax.experimental import pallas as pl
from jax.experimental.pallas import tpu as pltpu
from jax.sharding import PartitionSpec as P

LANES = 128
PANEL = 512
DEPTH = 1024
TURN = 15
PIECES = (32, 32, 32, 32)
CUTS = 2
FULL = 128
SLOTS = 3
MIB = 1 << 20


def in_vmem():
    return pl.BlockSpec(memory_space=pltpu.VMEM)


def in_hbm():
    return pl.BlockSpec(memory_space=pltpu.HBM)


def left(array):
    return pltpu.with_memory_space_constraint(array, pltpu.HBM)


def turn_kernel(starts, hidden_hbm, ids_hbm, own_ref, *refs):
    *piece_refs, hidden_ref, ids_ref, sems = refs
    units, rows = hidden_hbm.shape
    full = units // LANES
    stops = [at * LANES for at in range(0, full, TURN)] + [units]
    copies = [
        pltpu.make_async_copy(
            hidden_hbm.at[pl.ds(at, to - at)], hidden_ref.at[pl.ds(at, to - at)], sems.at[step]
        )
        for step, (at, to) in enumerate(zip(stops, stops[1:]))
    ]
    ids_copy = pltpu.make_async_copy(ids_hbm, ids_ref, sems.at[len(copies)])
    for copy in copies:
        copy.start()
    ids_copy.start()
    for step, copy in enumerate(copies):
        copy.wait()
        last = step == len(copies) - 1
        if last:
            ids_copy.wait()
        for block in range(stops[step] // LANES, full + 1 if last else stops[step + 1] // LANES):
            if block < full:
                tile = hidden_ref[block * LANES : (block + 1) * LANES, :]
            else:
                ids = jnp.broadcast_to(
                    ids_ref[...].astype(jnp.float32).astype(jnp.bfloat16),
                    ((full + 1) * LANES - units, rows),
                )
                tile = jnp.concatenate([hidden_ref[full * LANES :, :], ids], axis=0)
            turned = tile.T
            at = slice(block * LANES, (block + 1) * LANES)
            own_ref[:, at] = turned
            for first, piece_ref in zip(starts, piece_refs):
                piece_ref[:, at] = turned[first : first + piece_ref.shape[0]]


def part_rows(value, cols, send_ref, keep_ref):
    rows = send_ref.shape[0]
    keep_first = lax.rem(lax.axis_index("req"), 2) == lax.rem(lax.axis_index("tensor"), 2)
    value = value.astype(send_ref.dtype)
    first, second = value[:rows], value[rows : 2 * rows]
    send_ref[:, cols] = jnp.where(keep_first, second, first)
    keep_ref[:, cols] = jnp.where(keep_first, first, second)


def base_panel(panel, piece, panel_ref, send_ref, keep_ref):
    value = jnp.dot(piece(), panel_ref[...], preferred_element_type=jnp.float32)
    part_rows(value, slice(panel * PANEL, (panel + 1) * PANEL), send_ref, keep_ref)


def shrink_panel(adapters, units, piece, spread_ref, send_ref, keep_ref):
    width = send_ref.shape[1] - LANES
    wide = spread_ref.shape[1]
    rank = wide // adapters
    every = jnp.dot(piece(), spread_ref[...], preferred_element_type=jnp.float32)
    ids = piece()[:, units : units + 1].astype(jnp.float32)
    column = lax.broadcasted_iota(jnp.int32, every.shape, 1) // rank
    picked = jnp.where(column.astype(jnp.float32) == ids, every, 0.0)
    tile = picked[:, :LANES]
    for lane in range(LANES, wide, LANES):
        tile = tile + picked[:, lane : lane + LANES]
    tile = tile + pltpu.roll(tile, rank, 1)
    lane = lax.broadcasted_iota(jnp.int32, tile.shape, 1)
    tile = jnp.where(lane < rank, tile, ids)
    part_rows(tile, slice(width, width + LANES), send_ref, keep_ref)


def near_kernel(adapters, own_ref, other_ref, w_hbm, s_hbm, send_ref, keep_ref, *refs):
    *panel_refs, spread_ref = refs[: -SLOTS - 3]
    *stage_refs, tail_ref, w_sems, s_sems = refs[-SLOTS - 3 :]
    units = w_hbm.shape[0]
    copies = [
        pltpu.make_async_copy(
            w_hbm.at[:, pl.ds(panel * PANEL, PANEL)],
            panel_ref.at[pl.ds(0, units), :],
            w_sems.at[panel],
        )
        for panel, panel_ref in enumerate(panel_refs)
    ]
    cuts = [(at, min(at + DEPTH, units)) for at in range(0, units, DEPTH)]
    stages = [
        stage_refs[step % SLOTS] if to - at == DEPTH else tail_ref
        for step, (at, to) in enumerate(cuts)
    ]
    s_copies = [
        pltpu.make_async_copy(s_hbm.at[:, pl.ds(at, to - at)], stage, s_sems.at[step])
        for step, ((at, to), stage) in enumerate(zip(cuts, stages))
    ]
    for copy in s_copies[:SLOTS]:
        copy.start()
    s_copies[-1].start()
    for copy in copies:
        copy.start()
    for ref in (spread_ref, *panel_refs):
        ref[units:, :] = jnp.zeros_like(ref[units:, :])

    def piece():
        return jnp.concatenate([own_ref[...], other_ref[...]], axis=0)

    for step, ((at, to), stage) in enumerate(zip(cuts, stages)):
        s_copies[step].wait()
        spread_ref[at:to, :] = stage[...].T
        if step + SLOTS < len(cuts) - 1:
            s_copies[step + SLOTS].start()
    shrink_panel(adapters, units, piece, spread_ref, send_ref, keep_ref)
    for panel, panel_ref in enumerate(panel_refs):
        copies[panel].wait()
        base_panel(panel, piece, panel_ref, send_ref, keep_ref)


def far_kernel(adapters, units, direct_ref, *refs):
    passed_refs, refs = refs[:CUTS], refs[CUTS:]
    *panel_refs, spread_ref, send_ref, keep_ref = refs

    def piece():
        passed = jnp.concatenate([ref[...] for ref in passed_refs], axis=1)
        both = jnp.concatenate([direct_ref[...], passed], axis=0)
        return jnp.concatenate([both] * max(1, FULL // both.shape[0]), axis=0)

    shrink_panel(adapters, units, piece, spread_ref, send_ref, keep_ref)
    for panel, panel_ref in enumerate(panel_refs):
        base_panel(panel, piece, panel_ref, send_ref, keep_ref)


def add_kernel(at, near_a, near_b, far_a, far_b, send_ref, keep_ref):
    rows = send_ref.shape[0]
    keep_near = lax.axis_index("tensor") // 2 == lax.axis_index("req") // 2

    def total(first_ref, second_ref, cut):
        value = first_ref[cut].astype(jnp.float32) + second_ref[cut].astype(jnp.float32)
        return value.astype(send_ref.dtype)

    near = total(near_a, near_b, slice(at, at + rows))
    far = total(far_a, far_b, slice(0, rows))
    send_ref[...] = jnp.where(keep_near, far, near)
    keep_ref[...] = jnp.where(keep_near, near, far)


def last_kernel(n_tensor, adapters, expand_ref, *refs):
    out_ref = refs[-1]
    count = (len(refs) - 1) // 2
    kept, got = refs[:count], refs[count:-1]
    wide, width = expand_ref.shape
    rank = wide // adapters

    def whole(cols):
        parts = [
            first[:, cols].astype(jnp.float32) + second[:, cols].astype(jnp.float32)
            for first, second in zip(kept, got)
        ]
        return jnp.concatenate(parts, axis=0)

    small = whole(slice(width, width + LANES))
    ids = small[:, rank : rank + 1] * (1.0 / n_tensor)
    lane = lax.broadcasted_iota(jnp.int32, small.shape, 1)
    shrink = jnp.where(lane < rank, small, 0.0)
    shrink = shrink + pltpu.roll(shrink, rank, 1)
    spread = jnp.concatenate([shrink] * (wide // LANES), axis=1)
    column = lax.broadcasted_iota(jnp.int32, spread.shape, 1) // rank
    placed = jnp.where(column.astype(jnp.float32) == ids, spread, 0.0).astype(jnp.bfloat16)
    for at in range(0, width, PANEL):
        cols = slice(at, at + PANEL)
        adapter = jnp.dot(placed, expand_ref[:, cols], preferred_element_type=jnp.float32)
        out_ref[:, cols] = (whole(cols) + adapter).astype(out_ref.dtype)


def paired(n_tensor, n_req, hidden, weight, shrink, expand, ids):
    rows, units = hidden.shape
    width = weight.shape[1]
    adapters, rank = shrink.shape[1:]
    wide = adapters * rank
    room = (units // LANES + 1) * LANES
    payload = width + LANES
    bf16 = jnp.bfloat16
    counts = [rows * part // 128 for part in PIECES]
    starts = [sum(counts[:at]) for at in range(len(counts))]
    quick = pl.CostEstimate(flops=1, bytes_accessed=1, transcendentals=0)

    def params(mib):
        return pltpu.CompilerParams(vmem_limit_bytes=mib * MIB)

    def struct(count, lanes):
        return jax.ShapeDtypeStruct((count, lanes), bf16)

    own, *pieces = pl.pallas_call(
        functools.partial(turn_kernel, starts),
        out_shape=[struct(rows, room)] + [struct(count, room) for count in counts],
        in_specs=[in_hbm(), in_hbm()],
        out_specs=[in_vmem()] * (1 + len(counts)),
        scratch_shapes=[
            pltpu.VMEM((units, rows), bf16),
            pltpu.VMEM((1, rows), jnp.int32),
            pltpu.SemaphoreType.DMA((units // LANES // TURN + 2,)),
        ],
        compiler_params=params(4),
        name="turn",
    )(left(hidden.T), left(ids.reshape(1, rows)))

    across = [(i, i ^ 2) for i in range(n_req)]
    beside = [(i, i ^ 1) for i in range(n_req)]
    next_z = [(i, i ^ 1) for i in range(n_tensor)]
    far_z = [(i, i ^ 2) for i in range(n_tensor)]

    direct = [lax.ppermute(pieces[0], "req", across)]
    other = lax.ppermute(own, "req", beside)

    shrink_rows = shrink.transpose(1, 2, 0).reshape(wide, units)
    near_send, near_keep, *both = pl.pallas_call(
        functools.partial(near_kernel, adapters),
        out_shape=[struct(rows, payload)] * 2
        + [pltpu.VMEM((room, PANEL), bf16)] * (width // PANEL)
        + [pltpu.VMEM((room, wide), bf16)],
        in_specs=[in_vmem(), in_vmem(), in_hbm(), in_hbm()],
        out_specs=[in_vmem()] * (3 + width // PANEL),
        scratch_shapes=[
            *[pltpu.VMEM((wide, DEPTH), bf16)] * SLOTS,
            pltpu.VMEM((wide, units % DEPTH), bf16),
            pltpu.SemaphoreType.DMA((width // PANEL,)),
            pltpu.SemaphoreType.DMA((units // DEPTH + 1,)),
        ],
        compiler_params=params(6),
        cost_estimate=quick,
        name="near",
    )(own, other, left(weight), left(shrink_rows))

    def product(step, passed):
        return pl.pallas_call(
            functools.partial(far_kernel, adapters, units),
            out_shape=[struct(counts[step], payload)] * 2,
            in_specs=[in_vmem()] * (1 + CUTS + len(both)),
            out_specs=[in_vmem()] * 2,
            compiler_params=params(4),
            cost_estimate=quick,
            name="far",
        )(direct[step], *passed, *both)

    def add(step, keep, got):
        return pl.pallas_call(
            functools.partial(add_kernel, starts[step]),
            out_shape=[struct(counts[step], payload)] * 2,
            in_specs=[in_vmem()] * 4,
            out_specs=[in_vmem()] * 2,
            compiler_params=params(4),
            cost_estimate=quick,
            name="add",
        )(near_keep, near_got, keep, got)

    def over_core(part):
        tiles = room // LANES
        ends = [tiles * cut // CUTS * LANES for cut in range(CUTS + 1)]
        return [
            lax.ppermute(part[:, at:to], "req", beside) for at, to in zip(ends, ends[1:])
        ]

    after = lax.optimization_barrier
    steps = len(counts)
    near_got = lax.ppermute(near_send, "tensor", next_z)
    direct[0], near_keep = after((direct[0], near_keep))
    parts, kept, gots = [], [], []

    def add_part(step):
        send, keep = add(step, *parts[step])
        kept.append(keep)
        return send

    for step in range(steps):
        passed = over_core(direct[step])
        if step + 1 < steps:
            direct.append(lax.ppermute(pieces[step + 1], "req", across))
        send, keep = product(step, passed)
        hop = gots[step - 2 :] if step > 1 else []
        if step + 1 < steps:
            got = lax.ppermute(send, "tensor", next_z)
            direct[step + 1], keep, parts, hop = after((direct[step + 1], keep, parts, hop))
        else:
            send, parts, hop = after((send, parts, hop))
            got = lax.ppermute(send, "tensor", next_z)
        if step > 1:
            gots[step - 2 :] = hop
        if step > 0:
            send = add_part(step - 1)
            if step + 1 < steps:
                direct[step + 1], kept[-1] = after((direct[step + 1], kept[-1]))
            gots.append(lax.ppermute(send, "tensor", far_z))
        parts.append((keep, got))
    gots.append(lax.ppermute(add_part(steps - 1), "tensor", far_z))

    return pl.pallas_call(
        functools.partial(last_kernel, n_tensor, adapters),
        out_shape=struct(rows, width),
        in_specs=[in_vmem()] * (1 + 2 * steps),
        out_specs=in_vmem(),
        compiler_params=params(8),
        name="last",
    )(expand.reshape(wide, width), *kept, *gots)


def gathered(hidden, weight, shrink, expand, ids):
    rows, units = hidden.shape
    adapters, rank = shrink.shape[1:]
    width = weight.shape[1]
    columns = jnp.arange(adapters, dtype=jnp.int32)[None, :]
    onehot = (ids[:, None] == columns).astype(jnp.float32)
    every = jnp.dot(
        hidden, shrink.reshape(units, adapters * rank), preferred_element_type=jnp.float32
    )
    part = jnp.sum(every.reshape(rows, adapters, rank) * onehot[:, :, None], axis=1)
    all_ids = lax.all_gather(ids, "req", axis=0, tiled=True)
    base = jnp.dot(
        lax.all_gather(hidden, "req", axis=0, tiled=True),
        weight,
        preferred_element_type=jnp.float32,
    )
    base = lax.psum_scatter(
        base.astype(jnp.bfloat16), "tensor", scatter_dimension=0, tiled=True
    ).astype(jnp.float32)
    shrunk = lax.all_gather(
        lax.psum(part.astype(jnp.bfloat16), "tensor"), "req", axis=0, tiled=True
    )
    mine = base.shape[0]
    first = lax.axis_index("tensor") * mine
    shrunk = lax.dynamic_slice_in_dim(shrunk, first, mine, 0)
    mask = lax.dynamic_slice_in_dim(all_ids, first, mine, 0)[:, None] == columns
    placed = (shrunk[:, None, :] * mask.astype(jnp.bfloat16)[:, :, None]).reshape(
        mine, adapters * rank
    )
    adapter = jnp.dot(
        placed, expand.reshape(adapters * rank, width), preferred_element_type=jnp.float32
    )
    return (base + adapter).astype(jnp.bfloat16)


def solution(mesh):
    n_tensor, n_req = mesh.shape["tensor"], mesh.shape["req"]
    if n_tensor == 4 and n_req == 4:
        on_device = functools.partial(paired, n_tensor, n_req)
    else:
        on_device = gathered
    placed = (
        P(("rep", "req"), "tensor"),
        P("tensor", "req"),
        P("tensor", None, None),
        P(None, None, "req"),
        P(("rep", "req")),
    )
    return jax.shard_map(
        on_device,
        mesh=mesh,
        in_specs=placed,
        out_specs=P(("rep", "tensor"), "req"),
        check_vma=False,
    )
```

```python
import functools

import jax
import jax.numpy as jnp
from jax import lax
from jax.experimental import pallas as pl
from jax.experimental.pallas import tpu as pltpu
from jax.sharding import PartitionSpec as P

LANES = 128
PANEL = 512
DEPTH = 1024
TURN = 15
PIECES = (48, 48, 32)
CUTS = 2
FULL = 128
SLOTS = 3
MIB = 1 << 20


def in_vmem():
    return pl.BlockSpec(memory_space=pltpu.VMEM)


def in_hbm():
    return pl.BlockSpec(memory_space=pltpu.HBM)


def left(array):
    return pltpu.with_memory_space_constraint(array, pltpu.HBM)


def turn_kernel(starts, hidden_hbm, ids_hbm, own_ref, *refs):
    *piece_refs, hidden_ref, ids_ref, sems = refs
    units, rows = hidden_hbm.shape
    full = units // LANES
    stops = [at * LANES for at in range(0, full, TURN)] + [units]
    copies = [
        pltpu.make_async_copy(
            hidden_hbm.at[pl.ds(at, to - at)], hidden_ref.at[pl.ds(at, to - at)], sems.at[step]
        )
        for step, (at, to) in enumerate(zip(stops, stops[1:]))
    ]
    ids_copy = pltpu.make_async_copy(ids_hbm, ids_ref, sems.at[len(copies)])
    for copy in copies:
        copy.start()
    ids_copy.start()
    for step, copy in enumerate(copies):
        copy.wait()
        last = step == len(copies) - 1
        if last:
            ids_copy.wait()
        for block in range(stops[step] // LANES, full + 1 if last else stops[step + 1] // LANES):
            if block < full:
                tile = hidden_ref[block * LANES : (block + 1) * LANES, :]
            else:
                ids = jnp.broadcast_to(
                    ids_ref[...].astype(jnp.float32).astype(jnp.bfloat16),
                    ((full + 1) * LANES - units, rows),
                )
                tile = jnp.concatenate([hidden_ref[full * LANES :, :], ids], axis=0)
            turned = tile.T
            at = slice(block * LANES, (block + 1) * LANES)
            own_ref[:, at] = turned
            for first, piece_ref in zip(starts, piece_refs):
                piece_ref[:, at] = turned[first : first + piece_ref.shape[0]]


def part_rows(value, cols, send_ref, keep_ref):
    rows = send_ref.shape[0]
    keep_first = lax.rem(lax.axis_index("req"), 2) == lax.rem(lax.axis_index("tensor"), 2)
    value = value.astype(send_ref.dtype)
    first, second = value[:rows], value[rows : 2 * rows]
    send_ref[:, cols] = jnp.where(keep_first, second, first)
    keep_ref[:, cols] = jnp.where(keep_first, first, second)


def dots(blocks, panel_ref):
    return jnp.concatenate(
        [jnp.dot(rows, panel_ref[...], preferred_element_type=jnp.float32) for rows in blocks],
        axis=0,
    )


def base_panel(panel, piece, panel_ref, send_ref, keep_ref):
    cols = slice(panel * PANEL, (panel + 1) * PANEL)
    part_rows(dots(piece(), panel_ref), cols, send_ref, keep_ref)


def shrink_panel(adapters, units, piece, spread_ref, send_ref, keep_ref):
    width = send_ref.shape[1] - LANES
    wide = spread_ref.shape[1]
    rank = wide // adapters
    every = dots(piece(), spread_ref)
    ids = [rows[:, units : units + 1] for rows in piece()]
    ids = jnp.concatenate(ids, axis=0).astype(jnp.float32)
    column = lax.broadcasted_iota(jnp.int32, every.shape, 1) // rank
    picked = jnp.where(column.astype(jnp.float32) == ids, every, 0.0)
    tile = picked[:, :LANES]
    for lane in range(LANES, wide, LANES):
        tile = tile + picked[:, lane : lane + LANES]
    tile = tile + pltpu.roll(tile, rank, 1)
    lane = lax.broadcasted_iota(jnp.int32, tile.shape, 1)
    tile = jnp.where(lane < rank, tile, ids)
    part_rows(tile, slice(width, width + LANES), send_ref, keep_ref)


def near_kernel(adapters, own_ref, other_ref, w_hbm, s_hbm, send_ref, keep_ref, *refs):
    *panel_refs, spread_ref = refs[: -SLOTS - 3]
    *stage_refs, tail_ref, w_sems, s_sems = refs[-SLOTS - 3 :]
    units = w_hbm.shape[0]
    copies = [
        pltpu.make_async_copy(
            w_hbm.at[:, pl.ds(panel * PANEL, PANEL)],
            panel_ref.at[pl.ds(0, units), :],
            w_sems.at[panel],
        )
        for panel, panel_ref in enumerate(panel_refs)
    ]
    cuts = [(at, min(at + DEPTH, units)) for at in range(0, units, DEPTH)]
    stages = [
        stage_refs[step % SLOTS] if to - at == DEPTH else tail_ref
        for step, (at, to) in enumerate(cuts)
    ]
    s_copies = [
        pltpu.make_async_copy(s_hbm.at[:, pl.ds(at, to - at)], stage, s_sems.at[step])
        for step, ((at, to), stage) in enumerate(zip(cuts, stages))
    ]
    for copy in s_copies[:SLOTS]:
        copy.start()
    s_copies[-1].start()
    for copy in copies:
        copy.start()
    for ref in (spread_ref, *panel_refs):
        ref[units:, :] = jnp.zeros_like(ref[units:, :])

    def piece():
        return [own_ref[...], other_ref[...]]

    for step, ((at, to), stage) in enumerate(zip(cuts, stages)):
        s_copies[step].wait()
        spread_ref[at:to, :] = stage[...].T
        if step + SLOTS < len(cuts) - 1:
            s_copies[step + SLOTS].start()
    shrink_panel(adapters, units, piece, spread_ref, send_ref, keep_ref)
    for panel, panel_ref in enumerate(panel_refs):
        copies[panel].wait()
        base_panel(panel, piece, panel_ref, send_ref, keep_ref)


def far_kernel(adapters, units, direct_ref, *refs):
    passed_refs, refs = refs[:CUTS], refs[CUTS:]
    *panel_refs, spread_ref, send_ref, keep_ref = refs

    def piece():
        passed = jnp.concatenate([ref[...] for ref in passed_refs], axis=1)
        rows = jnp.concatenate([direct_ref[...], passed], axis=0)
        room = max(0, FULL - rows.shape[0])
        return [jnp.concatenate([rows, rows[:room]], axis=0)]

    shrink_panel(adapters, units, piece, spread_ref, send_ref, keep_ref)
    for panel, panel_ref in enumerate(panel_refs):
        base_panel(panel, piece, panel_ref, send_ref, keep_ref)


def add_kernel(at, near_a, near_b, far_a, far_b, send_ref, keep_ref):
    rows = send_ref.shape[0]
    keep_near = lax.axis_index("tensor") // 2 == lax.axis_index("req") // 2

    def total(first_ref, second_ref, cut):
        value = first_ref[cut].astype(jnp.float32) + second_ref[cut].astype(jnp.float32)
        return value.astype(send_ref.dtype)

    near = total(near_a, near_b, slice(at, at + rows))
    far = total(far_a, far_b, slice(0, rows))
    send_ref[...] = jnp.where(keep_near, far, near)
    keep_ref[...] = jnp.where(keep_near, near, far)


def last_kernel(n_tensor, adapters, expand_ref, *refs):
    out_ref = refs[-1]
    count = (len(refs) - 1) // 2
    kept, got = refs[:count], refs[count:-1]
    wide, width = expand_ref.shape
    rank = wide // adapters

    def whole(cols):
        parts = [
            first[:, cols].astype(jnp.float32) + second[:, cols].astype(jnp.float32)
            for first, second in zip(kept, got)
        ]
        return jnp.concatenate(parts, axis=0)

    small = whole(slice(width, width + LANES))
    ids = small[:, rank : rank + 1] * (1.0 / n_tensor)
    lane = lax.broadcasted_iota(jnp.int32, small.shape, 1)
    shrink = jnp.where(lane < rank, small, 0.0)
    shrink = shrink + pltpu.roll(shrink, rank, 1)
    spread = jnp.concatenate([shrink] * (wide // LANES), axis=1)
    column = lax.broadcasted_iota(jnp.int32, spread.shape, 1) // rank
    placed = jnp.where(column.astype(jnp.float32) == ids, spread, 0.0).astype(jnp.bfloat16)
    for at in range(0, width, PANEL):
        cols = slice(at, at + PANEL)
        adapter = jnp.dot(placed, expand_ref[:, cols], preferred_element_type=jnp.float32)
        out_ref[:, cols] = (whole(cols) + adapter).astype(out_ref.dtype)


def paired(n_tensor, n_req, hidden, weight, shrink, expand, ids):
    rows, units = hidden.shape
    width = weight.shape[1]
    adapters, rank = shrink.shape[1:]
    wide = adapters * rank
    room = (units // LANES + 1) * LANES
    payload = width + LANES
    bf16 = jnp.bfloat16
    counts = [rows * part // 128 for part in PIECES]
    starts = [sum(counts[:at]) for at in range(len(counts))]
    quick = pl.CostEstimate(flops=1, bytes_accessed=1, transcendentals=0)

    def params(mib):
        return pltpu.CompilerParams(vmem_limit_bytes=mib * MIB)

    def struct(count, lanes):
        return jax.ShapeDtypeStruct((count, lanes), bf16)

    own, *pieces = pl.pallas_call(
        functools.partial(turn_kernel, starts),
        out_shape=[struct(rows, room)] + [struct(count, room) for count in counts],
        in_specs=[in_hbm(), in_hbm()],
        out_specs=[in_vmem()] * (1 + len(counts)),
        scratch_shapes=[
            pltpu.VMEM((units, rows), bf16),
            pltpu.VMEM((1, rows), jnp.int32),
            pltpu.SemaphoreType.DMA((units // LANES // TURN + 2,)),
        ],
        compiler_params=params(4),
        name="turn",
    )(left(hidden.T), left(ids.reshape(1, rows)))

    across = [(i, i ^ 2) for i in range(n_req)]
    beside = [(i, i ^ 1) for i in range(n_req)]
    next_z = [(i, i ^ 1) for i in range(n_tensor)]
    far_z = [(i, i ^ 2) for i in range(n_tensor)]

    direct = [lax.ppermute(pieces[0], "req", across)]
    other = lax.ppermute(own, "req", beside)

    shrink_rows = shrink.transpose(1, 2, 0).reshape(wide, units)
    near_send, near_keep, *both = pl.pallas_call(
        functools.partial(near_kernel, adapters),
        out_shape=[struct(rows, payload)] * 2
        + [pltpu.VMEM((room, PANEL), bf16)] * (width // PANEL)
        + [pltpu.VMEM((room, wide), bf16)],
        in_specs=[in_vmem(), in_vmem(), in_hbm(), in_hbm()],
        out_specs=[in_vmem()] * (3 + width // PANEL),
        scratch_shapes=[
            *[pltpu.VMEM((wide, DEPTH), bf16)] * SLOTS,
            pltpu.VMEM((wide, units % DEPTH), bf16),
            pltpu.SemaphoreType.DMA((width // PANEL,)),
            pltpu.SemaphoreType.DMA((units // DEPTH + 1,)),
        ],
        compiler_params=params(6),
        cost_estimate=quick,
        name="near",
    )(own, other, left(weight), left(shrink_rows))

    def product(step, passed):
        return pl.pallas_call(
            functools.partial(far_kernel, adapters, units),
            out_shape=[struct(counts[step], payload)] * 2,
            in_specs=[in_vmem()] * (1 + CUTS + len(both)),
            out_specs=[in_vmem()] * 2,
            compiler_params=params(4),
            cost_estimate=quick,
            name="far",
        )(direct[step], *passed, *both)

    def add(step, keep, got):
        return pl.pallas_call(
            functools.partial(add_kernel, starts[step]),
            out_shape=[struct(counts[step], payload)] * 2,
            in_specs=[in_vmem()] * 4,
            out_specs=[in_vmem()] * 2,
            compiler_params=params(4),
            cost_estimate=quick,
            name="add",
        )(near_keep, near_got, keep, got)

    def over_core(part):
        tiles = room // LANES
        ends = [tiles * cut // CUTS * LANES for cut in range(CUTS + 1)]
        return [
            lax.ppermute(part[:, at:to], "req", beside) for at, to in zip(ends, ends[1:])
        ]

    after = lax.optimization_barrier
    steps = len(counts)
    near_got = lax.ppermute(near_send, "tensor", next_z)
    direct[0], near_keep = after((direct[0], near_keep))
    kept, gots = [], []

    for step in range(steps):
        passed = over_core(direct[step])
        if step + 1 < steps:
            direct.append(lax.ppermute(pieces[step + 1], "req", across))
        send, keep = product(step, passed)
        got = lax.ppermute(send, "tensor", next_z)
        keep, got, gots = after((keep, got, gots))
        send, stays = add(step, keep, got)
        if step + 1 < steps:
            direct[step + 1], stays = after((direct[step + 1], stays))
        kept.append(stays)
        gots.append(lax.ppermute(send, "tensor", far_z))

    return pl.pallas_call(
        functools.partial(last_kernel, n_tensor, adapters),
        out_shape=struct(rows, width),
        in_specs=[in_vmem()] * (1 + 2 * steps),
        out_specs=in_vmem(),
        compiler_params=params(8),
        name="last",
    )(expand.reshape(wide, width), *kept, *gots)


def gathered(hidden, weight, shrink, expand, ids):
    rows, units = hidden.shape
    adapters, rank = shrink.shape[1:]
    width = weight.shape[1]
    columns = jnp.arange(adapters, dtype=jnp.int32)[None, :]
    onehot = (ids[:, None] == columns).astype(jnp.float32)
    every = jnp.dot(
        hidden, shrink.reshape(units, adapters * rank), preferred_element_type=jnp.float32
    )
    part = jnp.sum(every.reshape(rows, adapters, rank) * onehot[:, :, None], axis=1)
    all_ids = lax.all_gather(ids, "req", axis=0, tiled=True)
    base = jnp.dot(
        lax.all_gather(hidden, "req", axis=0, tiled=True),
        weight,
        preferred_element_type=jnp.float32,
    )
    base = lax.psum_scatter(
        base.astype(jnp.bfloat16), "tensor", scatter_dimension=0, tiled=True
    ).astype(jnp.float32)
    shrunk = lax.all_gather(
        lax.psum(part.astype(jnp.bfloat16), "tensor"), "req", axis=0, tiled=True
    )
    mine = base.shape[0]
    first = lax.axis_index("tensor") * mine
    shrunk = lax.dynamic_slice_in_dim(shrunk, first, mine, 0)
    mask = lax.dynamic_slice_in_dim(all_ids, first, mine, 0)[:, None] == columns
    placed = (shrunk[:, None, :] * mask.astype(jnp.bfloat16)[:, :, None]).reshape(
        mine, adapters * rank
    )
    adapter = jnp.dot(
        placed, expand.reshape(adapters * rank, width), preferred_element_type=jnp.float32
    )
    return (base + adapter).astype(jnp.bfloat16)


def solution(mesh):
    n_tensor, n_req = mesh.shape["tensor"], mesh.shape["req"]
    if n_tensor == 4 and n_req == 4:
        on_device = functools.partial(paired, n_tensor, n_req)
    else:
        on_device = gathered
    placed = (
        P(("rep", "req"), "tensor"),
        P("tensor", "req"),
        P("tensor", None, None),
        P(None, None, "req"),
        P(("rep", "req")),
    )
    return jax.shard_map(
        on_device,
        mesh=mesh,
        in_specs=placed,
        out_specs=P(("rep", "tensor"), "req"),
        check_vma=False,
    )
```

```python
import functools

import jax
import jax.numpy as jnp
from jax import lax
from jax.experimental import pallas as pl
from jax.experimental.pallas import tpu as pltpu
from jax.sharding import PartitionSpec as P

LANES = 128
PANEL = 512
DEPTH = 1024
TURN = 15
PIECES = (32, 32, 32, 32)
CUTS = (2, 2, 4, 4)
MIB = 1 << 20


def in_vmem():
    return pl.BlockSpec(memory_space=pltpu.VMEM)


def in_hbm():
    return pl.BlockSpec(memory_space=pltpu.HBM)


def left(array):
    return pltpu.with_memory_space_constraint(array, pltpu.HBM)


def turn_kernel(starts, hidden_hbm, ids_hbm, own_ref, *refs):
    *piece_refs, hidden_ref, ids_ref, sems = refs
    units, rows = hidden_hbm.shape
    full = units // LANES
    stops = [at * LANES for at in range(0, full, TURN)] + [units]
    copies = [
        pltpu.make_async_copy(
            hidden_hbm.at[pl.ds(at, to - at)], hidden_ref.at[pl.ds(at, to - at)], sems.at[step]
        )
        for step, (at, to) in enumerate(zip(stops, stops[1:]))
    ]
    ids_copy = pltpu.make_async_copy(ids_hbm, ids_ref, sems.at[len(copies)])
    for copy in copies:
        copy.start()
    ids_copy.start()
    for step, copy in enumerate(copies):
        copy.wait()
        last = step == len(copies) - 1
        if last:
            ids_copy.wait()
        for block in range(stops[step] // LANES, full + 1 if last else stops[step + 1] // LANES):
            if block < full:
                tile = hidden_ref[block * LANES : (block + 1) * LANES, :]
            else:
                ids = jnp.broadcast_to(
                    ids_ref[...].astype(jnp.float32).astype(jnp.bfloat16),
                    ((full + 1) * LANES - units, rows),
                )
                tile = jnp.concatenate([hidden_ref[full * LANES :, :], ids], axis=0)
            turned = tile.T
            at = slice(block * LANES, (block + 1) * LANES)
            own_ref[:, at] = turned
            for first, piece_ref in zip(starts, piece_refs):
                piece_ref[:, at] = turned[first : first + piece_ref.shape[0]]


def load_kernel(w_hbm, s_hbm, token_ref, *refs):
    *panel_refs, spread_ref, s_ref, w_sems, s_sem = refs
    units = w_hbm.shape[0]
    copies = [
        pltpu.make_async_copy(
            w_hbm.at[:, pl.ds(panel * PANEL, PANEL)],
            panel_ref.at[pl.ds(0, units), :],
            w_sems.at[panel],
        )
        for panel, panel_ref in enumerate(panel_refs)
    ]
    s_copy = pltpu.make_async_copy(s_hbm, s_ref, s_sem)
    s_copy.start()
    for copy in copies:
        copy.start()
    token_ref[...] = jnp.zeros_like(token_ref)
    for ref in (spread_ref, *panel_refs):
        ref[units:, :] = jnp.zeros_like(ref[units:, :])
    s_copy.wait()
    for at in range(0, units, DEPTH):
        to = min(at + DEPTH, units)
        spread_ref[at:to, :] = s_ref[:, at:to].T
    for copy in copies:
        copy.wait()


def part_rows(value, cols, send_ref, keep_ref):
    rows = send_ref.shape[0] // 2
    keep_first = lax.rem(lax.axis_index("req"), 2) == lax.rem(lax.axis_index("tensor"), 2)
    value = value.astype(send_ref.dtype)
    for half in range(2):
        first = value[(2 * half) * rows : (2 * half + 1) * rows]
        second = value[(2 * half + 1) * rows : (2 * half + 2) * rows]
        at = slice(half * rows, (half + 1) * rows)
        send_ref[at, cols] = jnp.where(keep_first, second, first)
        keep_ref[at, cols] = jnp.where(keep_first, first, second)


def product_kernel(adapters, units, at, cuts, _, own_ref, other_ref, direct_ref, *refs):
    passed_refs, refs = refs[:cuts], refs[cuts:]
    *panel_refs, spread_ref, send_ref, keep_ref = refs
    rows = direct_ref.shape[0]
    width = send_ref.shape[1] - LANES
    wide = spread_ref.shape[1]
    rank = wide // adapters

    def piece():
        near = [own_ref[at : at + rows, :], other_ref[at : at + rows, :]]
        passed = jnp.concatenate([ref[...] for ref in passed_refs], axis=1)
        return jnp.concatenate([*near, direct_ref[...], passed], axis=0)

    every = jnp.dot(piece(), spread_ref[...], preferred_element_type=jnp.float32)
    ids = piece()[:, units : units + 1].astype(jnp.float32)
    column = lax.broadcasted_iota(jnp.int32, every.shape, 1) // rank
    picked = jnp.where(column.astype(jnp.float32) == ids, every, 0.0)
    tile = picked[:, :LANES]
    for lane in range(LANES, wide, LANES):
        tile = tile + picked[:, lane : lane + LANES]
    tile = tile + pltpu.roll(tile, rank, 1)
    lane = lax.broadcasted_iota(jnp.int32, tile.shape, 1)
    tile = jnp.where(lane < rank, tile, ids)
    part_rows(tile, slice(width, width + LANES), send_ref, keep_ref)

    for panel, panel_ref in enumerate(panel_refs):
        value = jnp.dot(
            piece(), panel_ref[...], preferred_element_type=jnp.float32
        )
        part_rows(value, slice(panel * PANEL, (panel + 1) * PANEL), send_ref, keep_ref)


def add_kernel(first_ref, second_ref, send_ref, keep_ref):
    rows = send_ref.shape[0]
    keep_near = lax.axis_index("tensor") // 2 == lax.axis_index("req") // 2

    def total(at):
        cut = slice(at, at + rows)
        value = first_ref[cut].astype(jnp.float32) + second_ref[cut].astype(jnp.float32)
        return value.astype(send_ref.dtype)

    near, far = total(0), total(rows)
    send_ref[...] = jnp.where(keep_near, far, near)
    keep_ref[...] = jnp.where(keep_near, near, far)


def last_kernel(n_tensor, adapters, expand_ref, *refs):
    out_ref = refs[-1]
    count = (len(refs) - 1) // 2
    kept, got = refs[:count], refs[count:-1]
    wide, width = expand_ref.shape
    rank = wide // adapters

    def whole(cols):
        parts = [
            first[:, cols].astype(jnp.float32) + second[:, cols].astype(jnp.float32)
            for first, second in zip(kept, got)
        ]
        return jnp.concatenate(parts, axis=0)

    small = whole(slice(width, width + LANES))
    ids = small[:, rank : rank + 1] * (1.0 / n_tensor)
    lane = lax.broadcasted_iota(jnp.int32, small.shape, 1)
    shrink = jnp.where(lane < rank, small, 0.0)
    shrink = shrink + pltpu.roll(shrink, rank, 1)
    spread = jnp.concatenate([shrink] * (wide // LANES), axis=1)
    column = lax.broadcasted_iota(jnp.int32, spread.shape, 1) // rank
    placed = jnp.where(column.astype(jnp.float32) == ids, spread, 0.0).astype(jnp.bfloat16)
    for at in range(0, width, PANEL):
        cols = slice(at, at + PANEL)
        adapter = jnp.dot(placed, expand_ref[:, cols], preferred_element_type=jnp.float32)
        out_ref[:, cols] = (whole(cols) + adapter).astype(out_ref.dtype)


def paired(n_tensor, n_req, hidden, weight, shrink, expand, ids):
    rows, units = hidden.shape
    width = weight.shape[1]
    adapters, rank = shrink.shape[1:]
    wide = adapters * rank
    room = (units // LANES + 1) * LANES
    payload = width + LANES
    bf16 = jnp.bfloat16
    counts = [rows * part // 128 for part in PIECES]
    starts = [sum(counts[:at]) for at in range(len(counts))]
    quick = pl.CostEstimate(flops=1, bytes_accessed=1, transcendentals=0)

    def params(mib):
        return pltpu.CompilerParams(vmem_limit_bytes=mib * MIB)

    def struct(count, lanes):
        return jax.ShapeDtypeStruct((count, lanes), bf16)

    own, *pieces = pl.pallas_call(
        functools.partial(turn_kernel, starts),
        out_shape=[struct(rows, room)] + [struct(count, room) for count in counts],
        in_specs=[in_hbm(), in_hbm()],
        out_specs=[in_vmem()] * (1 + len(counts)),
        scratch_shapes=[
            pltpu.VMEM((units, rows), bf16),
            pltpu.VMEM((1, rows), jnp.int32),
            pltpu.SemaphoreType.DMA((units // LANES // TURN + 2,)),
        ],
        compiler_params=params(4),
        name="turn",
    )(left(hidden.T), left(ids.reshape(1, rows)))

    across = [(i, i ^ 2) for i in range(n_req)]
    beside = [(i, i ^ 1) for i in range(n_req)]
    next_z = [(i, i ^ 1) for i in range(n_tensor)]
    far_z = [(i, i ^ 2) for i in range(n_tensor)]

    direct = [lax.ppermute(pieces[0], "req", across)]
    other = lax.ppermute(own, "req", beside)

    shrink_rows = shrink.transpose(1, 2, 0).reshape(wide, units)
    token, *both = pl.pallas_call(
        load_kernel,
        out_shape=[jax.ShapeDtypeStruct((8, LANES), jnp.float32)]
        + [pltpu.VMEM((room, PANEL), bf16)] * (width // PANEL)
        + [pltpu.VMEM((room, wide), bf16)],
        in_specs=[in_hbm(), in_hbm()],
        out_specs=[in_vmem()] * (2 + width // PANEL),
        scratch_shapes=[
            pltpu.VMEM((wide, units), bf16),
            pltpu.SemaphoreType.DMA((width // PANEL,)),
            pltpu.SemaphoreType.DMA,
        ],
        compiler_params=params(10),
        cost_estimate=quick,
        name="load",
    )(left(weight), left(shrink_rows))

    def product(step, passed, token):
        return pl.pallas_call(
            functools.partial(product_kernel, adapters, units, starts[step], len(passed)),
            out_shape=[struct(2 * counts[step], payload)] * 2,
            in_specs=[in_vmem()] * (4 + len(passed) + len(both)),
            out_specs=[in_vmem()] * 2,
            compiler_params=params(4),
            cost_estimate=quick,
            name="product",
        )(token, own, other, direct[step], *passed, *both)

    def add(step, keep, got):
        return pl.pallas_call(
            add_kernel,
            out_shape=[struct(counts[step], payload)] * 2,
            in_specs=[in_vmem()] * 2,
            out_specs=[in_vmem()] * 2,
            compiler_params=params(4),
            cost_estimate=quick,
            name="add",
        )(keep, got)

    def over_core(part, cuts):
        tiles = room // LANES
        ends = [tiles * cut // cuts * LANES for cut in range(cuts + 1)]
        return [
            lax.ppermute(part[:, at:to], "req", beside) for at, to in zip(ends, ends[1:])
        ]

    after = lax.optimization_barrier
    steps = len(counts)
    direct[0], token = after((direct[0], token))
    parts, kept, gots = [], [], []

    def add_part(step):
        keep, got = parts[step]
        send, keep = add(step, keep, got)
        kept.append(keep)
        return send

    for step in range(steps):
        passed = over_core(direct[step], CUTS[step])
        if step + 1 < steps:
            direct.append(lax.ppermute(pieces[step + 1], "req", across))
        send, keep = product(step, passed, token)
        hop = gots[step - 2 :] if step > 1 else []
        if step + 1 < steps:
            got = lax.ppermute(send, "tensor", next_z)
            direct[step + 1], keep, parts, hop = after((direct[step + 1], keep, parts, hop))
        else:
            send, parts, hop = after((send, parts, hop))
            got = lax.ppermute(send, "tensor", next_z)
        if step > 1:
            gots[step - 2 :] = hop
        if step > 0:
            send = add_part(step - 1)
            if step + 1 < steps:
                direct[step + 1], kept[-1] = after((direct[step + 1], kept[-1]))
            gots.append(lax.ppermute(send, "tensor", far_z))
        parts.append((keep, got))
    gots.append(lax.ppermute(add_part(steps - 1), "tensor", far_z))

    return pl.pallas_call(
        functools.partial(last_kernel, n_tensor, adapters),
        out_shape=struct(rows, width),
        in_specs=[in_vmem()] * (1 + 2 * steps),
        out_specs=in_vmem(),
        compiler_params=params(8),
        name="last",
    )(expand.reshape(wide, width), *kept, *gots)


def gathered(hidden, weight, shrink, expand, ids):
    rows, units = hidden.shape
    adapters, rank = shrink.shape[1:]
    width = weight.shape[1]
    columns = jnp.arange(adapters, dtype=jnp.int32)[None, :]
    onehot = (ids[:, None] == columns).astype(jnp.float32)
    every = jnp.dot(
        hidden, shrink.reshape(units, adapters * rank), preferred_element_type=jnp.float32
    )
    part = jnp.sum(every.reshape(rows, adapters, rank) * onehot[:, :, None], axis=1)
    all_ids = lax.all_gather(ids, "req", axis=0, tiled=True)
    base = jnp.dot(
        lax.all_gather(hidden, "req", axis=0, tiled=True),
        weight,
        preferred_element_type=jnp.float32,
    )
    base = lax.psum_scatter(
        base.astype(jnp.bfloat16), "tensor", scatter_dimension=0, tiled=True
    ).astype(jnp.float32)
    shrunk = lax.all_gather(
        lax.psum(part.astype(jnp.bfloat16), "tensor"), "req", axis=0, tiled=True
    )
    mine = base.shape[0]
    first = lax.axis_index("tensor") * mine
    shrunk = lax.dynamic_slice_in_dim(shrunk, first, mine, 0)
    mask = lax.dynamic_slice_in_dim(all_ids, first, mine, 0)[:, None] == columns
    placed = (shrunk[:, None, :] * mask.astype(jnp.bfloat16)[:, :, None]).reshape(
        mine, adapters * rank
    )
    adapter = jnp.dot(
        placed, expand.reshape(adapters * rank, width), preferred_element_type=jnp.float32
    )
    return (base + adapter).astype(jnp.bfloat16)


def solution(mesh):
    n_tensor, n_req = mesh.shape["tensor"], mesh.shape["req"]
    if n_tensor == 4 and n_req == 4:
        on_device = functools.partial(paired, n_tensor, n_req)
    else:
        on_device = gathered
    placed = (
        P(("rep", "req"), "tensor"),
        P("tensor", "req"),
        P("tensor", None, None),
        P(None, None, "req"),
        P(("rep", "req")),
    )
    return jax.shard_map(
        on_device,
        mesh=mesh,
        in_specs=placed,
        out_specs=P(("rep", "tensor"), "req"),
        check_vma=False,
    )
```

```python
import functools

import jax
import jax.numpy as jnp
from jax import lax
from jax.experimental import pallas as pl
from jax.experimental.pallas import tpu as pltpu
from jax.sharding import PartitionSpec as P

LANES = 128
PANEL = 512
DEPTH = 1024
TURN = 15
PIECES = (32, 32, 32, 32)
CUTS = 2
FULL = 128
MIB = 1 << 20


def in_vmem():
    return pl.BlockSpec(memory_space=pltpu.VMEM)


def in_hbm():
    return pl.BlockSpec(memory_space=pltpu.HBM)


def left(array):
    return pltpu.with_memory_space_constraint(array, pltpu.HBM)


def turn_kernel(starts, hidden_hbm, ids_hbm, own_ref, *refs):
    *piece_refs, hidden_ref, ids_ref, sems = refs
    units, rows = hidden_hbm.shape
    full = units // LANES
    stops = [at * LANES for at in range(0, full, TURN)] + [units]
    copies = [
        pltpu.make_async_copy(
            hidden_hbm.at[pl.ds(at, to - at)], hidden_ref.at[pl.ds(at, to - at)], sems.at[step]
        )
        for step, (at, to) in enumerate(zip(stops, stops[1:]))
    ]
    ids_copy = pltpu.make_async_copy(ids_hbm, ids_ref, sems.at[len(copies)])
    for copy in copies:
        copy.start()
    ids_copy.start()
    for step, copy in enumerate(copies):
        copy.wait()
        last = step == len(copies) - 1
        if last:
            ids_copy.wait()
        for block in range(stops[step] // LANES, full + 1 if last else stops[step + 1] // LANES):
            if block < full:
                tile = hidden_ref[block * LANES : (block + 1) * LANES, :]
            else:
                ids = jnp.broadcast_to(
                    ids_ref[...].astype(jnp.float32).astype(jnp.bfloat16),
                    ((full + 1) * LANES - units, rows),
                )
                tile = jnp.concatenate([hidden_ref[full * LANES :, :], ids], axis=0)
            turned = tile.T
            at = slice(block * LANES, (block + 1) * LANES)
            own_ref[:, at] = turned
            for first, piece_ref in zip(starts, piece_refs):
                piece_ref[:, at] = turned[first : first + piece_ref.shape[0]]


def load_kernel(w_hbm, s_hbm, token_ref, *refs):
    *panel_refs, spread_ref, s_ref, w_sems, s_sem = refs
    units = w_hbm.shape[0]
    copies = [
        pltpu.make_async_copy(
            w_hbm.at[:, pl.ds(panel * PANEL, PANEL)],
            panel_ref.at[pl.ds(0, units), :],
            w_sems.at[panel],
        )
        for panel, panel_ref in enumerate(panel_refs)
    ]
    s_copy = pltpu.make_async_copy(s_hbm, s_ref, s_sem)
    s_copy.start()
    for copy in copies:
        copy.start()
    token_ref[...] = jnp.zeros_like(token_ref)
    for ref in (spread_ref, *panel_refs):
        ref[units:, :] = jnp.zeros_like(ref[units:, :])
    s_copy.wait()
    for at in range(0, units, DEPTH):
        to = min(at + DEPTH, units)
        spread_ref[at:to, :] = s_ref[:, at:to].T
    for copy in copies:
        copy.wait()


def part_rows(rows, value, cols, send_ref, keep_ref):
    keep_first = lax.rem(lax.axis_index("req"), 2) == lax.rem(lax.axis_index("tensor"), 2)
    value = value.astype(send_ref.dtype)
    for at in range(0, send_ref.shape[0], rows):
        first, second = value[2 * at : 2 * at + rows], value[2 * at + rows : 2 * at + 2 * rows]
        send_ref[at : at + rows, cols] = jnp.where(keep_first, second, first)
        keep_ref[at : at + rows, cols] = jnp.where(keep_first, first, second)


def product_kernel(adapters, units, nears, _, own_ref, other_ref, direct_ref, *refs):
    passed_refs, refs = refs[:CUTS], refs[CUTS:]
    *panel_refs, spread_ref, send_ref, keep_ref = refs
    rows = direct_ref.shape[0]
    width = send_ref.shape[1] - LANES
    wide = spread_ref.shape[1]
    rank = wide // adapters

    def piece():
        passed = jnp.concatenate([ref[...] for ref in passed_refs], axis=1)
        whole = [direct_ref[...], passed]
        for at in nears:
            whole += [ref[at : at + rows, :] for ref in (own_ref, other_ref)]
        return jnp.concatenate(whole * max(1, FULL // (rows * len(whole))), axis=0)

    every = jnp.dot(piece(), spread_ref[...], preferred_element_type=jnp.float32)
    ids = piece()[:, units : units + 1].astype(jnp.float32)
    column = lax.broadcasted_iota(jnp.int32, every.shape, 1) // rank
    picked = jnp.where(column.astype(jnp.float32) == ids, every, 0.0)
    tile = picked[:, :LANES]
    for lane in range(LANES, wide, LANES):
        tile = tile + picked[:, lane : lane + LANES]
    tile = tile + pltpu.roll(tile, rank, 1)
    lane = lax.broadcasted_iota(jnp.int32, tile.shape, 1)
    tile = jnp.where(lane < rank, tile, ids)
    part_rows(rows, tile, slice(width, width + LANES), send_ref, keep_ref)

    for panel, panel_ref in enumerate(panel_refs):
        value = jnp.dot(
            piece(), panel_ref[...], preferred_element_type=jnp.float32
        )
        part_rows(rows, value, slice(panel * PANEL, (panel + 1) * PANEL), send_ref, keep_ref)


def add_kernel(near_at, near_a, near_b, far_a, far_b, send_ref, keep_ref):
    rows = send_ref.shape[0]
    keep_near = lax.axis_index("tensor") // 2 == lax.axis_index("req") // 2

    def total(first_ref, second_ref, at):
        cut = slice(at, at + rows)
        value = first_ref[cut].astype(jnp.float32) + second_ref[cut].astype(jnp.float32)
        return value.astype(send_ref.dtype)

    near, far = total(near_a, near_b, near_at), total(far_a, far_b, 0)
    send_ref[...] = jnp.where(keep_near, far, near)
    keep_ref[...] = jnp.where(keep_near, near, far)


def last_kernel(n_tensor, adapters, expand_ref, *refs):
    out_ref = refs[-1]
    count = (len(refs) - 1) // 2
    kept, got = refs[:count], refs[count:-1]
    wide, width = expand_ref.shape
    rank = wide // adapters

    def whole(cols):
        parts = [
            first[:, cols].astype(jnp.float32) + second[:, cols].astype(jnp.float32)
            for first, second in zip(kept, got)
        ]
        return jnp.concatenate(parts, axis=0)

    small = whole(slice(width, width + LANES))
    ids = small[:, rank : rank + 1] * (1.0 / n_tensor)
    lane = lax.broadcasted_iota(jnp.int32, small.shape, 1)
    shrink = jnp.where(lane < rank, small, 0.0)
    shrink = shrink + pltpu.roll(shrink, rank, 1)
    spread = jnp.concatenate([shrink] * (wide // LANES), axis=1)
    column = lax.broadcasted_iota(jnp.int32, spread.shape, 1) // rank
    placed = jnp.where(column.astype(jnp.float32) == ids, spread, 0.0).astype(jnp.bfloat16)
    for at in range(0, width, PANEL):
        cols = slice(at, at + PANEL)
        adapter = jnp.dot(placed, expand_ref[:, cols], preferred_element_type=jnp.float32)
        out_ref[:, cols] = (whole(cols) + adapter).astype(out_ref.dtype)


def paired(n_tensor, n_req, hidden, weight, shrink, expand, ids):
    rows, units = hidden.shape
    width = weight.shape[1]
    adapters, rank = shrink.shape[1:]
    wide = adapters * rank
    room = (units // LANES + 1) * LANES
    payload = width + LANES
    bf16 = jnp.bfloat16
    counts = [rows * part // 128 for part in PIECES]
    starts = [sum(counts[:at]) for at in range(len(counts))]
    quick = pl.CostEstimate(flops=1, bytes_accessed=1, transcendentals=0)

    def params(mib):
        return pltpu.CompilerParams(vmem_limit_bytes=mib * MIB)

    def struct(count, lanes):
        return jax.ShapeDtypeStruct((count, lanes), bf16)

    own, *pieces = pl.pallas_call(
        functools.partial(turn_kernel, starts),
        out_shape=[struct(rows, room)] + [struct(count, room) for count in counts],
        in_specs=[in_hbm(), in_hbm()],
        out_specs=[in_vmem()] * (1 + len(counts)),
        scratch_shapes=[
            pltpu.VMEM((units, rows), bf16),
            pltpu.VMEM((1, rows), jnp.int32),
            pltpu.SemaphoreType.DMA((units // LANES // TURN + 2,)),
        ],
        compiler_params=params(4),
        name="turn",
    )(left(hidden.T), left(ids.reshape(1, rows)))

    across = [(i, i ^ 2) for i in range(n_req)]
    beside = [(i, i ^ 1) for i in range(n_req)]
    next_z = [(i, i ^ 1) for i in range(n_tensor)]
    far_z = [(i, i ^ 2) for i in range(n_tensor)]

    direct = [lax.ppermute(pieces[0], "req", across)]
    other = lax.ppermute(own, "req", beside)

    shrink_rows = shrink.transpose(1, 2, 0).reshape(wide, units)
    token, *both = pl.pallas_call(
        load_kernel,
        out_shape=[jax.ShapeDtypeStruct((8, LANES), jnp.float32)]
        + [pltpu.VMEM((room, PANEL), bf16)] * (width // PANEL)
        + [pltpu.VMEM((room, wide), bf16)],
        in_specs=[in_hbm(), in_hbm()],
        out_specs=[in_vmem()] * (2 + width // PANEL),
        scratch_shapes=[
            pltpu.VMEM((wide, units), bf16),
            pltpu.SemaphoreType.DMA((width // PANEL,)),
            pltpu.SemaphoreType.DMA,
        ],
        compiler_params=params(10),
        cost_estimate=quick,
        name="load",
    )(left(weight), left(shrink_rows))

    def product(step, passed, token):
        nears = [starts[step]] if step + 1 < len(counts) else []
        nears += [starts[-1]] if step == 0 else []
        return pl.pallas_call(
            functools.partial(product_kernel, adapters, units, nears),
            out_shape=[struct((1 + len(nears)) * counts[step], payload)] * 2,
            in_specs=[in_vmem()] * (4 + CUTS + len(both)),
            out_specs=[in_vmem()] * 2,
            compiler_params=params(4),
            cost_estimate=quick,
            name="product",
        )(token, own, other, direct[step], *passed, *both)

    def add(step):
        last = step + 1 == len(counts)
        near_at = counts[step] * (2 if last else 1)
        return pl.pallas_call(
            functools.partial(add_kernel, near_at),
            out_shape=[struct(counts[step], payload)] * 2,
            in_specs=[in_vmem()] * 4,
            out_specs=[in_vmem()] * 2,
            compiler_params=params(4),
            cost_estimate=quick,
            name="add",
        )(*parts[0 if last else step], *parts[step])

    def over_core(part):
        tiles = room // LANES
        ends = [tiles * cut // CUTS * LANES for cut in range(CUTS + 1)]
        return [
            lax.ppermute(part[:, at:to], "req", beside) for at, to in zip(ends, ends[1:])
        ]

    after = lax.optimization_barrier
    steps = len(counts)
    direct[0], token = after((direct[0], token))
    parts, kept, gots = [], [], []

    def add_part(step):
        send, keep = add(step)
        kept.append(keep)
        return send

    for step in range(steps):
        passed = over_core(direct[step])
        if step + 1 < steps:
            direct.append(lax.ppermute(pieces[step + 1], "req", across))
        send, keep = product(step, passed, token)
        hop = gots[step - 2 :] if step > 1 else []
        if step + 1 < steps:
            got = lax.ppermute(send, "tensor", next_z)
            direct[step + 1], keep, parts, hop = after((direct[step + 1], keep, parts, hop))
        else:
            got = lax.ppermute(send, "tensor", next_z)
            parts, hop = after((parts, hop))
        if step > 1:
            gots[step - 2 :] = hop
        if step > 0:
            send = add_part(step - 1)
            if step + 1 < steps:
                direct[step + 1], kept[-1] = after((direct[step + 1], kept[-1]))
            gots.append(lax.ppermute(send, "tensor", far_z))
        parts.append((keep, got))
    gots.append(lax.ppermute(add_part(steps - 1), "tensor", far_z))

    return pl.pallas_call(
        functools.partial(last_kernel, n_tensor, adapters),
        out_shape=struct(rows, width),
        in_specs=[in_vmem()] * (1 + 2 * steps),
        out_specs=in_vmem(),
        compiler_params=params(8),
        name="last",
    )(expand.reshape(wide, width), *kept, *gots)


def gathered(hidden, weight, shrink, expand, ids):
    rows, units = hidden.shape
    adapters, rank = shrink.shape[1:]
    width = weight.shape[1]
    columns = jnp.arange(adapters, dtype=jnp.int32)[None, :]
    onehot = (ids[:, None] == columns).astype(jnp.float32)
    every = jnp.dot(
        hidden, shrink.reshape(units, adapters * rank), preferred_element_type=jnp.float32
    )
    part = jnp.sum(every.reshape(rows, adapters, rank) * onehot[:, :, None], axis=1)
    all_ids = lax.all_gather(ids, "req", axis=0, tiled=True)
    base = jnp.dot(
        lax.all_gather(hidden, "req", axis=0, tiled=True),
        weight,
        preferred_element_type=jnp.float32,
    )
    base = lax.psum_scatter(
        base.astype(jnp.bfloat16), "tensor", scatter_dimension=0, tiled=True
    ).astype(jnp.float32)
    shrunk = lax.all_gather(
        lax.psum(part.astype(jnp.bfloat16), "tensor"), "req", axis=0, tiled=True
    )
    mine = base.shape[0]
    first = lax.axis_index("tensor") * mine
    shrunk = lax.dynamic_slice_in_dim(shrunk, first, mine, 0)
    mask = lax.dynamic_slice_in_dim(all_ids, first, mine, 0)[:, None] == columns
    placed = (shrunk[:, None, :] * mask.astype(jnp.bfloat16)[:, :, None]).reshape(
        mine, adapters * rank
    )
    adapter = jnp.dot(
        placed, expand.reshape(adapters * rank, width), preferred_element_type=jnp.float32
    )
    return (base + adapter).astype(jnp.bfloat16)


def solution(mesh):
    n_tensor, n_req = mesh.shape["tensor"], mesh.shape["req"]
    if n_tensor == 4 and n_req == 4:
        on_device = functools.partial(paired, n_tensor, n_req)
    else:
        on_device = gathered
    placed = (
        P(("rep", "req"), "tensor"),
        P("tensor", "req"),
        P("tensor", None, None),
        P(None, None, "req"),
        P(("rep", "req")),
    )
    return jax.shard_map(
        on_device,
        mesh=mesh,
        in_specs=placed,
        out_specs=P(("rep", "tensor"), "req"),
        check_vma=False,
    )
```

```python
import functools

import jax
import jax.numpy as jnp
from jax import lax
from jax.experimental import pallas as pl
from jax.experimental.pallas import tpu as pltpu
from jax.sharding import PartitionSpec as P

LANES = 128
PANEL = 512
DEPTH = 1024
TURN = 15
PIECES = (32, 32, 32, 32)
CUTS = 2
FULL = 128
EARLY = 2
MIB = 1 << 20


def in_vmem():
    return pl.BlockSpec(memory_space=pltpu.VMEM)


def in_hbm():
    return pl.BlockSpec(memory_space=pltpu.HBM)


def left(array):
    return pltpu.with_memory_space_constraint(array, pltpu.HBM)


def turn_kernel(starts, hidden_hbm, ids_hbm, own_ref, *refs):
    *piece_refs, hidden_ref, ids_ref, sems = refs
    units, rows = hidden_hbm.shape
    full = units // LANES
    stops = [at * LANES for at in range(0, full, TURN)] + [units]
    copies = [
        pltpu.make_async_copy(
            hidden_hbm.at[pl.ds(at, to - at)], hidden_ref.at[pl.ds(at, to - at)], sems.at[step]
        )
        for step, (at, to) in enumerate(zip(stops, stops[1:]))
    ]
    ids_copy = pltpu.make_async_copy(ids_hbm, ids_ref, sems.at[len(copies)])
    for copy in copies:
        copy.start()
    ids_copy.start()
    for step, copy in enumerate(copies):
        copy.wait()
        last = step == len(copies) - 1
        if last:
            ids_copy.wait()
        for block in range(stops[step] // LANES, full + 1 if last else stops[step + 1] // LANES):
            if block < full:
                tile = hidden_ref[block * LANES : (block + 1) * LANES, :]
            else:
                ids = jnp.broadcast_to(
                    ids_ref[...].astype(jnp.float32).astype(jnp.bfloat16),
                    ((full + 1) * LANES - units, rows),
                )
                tile = jnp.concatenate([hidden_ref[full * LANES :, :], ids], axis=0)
            turned = tile.T
            at = slice(block * LANES, (block + 1) * LANES)
            own_ref[:, at] = turned
            for first, piece_ref in zip(starts, piece_refs):
                piece_ref[:, at] = turned[first : first + piece_ref.shape[0]]


def load_kernel(w_hbm, s_hbm, token_ref, *refs):
    *panel_refs, spread_ref, s_ref, w_sems, s_sem = refs
    units = w_hbm.shape[0]
    copies = [
        pltpu.make_async_copy(
            w_hbm.at[:, pl.ds(panel * PANEL, PANEL)],
            panel_ref.at[pl.ds(0, units), :],
            w_sems.at[panel],
        )
        for panel, panel_ref in enumerate(panel_refs)
    ]
    s_copy = pltpu.make_async_copy(s_hbm, s_ref, s_sem)
    s_copy.start()
    for copy in copies:
        copy.start()
    token_ref[...] = jnp.zeros_like(token_ref)
    for ref in (spread_ref, *panel_refs):
        ref[units:, :] = jnp.zeros_like(ref[units:, :])
    s_copy.wait()
    for at in range(0, units, DEPTH):
        to = min(at + DEPTH, units)
        spread_ref[at:to, :] = s_ref[:, at:to].T
    for copy in copies:
        copy.wait()


def part_rows(rows, value, cols, send_ref, keep_ref):
    keep_first = lax.rem(lax.axis_index("req"), 2) == lax.rem(lax.axis_index("tensor"), 2)
    value = value.astype(send_ref.dtype)
    for at in range(0, send_ref.shape[0], rows):
        first, second = value[2 * at : 2 * at + rows], value[2 * at + rows : 2 * at + 2 * rows]
        send_ref[at : at + rows, cols] = jnp.where(keep_first, second, first)
        keep_ref[at : at + rows, cols] = jnp.where(keep_first, first, second)


def product_kernel(adapters, units, rows, far, nears, _, own_ref, other_ref, *refs):
    far_refs, refs = refs[: far * (1 + CUTS)], refs[far * (1 + CUTS) :]
    *panel_refs, spread_ref, send_ref, keep_ref = refs
    width = send_ref.shape[1] - LANES
    wide = spread_ref.shape[1]
    rank = wide // adapters

    def piece():
        whole = []
        if far:
            whole = [far_refs[0][...], jnp.concatenate([ref[...] for ref in far_refs[1:]], axis=1)]
        for at in nears:
            whole += [ref[at : at + rows, :] for ref in (own_ref, other_ref)]
        return jnp.concatenate(whole * max(1, FULL // (rows * len(whole))), axis=0)

    every = jnp.dot(piece(), spread_ref[...], preferred_element_type=jnp.float32)
    ids = piece()[:, units : units + 1].astype(jnp.float32)
    column = lax.broadcasted_iota(jnp.int32, every.shape, 1) // rank
    picked = jnp.where(column.astype(jnp.float32) == ids, every, 0.0)
    tile = picked[:, :LANES]
    for lane in range(LANES, wide, LANES):
        tile = tile + picked[:, lane : lane + LANES]
    tile = tile + pltpu.roll(tile, rank, 1)
    lane = lax.broadcasted_iota(jnp.int32, tile.shape, 1)
    tile = jnp.where(lane < rank, tile, ids)
    part_rows(rows, tile, slice(width, width + LANES), send_ref, keep_ref)

    for panel, panel_ref in enumerate(panel_refs):
        value = jnp.dot(
            piece(), panel_ref[...], preferred_element_type=jnp.float32
        )
        part_rows(rows, value, slice(panel * PANEL, (panel + 1) * PANEL), send_ref, keep_ref)


def add_kernel(near_at, near_a, near_b, far_a, far_b, send_ref, keep_ref):
    rows = send_ref.shape[0]
    keep_near = lax.axis_index("tensor") // 2 == lax.axis_index("req") // 2

    def total(first_ref, second_ref, at):
        cut = slice(at, at + rows)
        value = first_ref[cut].astype(jnp.float32) + second_ref[cut].astype(jnp.float32)
        return value.astype(send_ref.dtype)

    near, far = total(near_a, near_b, near_at), total(far_a, far_b, 0)
    send_ref[...] = jnp.where(keep_near, far, near)
    keep_ref[...] = jnp.where(keep_near, near, far)


def last_kernel(n_tensor, adapters, expand_ref, *refs):
    out_ref = refs[-1]
    count = (len(refs) - 1) // 2
    kept, got = refs[:count], refs[count:-1]
    wide, width = expand_ref.shape
    rank = wide // adapters

    def whole(cols):
        parts = [
            first[:, cols].astype(jnp.float32) + second[:, cols].astype(jnp.float32)
            for first, second in zip(kept, got)
        ]
        return jnp.concatenate(parts, axis=0)

    small = whole(slice(width, width + LANES))
    ids = small[:, rank : rank + 1] * (1.0 / n_tensor)
    lane = lax.broadcasted_iota(jnp.int32, small.shape, 1)
    shrink = jnp.where(lane < rank, small, 0.0)
    shrink = shrink + pltpu.roll(shrink, rank, 1)
    spread = jnp.concatenate([shrink] * (wide // LANES), axis=1)
    column = lax.broadcasted_iota(jnp.int32, spread.shape, 1) // rank
    placed = jnp.where(column.astype(jnp.float32) == ids, spread, 0.0).astype(jnp.bfloat16)
    for at in range(0, width, PANEL):
        cols = slice(at, at + PANEL)
        adapter = jnp.dot(placed, expand_ref[:, cols], preferred_element_type=jnp.float32)
        out_ref[:, cols] = (whole(cols) + adapter).astype(out_ref.dtype)


def paired(n_tensor, n_req, hidden, weight, shrink, expand, ids):
    rows, units = hidden.shape
    width = weight.shape[1]
    adapters, rank = shrink.shape[1:]
    wide = adapters * rank
    room = (units // LANES + 1) * LANES
    payload = width + LANES
    bf16 = jnp.bfloat16
    counts = [rows * part // 128 for part in PIECES]
    starts = [sum(counts[:at]) for at in range(len(counts))]
    quick = pl.CostEstimate(flops=1, bytes_accessed=1, transcendentals=0)

    def params(mib):
        return pltpu.CompilerParams(vmem_limit_bytes=mib * MIB)

    def struct(count, lanes):
        return jax.ShapeDtypeStruct((count, lanes), bf16)

    own, *pieces = pl.pallas_call(
        functools.partial(turn_kernel, starts),
        out_shape=[struct(rows, room)] + [struct(count, room) for count in counts],
        in_specs=[in_hbm(), in_hbm()],
        out_specs=[in_vmem()] * (1 + len(counts)),
        scratch_shapes=[
            pltpu.VMEM((units, rows), bf16),
            pltpu.VMEM((1, rows), jnp.int32),
            pltpu.SemaphoreType.DMA((units // LANES // TURN + 2,)),
        ],
        compiler_params=params(4),
        name="turn",
    )(left(hidden.T), left(ids.reshape(1, rows)))

    across = [(i, i ^ 2) for i in range(n_req)]
    beside = [(i, i ^ 1) for i in range(n_req)]
    next_z = [(i, i ^ 1) for i in range(n_tensor)]
    far_z = [(i, i ^ 2) for i in range(n_tensor)]

    direct = [lax.ppermute(pieces[0], "req", across)]
    other = lax.ppermute(own, "req", beside)

    shrink_rows = shrink.transpose(1, 2, 0).reshape(wide, units)
    token, *both = pl.pallas_call(
        load_kernel,
        out_shape=[jax.ShapeDtypeStruct((8, LANES), jnp.float32)]
        + [pltpu.VMEM((room, PANEL), bf16)] * (width // PANEL)
        + [pltpu.VMEM((room, wide), bf16)],
        in_specs=[in_hbm(), in_hbm()],
        out_specs=[in_vmem()] * (2 + width // PANEL),
        scratch_shapes=[
            pltpu.VMEM((wide, units), bf16),
            pltpu.SemaphoreType.DMA((width // PANEL,)),
            pltpu.SemaphoreType.DMA,
        ],
        compiler_params=params(10),
        cost_estimate=quick,
        name="load",
    )(left(weight), left(shrink_rows))

    def product(rows, nears, *far):
        return pl.pallas_call(
            functools.partial(product_kernel, adapters, units, rows, len(far) > 0, nears),
            out_shape=[struct((len(nears) + (len(far) > 0)) * rows, payload)] * 2,
            in_specs=[in_vmem()] * (3 + len(far) + len(both)),
            out_specs=[in_vmem()] * 2,
            compiler_params=params(4),
            cost_estimate=quick,
            name="product",
        )(token, own, other, *far, *both)

    def add(step):
        near, near_at = (parts[step], counts[step]) if step < EARLY else (late, late_at[step])
        return pl.pallas_call(
            functools.partial(add_kernel, near_at),
            out_shape=[struct(counts[step], payload)] * 2,
            in_specs=[in_vmem()] * 4,
            out_specs=[in_vmem()] * 2,
            compiler_params=params(4),
            cost_estimate=quick,
            name="add",
        )(*near, *parts[step])

    def over_core(part):
        tiles = room // LANES
        ends = [tiles * cut // CUTS * LANES for cut in range(CUTS + 1)]
        return [
            lax.ppermute(part[:, at:to], "req", beside) for at, to in zip(ends, ends[1:])
        ]

    after = lax.optimization_barrier
    steps = len(counts)
    direct[0], token = after((direct[0], token))
    parts, kept, gots = [], [], []

    def add_part(step):
        send, keep = add(step)
        kept.append(keep)
        return send

    late_at = {step: starts[step] - starts[EARLY] for step in range(EARLY, steps)}
    late_send, late_keep = product(counts[-1], starts[EARLY:])
    late = (late_keep, lax.ppermute(late_send, "tensor", next_z))
    for step in range(steps):
        passed = over_core(direct[step])
        if step == 0:
            passed, late_keep = after((passed, late_keep))
            late = (late_keep, late[1])
        if step + 1 < steps:
            direct.append(lax.ppermute(pieces[step + 1], "req", across))
        send, keep = product(
            counts[step], starts[step : step + 1] if step < EARLY else [], direct[step], *passed
        )
        hop = gots[step - 2 :] if step > 1 else []
        got = lax.ppermute(send, "tensor", next_z)
        if step + 1 < steps:
            direct[step + 1], keep, parts, hop = after((direct[step + 1], keep, parts, hop))
            if step == 0:
                direct[1], late = after((direct[1], late))
        else:
            parts, hop = after((parts, hop))
        if step > 1:
            gots[step - 2 :] = hop
        if step > 0:
            send = add_part(step - 1)
            if step + 1 < steps:
                direct[step + 1], kept[-1] = after((direct[step + 1], kept[-1]))
            gots.append(lax.ppermute(send, "tensor", far_z))
        parts.append((keep, got))
    gots.append(lax.ppermute(add_part(steps - 1), "tensor", far_z))

    return pl.pallas_call(
        functools.partial(last_kernel, n_tensor, adapters),
        out_shape=struct(rows, width),
        in_specs=[in_vmem()] * (1 + 2 * steps),
        out_specs=in_vmem(),
        compiler_params=params(8),
        name="last",
    )(expand.reshape(wide, width), *kept, *gots)


def gathered(hidden, weight, shrink, expand, ids):
    rows, units = hidden.shape
    adapters, rank = shrink.shape[1:]
    width = weight.shape[1]
    columns = jnp.arange(adapters, dtype=jnp.int32)[None, :]
    onehot = (ids[:, None] == columns).astype(jnp.float32)
    every = jnp.dot(
        hidden, shrink.reshape(units, adapters * rank), preferred_element_type=jnp.float32
    )
    part = jnp.sum(every.reshape(rows, adapters, rank) * onehot[:, :, None], axis=1)
    all_ids = lax.all_gather(ids, "req", axis=0, tiled=True)
    base = jnp.dot(
        lax.all_gather(hidden, "req", axis=0, tiled=True),
        weight,
        preferred_element_type=jnp.float32,
    )
    base = lax.psum_scatter(
        base.astype(jnp.bfloat16), "tensor", scatter_dimension=0, tiled=True
    ).astype(jnp.float32)
    shrunk = lax.all_gather(
        lax.psum(part.astype(jnp.bfloat16), "tensor"), "req", axis=0, tiled=True
    )
    mine = base.shape[0]
    first = lax.axis_index("tensor") * mine
    shrunk = lax.dynamic_slice_in_dim(shrunk, first, mine, 0)
    mask = lax.dynamic_slice_in_dim(all_ids, first, mine, 0)[:, None] == columns
    placed = (shrunk[:, None, :] * mask.astype(jnp.bfloat16)[:, :, None]).reshape(
        mine, adapters * rank
    )
    adapter = jnp.dot(
        placed, expand.reshape(adapters * rank, width), preferred_element_type=jnp.float32
    )
    return (base + adapter).astype(jnp.bfloat16)


def solution(mesh):
    n_tensor, n_req = mesh.shape["tensor"], mesh.shape["req"]
    if n_tensor == 4 and n_req == 4:
        on_device = functools.partial(paired, n_tensor, n_req)
    else:
        on_device = gathered
    placed = (
        P(("rep", "req"), "tensor"),
        P("tensor", "req"),
        P("tensor", None, None),
        P(None, None, "req"),
        P(("rep", "req")),
    )
    return jax.shard_map(
        on_device,
        mesh=mesh,
        in_specs=placed,
        out_specs=P(("rep", "tensor"), "req"),
        check_vma=False,
    )
```

```python
import functools

import jax
import jax.numpy as jnp
from jax import lax
from jax.experimental import pallas as pl
from jax.experimental.pallas import tpu as pltpu
from jax.sharding import PartitionSpec as P

LANES = 128
PANEL = 512
DEPTH = 1024
TURN = 15
PIECES = (32, 32, 32, 32)
CUTS = 2
FULL = 128
MIB = 1 << 20


def in_vmem():
    return pl.BlockSpec(memory_space=pltpu.VMEM)


def in_hbm():
    return pl.BlockSpec(memory_space=pltpu.HBM)


def left(array):
    return pltpu.with_memory_space_constraint(array, pltpu.HBM)


def turn_kernel(starts, hidden_hbm, ids_hbm, own_ref, *refs):
    *piece_refs, hidden_ref, ids_ref, sems = refs
    units, rows = hidden_hbm.shape
    full = units // LANES
    stops = [at * LANES for at in range(0, full, TURN)] + [units]
    copies = [
        pltpu.make_async_copy(
            hidden_hbm.at[pl.ds(at, to - at)], hidden_ref.at[pl.ds(at, to - at)], sems.at[step]
        )
        for step, (at, to) in enumerate(zip(stops, stops[1:]))
    ]
    ids_copy = pltpu.make_async_copy(ids_hbm, ids_ref, sems.at[len(copies)])
    for copy in copies:
        copy.start()
    ids_copy.start()
    for step, copy in enumerate(copies):
        copy.wait()
        last = step == len(copies) - 1
        if last:
            ids_copy.wait()
        for block in range(stops[step] // LANES, full + 1 if last else stops[step + 1] // LANES):
            if block < full:
                tile = hidden_ref[block * LANES : (block + 1) * LANES, :]
            else:
                ids = jnp.broadcast_to(
                    ids_ref[...].astype(jnp.float32).astype(jnp.bfloat16),
                    ((full + 1) * LANES - units, rows),
                )
                tile = jnp.concatenate([hidden_ref[full * LANES :, :], ids], axis=0)
            turned = tile.T
            at = slice(block * LANES, (block + 1) * LANES)
            own_ref[:, at] = turned
            for first, piece_ref in zip(starts, piece_refs):
                piece_ref[:, at] = turned[first : first + piece_ref.shape[0]]


def load_kernel(w_hbm, s_hbm, token_ref, *refs):
    *panel_refs, spread_ref, s_ref, w_sems, s_sem = refs
    units = w_hbm.shape[0]
    copies = [
        pltpu.make_async_copy(
            w_hbm.at[:, pl.ds(panel * PANEL, PANEL)],
            panel_ref.at[pl.ds(0, units), :],
            w_sems.at[panel],
        )
        for panel, panel_ref in enumerate(panel_refs)
    ]
    s_copy = pltpu.make_async_copy(s_hbm, s_ref, s_sem)
    s_copy.start()
    for copy in copies:
        copy.start()
    token_ref[...] = jnp.zeros_like(token_ref)
    for ref in (spread_ref, *panel_refs):
        ref[units:, :] = jnp.zeros_like(ref[units:, :])
    s_copy.wait()
    for at in range(0, units, DEPTH):
        to = min(at + DEPTH, units)
        spread_ref[at:to, :] = s_ref[:, at:to].T
    for copy in copies:
        copy.wait()


def part_rows(rows, value, cols, send_ref, keep_ref):
    keep_first = lax.rem(lax.axis_index("req"), 2) == lax.rem(lax.axis_index("tensor"), 2)
    value = value.astype(send_ref.dtype)
    for at in range(0, send_ref.shape[0], rows):
        first, second = value[2 * at : 2 * at + rows], value[2 * at + rows : 2 * at + 2 * rows]
        send_ref[at : at + rows, cols] = jnp.where(keep_first, second, first)
        keep_ref[at : at + rows, cols] = jnp.where(keep_first, first, second)


def product_kernel(adapters, units, nears, _, own_ref, other_ref, direct_ref, *refs):
    passed_refs, refs = refs[:CUTS], refs[CUTS:]
    *panel_refs, spread_ref, send_ref, keep_ref = refs
    rows = direct_ref.shape[0]
    width = send_ref.shape[1] - LANES
    wide = spread_ref.shape[1]
    rank = wide // adapters

    def piece():
        passed = jnp.concatenate([ref[...] for ref in passed_refs], axis=1)
        whole = [direct_ref[...], passed]
        for at in nears:
            whole += [ref[at : at + rows, :] for ref in (own_ref, other_ref)]
        return jnp.concatenate(whole * max(1, FULL // (rows * len(whole))), axis=0)

    every = jnp.dot(piece(), spread_ref[...], preferred_element_type=jnp.float32)
    ids = piece()[:, units : units + 1].astype(jnp.float32)
    column = lax.broadcasted_iota(jnp.int32, every.shape, 1) // rank
    picked = jnp.where(column.astype(jnp.float32) == ids, every, 0.0)
    tile = picked[:, :LANES]
    for lane in range(LANES, wide, LANES):
        tile = tile + picked[:, lane : lane + LANES]
    tile = tile + pltpu.roll(tile, rank, 1)
    lane = lax.broadcasted_iota(jnp.int32, tile.shape, 1)
    tile = jnp.where(lane < rank, tile, ids)
    part_rows(rows, tile, slice(width, width + LANES), send_ref, keep_ref)

    for panel, panel_ref in enumerate(panel_refs):
        value = jnp.dot(
            piece(), panel_ref[...], preferred_element_type=jnp.float32
        )
        part_rows(rows, value, slice(panel * PANEL, (panel + 1) * PANEL), send_ref, keep_ref)


def add_kernel(near_at, near_a, near_b, far_a, far_b, send_ref, keep_ref):
    rows = send_ref.shape[0]
    keep_near = lax.axis_index("tensor") // 2 == lax.axis_index("req") // 2

    def total(first_ref, second_ref, at):
        cut = slice(at, at + rows)
        value = first_ref[cut].astype(jnp.float32) + second_ref[cut].astype(jnp.float32)
        return value.astype(send_ref.dtype)

    near, far = total(near_a, near_b, near_at), total(far_a, far_b, 0)
    send_ref[...] = jnp.where(keep_near, far, near)
    keep_ref[...] = jnp.where(keep_near, near, far)


def last_kernel(n_tensor, adapters, expand_ref, *refs):
    out_ref = refs[-1]
    count = (len(refs) - 1) // 2
    kept, got = refs[:count], refs[count:-1]
    wide, width = expand_ref.shape
    rank = wide // adapters

    def whole(cols):
        parts = [
            first[:, cols].astype(jnp.float32) + second[:, cols].astype(jnp.float32)
            for first, second in zip(kept, got)
        ]
        return jnp.concatenate(parts, axis=0)

    small = whole(slice(width, width + LANES))
    ids = small[:, rank : rank + 1] * (1.0 / n_tensor)
    lane = lax.broadcasted_iota(jnp.int32, small.shape, 1)
    shrink = jnp.where(lane < rank, small, 0.0)
    shrink = shrink + pltpu.roll(shrink, rank, 1)
    spread = jnp.concatenate([shrink] * (wide // LANES), axis=1)
    column = lax.broadcasted_iota(jnp.int32, spread.shape, 1) // rank
    placed = jnp.where(column.astype(jnp.float32) == ids, spread, 0.0).astype(jnp.bfloat16)
    for at in range(0, width, PANEL):
        cols = slice(at, at + PANEL)
        adapter = jnp.dot(placed, expand_ref[:, cols], preferred_element_type=jnp.float32)
        out_ref[:, cols] = (whole(cols) + adapter).astype(out_ref.dtype)


def paired(n_tensor, n_req, hidden, weight, shrink, expand, ids):
    rows, units = hidden.shape
    width = weight.shape[1]
    adapters, rank = shrink.shape[1:]
    wide = adapters * rank
    room = (units // LANES + 1) * LANES
    payload = width + LANES
    bf16 = jnp.bfloat16
    counts = [rows * part // 128 for part in PIECES]
    starts = [sum(counts[:at]) for at in range(len(counts))]
    quick = pl.CostEstimate(flops=1, bytes_accessed=1, transcendentals=0)

    def params(mib):
        return pltpu.CompilerParams(vmem_limit_bytes=mib * MIB)

    def struct(count, lanes):
        return jax.ShapeDtypeStruct((count, lanes), bf16)

    own, *pieces = pl.pallas_call(
        functools.partial(turn_kernel, starts),
        out_shape=[struct(rows, room)] + [struct(count, room) for count in counts],
        in_specs=[in_hbm(), in_hbm()],
        out_specs=[in_vmem()] * (1 + len(counts)),
        scratch_shapes=[
            pltpu.VMEM((units, rows), bf16),
            pltpu.VMEM((1, rows), jnp.int32),
            pltpu.SemaphoreType.DMA((units // LANES // TURN + 2,)),
        ],
        compiler_params=params(4),
        name="turn",
    )(left(hidden.T), left(ids.reshape(1, rows)))

    across = [(i, i ^ 2) for i in range(n_req)]
    beside = [(i, i ^ 1) for i in range(n_req)]
    next_z = [(i, i ^ 1) for i in range(n_tensor)]
    far_z = [(i, i ^ 2) for i in range(n_tensor)]

    direct = [lax.ppermute(pieces[0], "req", across)]
    other = lax.ppermute(own, "req", beside)

    shrink_rows = shrink.transpose(1, 2, 0).reshape(wide, units)
    token, *both = pl.pallas_call(
        load_kernel,
        out_shape=[jax.ShapeDtypeStruct((8, LANES), jnp.float32)]
        + [pltpu.VMEM((room, PANEL), bf16)] * (width // PANEL)
        + [pltpu.VMEM((room, wide), bf16)],
        in_specs=[in_hbm(), in_hbm()],
        out_specs=[in_vmem()] * (2 + width // PANEL),
        scratch_shapes=[
            pltpu.VMEM((wide, units), bf16),
            pltpu.SemaphoreType.DMA((width // PANEL,)),
            pltpu.SemaphoreType.DMA,
        ],
        compiler_params=params(10),
        cost_estimate=quick,
        name="load",
    )(left(weight), left(shrink_rows))

    def product(step, passed, token):
        nears = [starts[step]] if step + 1 < len(counts) else []
        nears += [starts[-1]] if step == 0 else []
        return pl.pallas_call(
            functools.partial(product_kernel, adapters, units, nears),
            out_shape=[struct((1 + len(nears)) * counts[step], payload)] * 2,
            in_specs=[in_vmem()] * (4 + CUTS + len(both)),
            out_specs=[in_vmem()] * 2,
            compiler_params=params(4),
            cost_estimate=quick,
            name="product",
        )(token, own, other, direct[step], *passed, *both)

    def add(step):
        last = step + 1 == len(counts)
        near_at = counts[step] * (2 if last else 1)
        return pl.pallas_call(
            functools.partial(add_kernel, near_at),
            out_shape=[struct(counts[step], payload)] * 2,
            in_specs=[in_vmem()] * 4,
            out_specs=[in_vmem()] * 2,
            compiler_params=params(4),
            cost_estimate=quick,
            name="add",
        )(*parts[0 if last else step], *parts[step])

    def over_core(part):
        tiles = room // LANES
        ends = [tiles * cut // CUTS * LANES for cut in range(CUTS + 1)]
        return [
            lax.ppermute(part[:, at:to], "req", beside) for at, to in zip(ends, ends[1:])
        ]

    after = lax.optimization_barrier
    steps = len(counts)
    direct[0], token = after((direct[0], token))
    parts, kept, gots = [], [], []

    def add_part(step):
        send, keep = add(step)
        kept.append(keep)
        return send

    for step in range(steps):
        passed = over_core(direct[step])
        if step + 1 < steps:
            direct.append(lax.ppermute(pieces[step + 1], "req", across))
        send, keep = product(step, passed, token)
        hop = gots[step - 2 :] if step > 1 else []
        if step + 1 < steps:
            got = lax.ppermute(send, "tensor", next_z)
            direct[step + 1], keep, parts, hop = after((direct[step + 1], keep, parts, hop))
        else:
            got = lax.ppermute(send, "tensor", next_z)
        if step > 1 and step + 1 < steps:
            gots[step - 2 :] = hop
        if step > 0:
            send = add_part(step - 1)
            if step + 1 < steps:
                direct[step + 1], kept[-1] = after((direct[step + 1], kept[-1]))
            gots.append(lax.ppermute(send, "tensor", far_z))
        parts.append((keep, got))
    parts[-1], gots[-2] = after((parts[-1], gots[-2]))
    gots.append(lax.ppermute(add_part(steps - 1), "tensor", far_z))

    return pl.pallas_call(
        functools.partial(last_kernel, n_tensor, adapters),
        out_shape=struct(rows, width),
        in_specs=[in_vmem()] * (1 + 2 * steps),
        out_specs=in_vmem(),
        compiler_params=params(8),
        name="last",
    )(expand.reshape(wide, width), *kept, *gots)


def gathered(hidden, weight, shrink, expand, ids):
    rows, units = hidden.shape
    adapters, rank = shrink.shape[1:]
    width = weight.shape[1]
    columns = jnp.arange(adapters, dtype=jnp.int32)[None, :]
    onehot = (ids[:, None] == columns).astype(jnp.float32)
    every = jnp.dot(
        hidden, shrink.reshape(units, adapters * rank), preferred_element_type=jnp.float32
    )
    part = jnp.sum(every.reshape(rows, adapters, rank) * onehot[:, :, None], axis=1)
    all_ids = lax.all_gather(ids, "req", axis=0, tiled=True)
    base = jnp.dot(
        lax.all_gather(hidden, "req", axis=0, tiled=True),
        weight,
        preferred_element_type=jnp.float32,
    )
    base = lax.psum_scatter(
        base.astype(jnp.bfloat16), "tensor", scatter_dimension=0, tiled=True
    ).astype(jnp.float32)
    shrunk = lax.all_gather(
        lax.psum(part.astype(jnp.bfloat16), "tensor"), "req", axis=0, tiled=True
    )
    mine = base.shape[0]
    first = lax.axis_index("tensor") * mine
    shrunk = lax.dynamic_slice_in_dim(shrunk, first, mine, 0)
    mask = lax.dynamic_slice_in_dim(all_ids, first, mine, 0)[:, None] == columns
    placed = (shrunk[:, None, :] * mask.astype(jnp.bfloat16)[:, :, None]).reshape(
        mine, adapters * rank
    )
    adapter = jnp.dot(
        placed, expand.reshape(adapters * rank, width), preferred_element_type=jnp.float32
    )
    return (base + adapter).astype(jnp.bfloat16)


def solution(mesh):
    n_tensor, n_req = mesh.shape["tensor"], mesh.shape["req"]
    if n_tensor == 4 and n_req == 4:
        on_device = functools.partial(paired, n_tensor, n_req)
    else:
        on_device = gathered
    placed = (
        P(("rep", "req"), "tensor"),
        P("tensor", "req"),
        P("tensor", None, None),
        P(None, None, "req"),
        P(("rep", "req")),
    )
    return jax.shard_map(
        on_device,
        mesh=mesh,
        in_specs=placed,
        out_specs=P(("rep", "tensor"), "req"),
        check_vma=False,
    )
```

```python
import functools

import jax
import jax.numpy as jnp
from jax import lax
from jax.experimental import pallas as pl
from jax.experimental.pallas import tpu as pltpu
from jax.sharding import PartitionSpec as P

LANES = 128
PANEL = 512
DEPTH = 1024
TURN = 15
PIECES = (32, 32, 32, 32)
CUTS = (2, 2, 2, 1)
FULL = 128
MIB = 1 << 20


def in_vmem():
    return pl.BlockSpec(memory_space=pltpu.VMEM)


def in_hbm():
    return pl.BlockSpec(memory_space=pltpu.HBM)


def left(array):
    return pltpu.with_memory_space_constraint(array, pltpu.HBM)


def turn_kernel(starts, hidden_hbm, ids_hbm, own_ref, *refs):
    *piece_refs, hidden_ref, ids_ref, sems = refs
    units, rows = hidden_hbm.shape
    full = units // LANES
    stops = [at * LANES for at in range(0, full, TURN)] + [units]
    copies = [
        pltpu.make_async_copy(
            hidden_hbm.at[pl.ds(at, to - at)], hidden_ref.at[pl.ds(at, to - at)], sems.at[step]
        )
        for step, (at, to) in enumerate(zip(stops, stops[1:]))
    ]
    ids_copy = pltpu.make_async_copy(ids_hbm, ids_ref, sems.at[len(copies)])
    for copy in copies:
        copy.start()
    ids_copy.start()
    for step, copy in enumerate(copies):
        copy.wait()
        last = step == len(copies) - 1
        if last:
            ids_copy.wait()
        for block in range(stops[step] // LANES, full + 1 if last else stops[step + 1] // LANES):
            if block < full:
                tile = hidden_ref[block * LANES : (block + 1) * LANES, :]
            else:
                ids = jnp.broadcast_to(
                    ids_ref[...].astype(jnp.float32).astype(jnp.bfloat16),
                    ((full + 1) * LANES - units, rows),
                )
                tile = jnp.concatenate([hidden_ref[full * LANES :, :], ids], axis=0)
            turned = tile.T
            at = slice(block * LANES, (block + 1) * LANES)
            own_ref[:, at] = turned
            for first, piece_ref in zip(starts, piece_refs):
                piece_ref[:, at] = turned[first : first + piece_ref.shape[0]]


def load_kernel(w_hbm, s_hbm, token_ref, *refs):
    *panel_refs, spread_ref, s_ref, w_sems, s_sem = refs
    units = w_hbm.shape[0]
    copies = [
        pltpu.make_async_copy(
            w_hbm.at[:, pl.ds(panel * PANEL, PANEL)],
            panel_ref.at[pl.ds(0, units), :],
            w_sems.at[panel],
        )
        for panel, panel_ref in enumerate(panel_refs)
    ]
    s_copy = pltpu.make_async_copy(s_hbm, s_ref, s_sem)
    s_copy.start()
    for copy in copies:
        copy.start()
    token_ref[...] = jnp.zeros_like(token_ref)
    for ref in (spread_ref, *panel_refs):
        ref[units:, :] = jnp.zeros_like(ref[units:, :])
    s_copy.wait()
    for at in range(0, units, DEPTH):
        to = min(at + DEPTH, units)
        spread_ref[at:to, :] = s_ref[:, at:to].T
    for copy in copies:
        copy.wait()


def part_rows(rows, value, cols, send_ref, keep_ref):
    keep_first = lax.rem(lax.axis_index("req"), 2) == lax.rem(lax.axis_index("tensor"), 2)
    value = value.astype(send_ref.dtype)
    for at in range(0, send_ref.shape[0], rows):
        first, second = value[2 * at : 2 * at + rows], value[2 * at + rows : 2 * at + 2 * rows]
        send_ref[at : at + rows, cols] = jnp.where(keep_first, second, first)
        keep_ref[at : at + rows, cols] = jnp.where(keep_first, first, second)


def product_kernel(adapters, units, cuts, nears, _, own_ref, other_ref, direct_ref, *refs):
    passed_refs, refs = refs[:cuts], refs[cuts:]
    *panel_refs, spread_ref, send_ref, keep_ref = refs
    rows = direct_ref.shape[0]
    width = send_ref.shape[1] - LANES
    wide = spread_ref.shape[1]
    rank = wide // adapters

    def piece():
        passed = jnp.concatenate([ref[...] for ref in passed_refs], axis=1)
        whole = [direct_ref[...], passed]
        for at in nears:
            whole += [ref[at : at + rows, :] for ref in (own_ref, other_ref)]
        return jnp.concatenate(whole * max(1, FULL // (rows * len(whole))), axis=0)

    every = jnp.dot(piece(), spread_ref[...], preferred_element_type=jnp.float32)
    ids = piece()[:, units : units + 1].astype(jnp.float32)
    column = lax.broadcasted_iota(jnp.int32, every.shape, 1) // rank
    picked = jnp.where(column.astype(jnp.float32) == ids, every, 0.0)
    tile = picked[:, :LANES]
    for lane in range(LANES, wide, LANES):
        tile = tile + picked[:, lane : lane + LANES]
    tile = tile + pltpu.roll(tile, rank, 1)
    lane = lax.broadcasted_iota(jnp.int32, tile.shape, 1)
    tile = jnp.where(lane < rank, tile, ids)
    part_rows(rows, tile, slice(width, width + LANES), send_ref, keep_ref)

    for panel, panel_ref in enumerate(panel_refs):
        value = jnp.dot(
            piece(), panel_ref[...], preferred_element_type=jnp.float32
        )
        part_rows(rows, value, slice(panel * PANEL, (panel + 1) * PANEL), send_ref, keep_ref)


def add_kernel(near_at, near_a, near_b, far_a, far_b, send_ref, keep_ref):
    rows = send_ref.shape[0]
    keep_near = lax.axis_index("tensor") // 2 == lax.axis_index("req") // 2

    def total(first_ref, second_ref, at):
        cut = slice(at, at + rows)
        value = first_ref[cut].astype(jnp.float32) + second_ref[cut].astype(jnp.float32)
        return value.astype(send_ref.dtype)

    near, far = total(near_a, near_b, near_at), total(far_a, far_b, 0)
    send_ref[...] = jnp.where(keep_near, far, near)
    keep_ref[...] = jnp.where(keep_near, near, far)


def last_kernel(n_tensor, adapters, expand_ref, *refs):
    out_ref = refs[-1]
    count = (len(refs) - 1) // 2
    kept, got = refs[:count], refs[count:-1]
    wide, width = expand_ref.shape
    rank = wide // adapters

    def whole(cols):
        parts = [
            first[:, cols].astype(jnp.float32) + second[:, cols].astype(jnp.float32)
            for first, second in zip(kept, got)
        ]
        return jnp.concatenate(parts, axis=0)

    small = whole(slice(width, width + LANES))
    ids = small[:, rank : rank + 1] * (1.0 / n_tensor)
    lane = lax.broadcasted_iota(jnp.int32, small.shape, 1)
    shrink = jnp.where(lane < rank, small, 0.0)
    shrink = shrink + pltpu.roll(shrink, rank, 1)
    spread = jnp.concatenate([shrink] * (wide // LANES), axis=1)
    column = lax.broadcasted_iota(jnp.int32, spread.shape, 1) // rank
    placed = jnp.where(column.astype(jnp.float32) == ids, spread, 0.0).astype(jnp.bfloat16)
    for at in range(0, width, PANEL):
        cols = slice(at, at + PANEL)
        adapter = jnp.dot(placed, expand_ref[:, cols], preferred_element_type=jnp.float32)
        out_ref[:, cols] = (whole(cols) + adapter).astype(out_ref.dtype)


def paired(n_tensor, n_req, hidden, weight, shrink, expand, ids):
    rows, units = hidden.shape
    width = weight.shape[1]
    adapters, rank = shrink.shape[1:]
    wide = adapters * rank
    room = (units // LANES + 1) * LANES
    payload = width + LANES
    bf16 = jnp.bfloat16
    counts = [rows * part // 128 for part in PIECES]
    starts = [sum(counts[:at]) for at in range(len(counts))]
    quick = pl.CostEstimate(flops=1, bytes_accessed=1, transcendentals=0)

    def params(mib):
        return pltpu.CompilerParams(vmem_limit_bytes=mib * MIB)

    def struct(count, lanes):
        return jax.ShapeDtypeStruct((count, lanes), bf16)

    own, *pieces = pl.pallas_call(
        functools.partial(turn_kernel, starts),
        out_shape=[struct(rows, room)] + [struct(count, room) for count in counts],
        in_specs=[in_hbm(), in_hbm()],
        out_specs=[in_vmem()] * (1 + len(counts)),
        scratch_shapes=[
            pltpu.VMEM((units, rows), bf16),
            pltpu.VMEM((1, rows), jnp.int32),
            pltpu.SemaphoreType.DMA((units // LANES // TURN + 2,)),
        ],
        compiler_params=params(4),
        name="turn",
    )(left(hidden.T), left(ids.reshape(1, rows)))

    across = [(i, i ^ 2) for i in range(n_req)]
    beside = [(i, i ^ 1) for i in range(n_req)]
    next_z = [(i, i ^ 1) for i in range(n_tensor)]
    far_z = [(i, i ^ 2) for i in range(n_tensor)]

    direct = [lax.ppermute(pieces[0], "req", across)]
    other = lax.ppermute(own, "req", beside)

    shrink_rows = shrink.transpose(1, 2, 0).reshape(wide, units)
    token, *both = pl.pallas_call(
        load_kernel,
        out_shape=[jax.ShapeDtypeStruct((8, LANES), jnp.float32)]
        + [pltpu.VMEM((room, PANEL), bf16)] * (width // PANEL)
        + [pltpu.VMEM((room, wide), bf16)],
        in_specs=[in_hbm(), in_hbm()],
        out_specs=[in_vmem()] * (2 + width // PANEL),
        scratch_shapes=[
            pltpu.VMEM((wide, units), bf16),
            pltpu.SemaphoreType.DMA((width // PANEL,)),
            pltpu.SemaphoreType.DMA,
        ],
        compiler_params=params(10),
        cost_estimate=quick,
        name="load",
    )(left(weight), left(shrink_rows))

    def product(step, passed, token):
        nears = [starts[step]] if step + 1 < len(counts) else []
        nears += [starts[-1]] if step == 0 else []
        return pl.pallas_call(
            functools.partial(product_kernel, adapters, units, len(passed), nears),
            out_shape=[struct((1 + len(nears)) * counts[step], payload)] * 2,
            in_specs=[in_vmem()] * (4 + len(passed) + len(both)),
            out_specs=[in_vmem()] * 2,
            compiler_params=params(4),
            cost_estimate=quick,
            name="product",
        )(token, own, other, direct[step], *passed, *both)

    def add(step):
        last = step + 1 == len(counts)
        near_at = counts[step] * (2 if last else 1)
        return pl.pallas_call(
            functools.partial(add_kernel, near_at),
            out_shape=[struct(counts[step], payload)] * 2,
            in_specs=[in_vmem()] * 4,
            out_specs=[in_vmem()] * 2,
            compiler_params=params(4),
            cost_estimate=quick,
            name="add",
        )(*parts[0 if last else step], *parts[step])

    def over_core(part, cuts):
        tiles = room // LANES
        ends = [tiles * cut // cuts * LANES for cut in range(cuts + 1)]
        return [
            lax.ppermute(part[:, at:to], "req", beside) for at, to in zip(ends, ends[1:])
        ]

    after = lax.optimization_barrier
    steps = len(counts)
    direct[0], token = after((direct[0], token))
    parts, kept, gots = [], [], []

    def add_part(step):
        send, keep = add(step)
        kept.append(keep)
        return send

    for step in range(steps):
        passed = over_core(direct[step], CUTS[step])
        if step + 1 < steps:
            direct.append(lax.ppermute(pieces[step + 1], "req", across))
        send, keep = product(step, passed, token)
        hop = gots[step - 2 :] if step > 1 else []
        if step + 1 < steps:
            got = lax.ppermute(send, "tensor", next_z)
            direct[step + 1], keep, parts, hop = after((direct[step + 1], keep, parts, hop))
        else:
            got = lax.ppermute(send, "tensor", next_z)
        if step > 1 and step + 1 < steps:
            gots[step - 2 :] = hop
        if step > 0:
            send = add_part(step - 1)
            if step + 1 < steps:
                direct[step + 1], kept[-1] = after((direct[step + 1], kept[-1]))
            gots.append(lax.ppermute(send, "tensor", far_z))
        parts.append((keep, got))
    parts[-1], gots[-2] = after((parts[-1], gots[-2]))
    gots.append(lax.ppermute(add_part(steps - 1), "tensor", far_z))

    return pl.pallas_call(
        functools.partial(last_kernel, n_tensor, adapters),
        out_shape=struct(rows, width),
        in_specs=[in_vmem()] * (1 + 2 * steps),
        out_specs=in_vmem(),
        compiler_params=params(8),
        name="last",
    )(expand.reshape(wide, width), *kept, *gots)


def gathered(hidden, weight, shrink, expand, ids):
    rows, units = hidden.shape
    adapters, rank = shrink.shape[1:]
    width = weight.shape[1]
    columns = jnp.arange(adapters, dtype=jnp.int32)[None, :]
    onehot = (ids[:, None] == columns).astype(jnp.float32)
    every = jnp.dot(
        hidden, shrink.reshape(units, adapters * rank), preferred_element_type=jnp.float32
    )
    part = jnp.sum(every.reshape(rows, adapters, rank) * onehot[:, :, None], axis=1)
    all_ids = lax.all_gather(ids, "req", axis=0, tiled=True)
    base = jnp.dot(
        lax.all_gather(hidden, "req", axis=0, tiled=True),
        weight,
        preferred_element_type=jnp.float32,
    )
    base = lax.psum_scatter(
        base.astype(jnp.bfloat16), "tensor", scatter_dimension=0, tiled=True
    ).astype(jnp.float32)
    shrunk = lax.all_gather(
        lax.psum(part.astype(jnp.bfloat16), "tensor"), "req", axis=0, tiled=True
    )
    mine = base.shape[0]
    first = lax.axis_index("tensor") * mine
    shrunk = lax.dynamic_slice_in_dim(shrunk, first, mine, 0)
    mask = lax.dynamic_slice_in_dim(all_ids, first, mine, 0)[:, None] == columns
    placed = (shrunk[:, None, :] * mask.astype(jnp.bfloat16)[:, :, None]).reshape(
        mine, adapters * rank
    )
    adapter = jnp.dot(
        placed, expand.reshape(adapters * rank, width), preferred_element_type=jnp.float32
    )
    return (base + adapter).astype(jnp.bfloat16)


def solution(mesh):
    n_tensor, n_req = mesh.shape["tensor"], mesh.shape["req"]
    if n_tensor == 4 and n_req == 4:
        on_device = functools.partial(paired, n_tensor, n_req)
    else:
        on_device = gathered
    placed = (
        P(("rep", "req"), "tensor"),
        P("tensor", "req"),
        P("tensor", None, None),
        P(None, None, "req"),
        P(("rep", "req")),
    )
    return jax.shard_map(
        on_device,
        mesh=mesh,
        in_specs=placed,
        out_specs=P(("rep", "tensor"), "req"),
        check_vma=False,
    )
```

```python
import functools

import jax
import jax.numpy as jnp
from jax import lax
from jax.experimental import pallas as pl
from jax.experimental.pallas import tpu as pltpu
from jax.sharding import PartitionSpec as P

LANES = 128
PANEL = 512
DEPTH = 1024
TURN = 15
PIECES = (32, 32, 32, 32)
CUTS = (2, 2, 2, 1)
FULL = 128
MIB = 1 << 20


def in_vmem():
    return pl.BlockSpec(memory_space=pltpu.VMEM)


def in_hbm():
    return pl.BlockSpec(memory_space=pltpu.HBM)


def left(array):
    return pltpu.with_memory_space_constraint(array, pltpu.HBM)


def turn_kernel(starts, hidden_hbm, ids_hbm, own_ref, *refs):
    *piece_refs, hidden_ref, ids_ref, sems = refs
    units, rows = hidden_hbm.shape
    full = units // LANES
    stops = [at * LANES for at in range(0, full, TURN)] + [units]
    copies = [
        pltpu.make_async_copy(
            hidden_hbm.at[pl.ds(at, to - at)], hidden_ref.at[pl.ds(at, to - at)], sems.at[step]
        )
        for step, (at, to) in enumerate(zip(stops, stops[1:]))
    ]
    ids_copy = pltpu.make_async_copy(ids_hbm, ids_ref, sems.at[len(copies)])
    for copy in copies:
        copy.start()
    ids_copy.start()
    for step, copy in enumerate(copies):
        copy.wait()
        last = step == len(copies) - 1
        if last:
            ids_copy.wait()
        for block in range(stops[step] // LANES, full + 1 if last else stops[step + 1] // LANES):
            if block < full:
                tile = hidden_ref[block * LANES : (block + 1) * LANES, :]
            else:
                ids = jnp.broadcast_to(
                    ids_ref[...].astype(jnp.float32).astype(jnp.bfloat16),
                    ((full + 1) * LANES - units, rows),
                )
                tile = jnp.concatenate([hidden_ref[full * LANES :, :], ids], axis=0)
            turned = tile.T
            at = slice(block * LANES, (block + 1) * LANES)
            own_ref[:, at] = turned
            for first, piece_ref in zip(starts, piece_refs):
                piece_ref[:, at] = turned[first : first + piece_ref.shape[0]]


def load_kernel(w_hbm, s_hbm, token_ref, *refs):
    *panel_refs, spread_ref, s_ref, w_sems, s_sem = refs
    units = w_hbm.shape[0]
    copies = [
        pltpu.make_async_copy(
            w_hbm.at[:, pl.ds(panel * PANEL, PANEL)],
            panel_ref.at[pl.ds(0, units), :],
            w_sems.at[panel],
        )
        for panel, panel_ref in enumerate(panel_refs)
    ]
    s_copy = pltpu.make_async_copy(s_hbm, s_ref, s_sem)
    s_copy.start()
    for copy in copies:
        copy.start()
    token_ref[...] = jnp.zeros_like(token_ref)
    for ref in (spread_ref, *panel_refs):
        ref[units:, :] = jnp.zeros_like(ref[units:, :])
    s_copy.wait()
    for at in range(0, units, DEPTH):
        to = min(at + DEPTH, units)
        spread_ref[at:to, :] = s_ref[:, at:to].T
    for copy in copies:
        copy.wait()


def part_rows(rows, value, cols, outs):
    keep_first = lax.rem(lax.axis_index("req"), 2) == lax.rem(lax.axis_index("tensor"), 2)
    value = value.astype(outs[0].dtype)
    base = 0
    for send_ref, keep_ref in zip(outs[::2], outs[1::2]):
        for at in range(0, send_ref.shape[0], rows):
            first, second = value[base : base + rows], value[base + rows : base + 2 * rows]
            send_ref[at : at + rows, cols] = jnp.where(keep_first, second, first)
            keep_ref[at : at + rows, cols] = jnp.where(keep_first, first, second)
            base += 2 * rows


def product_kernel(adapters, units, cuts, nears, n_outs, _, own_ref, other_ref, direct_ref, *refs):
    passed_refs, refs = refs[:cuts], refs[cuts:]
    outs, (*panel_refs, spread_ref) = refs[-n_outs:], refs[:-n_outs]
    rows = direct_ref.shape[0]
    width = outs[0].shape[1] - LANES
    wide = spread_ref.shape[1]
    rank = wide // adapters

    def piece():
        passed = jnp.concatenate([ref[...] for ref in passed_refs], axis=1)
        whole = [direct_ref[...], passed]
        for at in nears:
            whole += [ref[at : at + rows, :] for ref in (own_ref, other_ref)]
        return jnp.concatenate(whole * max(1, FULL // (rows * len(whole))), axis=0)

    every = jnp.dot(piece(), spread_ref[...], preferred_element_type=jnp.float32)
    ids = piece()[:, units : units + 1].astype(jnp.float32)
    column = lax.broadcasted_iota(jnp.int32, every.shape, 1) // rank
    picked = jnp.where(column.astype(jnp.float32) == ids, every, 0.0)
    tile = picked[:, :LANES]
    for lane in range(LANES, wide, LANES):
        tile = tile + picked[:, lane : lane + LANES]
    tile = tile + pltpu.roll(tile, rank, 1)
    lane = lax.broadcasted_iota(jnp.int32, tile.shape, 1)
    tile = jnp.where(lane < rank, tile, ids)
    part_rows(rows, tile, slice(width, width + LANES), outs)

    for panel, panel_ref in enumerate(panel_refs):
        value = jnp.dot(
            piece(), panel_ref[...], preferred_element_type=jnp.float32
        )
        part_rows(rows, value, slice(panel * PANEL, (panel + 1) * PANEL), outs)


def add_kernel(near_at, near_a, near_b, far_a, far_b, send_ref, keep_ref):
    rows = send_ref.shape[0]
    keep_near = lax.axis_index("tensor") // 2 == lax.axis_index("req") // 2

    def total(first_ref, second_ref, at):
        cut = slice(at, at + rows)
        value = first_ref[cut].astype(jnp.float32) + second_ref[cut].astype(jnp.float32)
        return value.astype(send_ref.dtype)

    near, far = total(near_a, near_b, near_at), total(far_a, far_b, 0)
    send_ref[...] = jnp.where(keep_near, far, near)
    keep_ref[...] = jnp.where(keep_near, near, far)


def last_kernel(n_tensor, adapters, expand_ref, *refs):
    out_ref = refs[-1]
    count = (len(refs) - 1) // 2
    kept, got = refs[:count], refs[count:-1]
    wide, width = expand_ref.shape
    rank = wide // adapters

    def whole(cols):
        parts = [
            first[:, cols].astype(jnp.float32) + second[:, cols].astype(jnp.float32)
            for first, second in zip(kept, got)
        ]
        return jnp.concatenate(parts, axis=0)

    small = whole(slice(width, width + LANES))
    ids = small[:, rank : rank + 1] * (1.0 / n_tensor)
    lane = lax.broadcasted_iota(jnp.int32, small.shape, 1)
    shrink = jnp.where(lane < rank, small, 0.0)
    shrink = shrink + pltpu.roll(shrink, rank, 1)
    spread = jnp.concatenate([shrink] * (wide // LANES), axis=1)
    column = lax.broadcasted_iota(jnp.int32, spread.shape, 1) // rank
    placed = jnp.where(column.astype(jnp.float32) == ids, spread, 0.0).astype(jnp.bfloat16)
    for at in range(0, width, PANEL):
        cols = slice(at, at + PANEL)
        adapter = jnp.dot(placed, expand_ref[:, cols], preferred_element_type=jnp.float32)
        out_ref[:, cols] = (whole(cols) + adapter).astype(out_ref.dtype)


def paired(n_tensor, n_req, hidden, weight, shrink, expand, ids):
    rows, units = hidden.shape
    width = weight.shape[1]
    adapters, rank = shrink.shape[1:]
    wide = adapters * rank
    room = (units // LANES + 1) * LANES
    payload = width + LANES
    bf16 = jnp.bfloat16
    counts = [rows * part // 128 for part in PIECES]
    starts = [sum(counts[:at]) for at in range(len(counts))]
    quick = pl.CostEstimate(flops=1, bytes_accessed=1, transcendentals=0)

    def params(mib):
        return pltpu.CompilerParams(vmem_limit_bytes=mib * MIB)

    def struct(count, lanes):
        return jax.ShapeDtypeStruct((count, lanes), bf16)

    own, *pieces = pl.pallas_call(
        functools.partial(turn_kernel, starts),
        out_shape=[struct(rows, room)] + [struct(count, room) for count in counts],
        in_specs=[in_hbm(), in_hbm()],
        out_specs=[in_vmem()] * (1 + len(counts)),
        scratch_shapes=[
            pltpu.VMEM((units, rows), bf16),
            pltpu.VMEM((1, rows), jnp.int32),
            pltpu.SemaphoreType.DMA((units // LANES // TURN + 2,)),
        ],
        compiler_params=params(4),
        name="turn",
    )(left(hidden.T), left(ids.reshape(1, rows)))

    across = [(i, i ^ 2) for i in range(n_req)]
    beside = [(i, i ^ 1) for i in range(n_req)]
    next_z = [(i, i ^ 1) for i in range(n_tensor)]
    far_z = [(i, i ^ 2) for i in range(n_tensor)]

    direct = [lax.ppermute(pieces[0], "req", across)]
    other = lax.ppermute(own, "req", beside)

    shrink_rows = shrink.transpose(1, 2, 0).reshape(wide, units)
    token, *both = pl.pallas_call(
        load_kernel,
        out_shape=[jax.ShapeDtypeStruct((8, LANES), jnp.float32)]
        + [pltpu.VMEM((room, PANEL), bf16)] * (width // PANEL)
        + [pltpu.VMEM((room, wide), bf16)],
        in_specs=[in_hbm(), in_hbm()],
        out_specs=[in_vmem()] * (2 + width // PANEL),
        scratch_shapes=[
            pltpu.VMEM((wide, units), bf16),
            pltpu.SemaphoreType.DMA((width // PANEL,)),
            pltpu.SemaphoreType.DMA,
        ],
        compiler_params=params(10),
        cost_estimate=quick,
        name="load",
    )(left(weight), left(shrink_rows))

    def product(step, passed, token):
        nears = [starts[step]] if step + 1 < len(counts) else []
        shapes = [struct((1 + len(nears)) * counts[step], payload)] * 2
        if step == 0:
            nears.append(starts[-1])
            shapes += [struct(counts[step], payload)] * 2
        return pl.pallas_call(
            functools.partial(product_kernel, adapters, units, len(passed), nears, len(shapes)),
            out_shape=shapes,
            in_specs=[in_vmem()] * (4 + len(passed) + len(both)),
            out_specs=[in_vmem()] * len(shapes),
            compiler_params=params(4),
            cost_estimate=quick,
            name="product",
        )(token, own, other, direct[step], *passed, *both)

    def add(step):
        last = step + 1 == len(counts)
        near_at = 0 if last else counts[step]
        return pl.pallas_call(
            functools.partial(add_kernel, near_at),
            out_shape=[struct(counts[step], payload)] * 2,
            in_specs=[in_vmem()] * 4,
            out_specs=[in_vmem()] * 2,
            compiler_params=params(4),
            cost_estimate=quick,
            name="add",
        )(*(late if last else parts[step]), *parts[step])

    def over_core(part, cuts):
        tiles = room // LANES
        ends = [tiles * cut // cuts * LANES for cut in range(cuts + 1)]
        return [
            lax.ppermute(part[:, at:to], "req", beside) for at, to in zip(ends, ends[1:])
        ]

    after = lax.optimization_barrier
    steps = len(counts)
    direct[0], token = after((direct[0], token))
    parts, kept, gots = [], [], []

    def add_part(step):
        send, keep = add(step)
        kept.append(keep)
        return send

    for step in range(steps):
        passed = over_core(direct[step], CUTS[step])
        if step + 1 < steps:
            direct.append(lax.ppermute(pieces[step + 1], "req", across))
        send, keep, *extra = product(step, passed, token)
        if extra:
            late = (extra[1], lax.ppermute(extra[0], "tensor", next_z))
        hop = gots[step - 2 :] if step > 1 else []
        if step + 1 < steps:
            got = lax.ppermute(send, "tensor", next_z)
            direct[step + 1], keep, parts, hop = after((direct[step + 1], keep, parts, hop))
            if step + 2 == steps:
                direct[step + 1], late = after((direct[step + 1], late))
        else:
            got = lax.ppermute(send, "tensor", next_z)
        if step > 1 and step + 1 < steps:
            gots[step - 2 :] = hop
        if step > 0:
            send = add_part(step - 1)
            if step + 1 < steps:
                direct[step + 1], kept[-1] = after((direct[step + 1], kept[-1]))
            gots.append(lax.ppermute(send, "tensor", far_z))
        parts.append((keep, got))
    parts[-1], gots[-2] = after((parts[-1], gots[-2]))
    gots.append(lax.ppermute(add_part(steps - 1), "tensor", far_z))

    return pl.pallas_call(
        functools.partial(last_kernel, n_tensor, adapters),
        out_shape=struct(rows, width),
        in_specs=[in_vmem()] * (1 + 2 * steps),
        out_specs=in_vmem(),
        compiler_params=params(8),
        name="last",
    )(expand.reshape(wide, width), *kept, *gots)


def gathered(hidden, weight, shrink, expand, ids):
    rows, units = hidden.shape
    adapters, rank = shrink.shape[1:]
    width = weight.shape[1]
    columns = jnp.arange(adapters, dtype=jnp.int32)[None, :]
    onehot = (ids[:, None] == columns).astype(jnp.float32)
    every = jnp.dot(
        hidden, shrink.reshape(units, adapters * rank), preferred_element_type=jnp.float32
    )
    part = jnp.sum(every.reshape(rows, adapters, rank) * onehot[:, :, None], axis=1)
    all_ids = lax.all_gather(ids, "req", axis=0, tiled=True)
    base = jnp.dot(
        lax.all_gather(hidden, "req", axis=0, tiled=True),
        weight,
        preferred_element_type=jnp.float32,
    )
    base = lax.psum_scatter(
        base.astype(jnp.bfloat16), "tensor", scatter_dimension=0, tiled=True
    ).astype(jnp.float32)
    shrunk = lax.all_gather(
        lax.psum(part.astype(jnp.bfloat16), "tensor"), "req", axis=0, tiled=True
    )
    mine = base.shape[0]
    first = lax.axis_index("tensor") * mine
    shrunk = lax.dynamic_slice_in_dim(shrunk, first, mine, 0)
    mask = lax.dynamic_slice_in_dim(all_ids, first, mine, 0)[:, None] == columns
    placed = (shrunk[:, None, :] * mask.astype(jnp.bfloat16)[:, :, None]).reshape(
        mine, adapters * rank
    )
    adapter = jnp.dot(
        placed, expand.reshape(adapters * rank, width), preferred_element_type=jnp.float32
    )
    return (base + adapter).astype(jnp.bfloat16)


def solution(mesh):
    n_tensor, n_req = mesh.shape["tensor"], mesh.shape["req"]
    if n_tensor == 4 and n_req == 4:
        on_device = functools.partial(paired, n_tensor, n_req)
    else:
        on_device = gathered
    placed = (
        P(("rep", "req"), "tensor"),
        P("tensor", "req"),
        P("tensor", None, None),
        P(None, None, "req"),
        P(("rep", "req")),
    )
    return jax.shard_map(
        on_device,
        mesh=mesh,
        in_specs=placed,
        out_specs=P(("rep", "tensor"), "req"),
        check_vma=False,
    )
```

```python
import functools

import jax
import jax.numpy as jnp
from jax import lax
from jax.experimental import pallas as pl
from jax.experimental.pallas import tpu as pltpu
from jax.sharding import PartitionSpec as P

LANES = 128
PANEL = 512
DEPTH = 1024
TURN = 6
PIECES = (32, 32, 32, 32)
CUTS = (2, 2, 2, 1)
FULL = 128
MIB = 1 << 20


def in_vmem():
    return pl.BlockSpec(memory_space=pltpu.VMEM)


def in_hbm():
    return pl.BlockSpec(memory_space=pltpu.HBM)


def left(array):
    return pltpu.with_memory_space_constraint(array, pltpu.HBM)


def turn_kernel(starts, hidden_hbm, ids_hbm, own_ref, *refs):
    *piece_refs, hidden_ref, ids_ref, sems = refs
    units, rows = hidden_hbm.shape
    full = units // LANES
    stops = [at * LANES for at in range(0, full, TURN)] + [units]
    copies = [
        pltpu.make_async_copy(
            hidden_hbm.at[pl.ds(at, to - at)], hidden_ref.at[pl.ds(at, to - at)], sems.at[step]
        )
        for step, (at, to) in enumerate(zip(stops, stops[1:]))
    ]
    ids_copy = pltpu.make_async_copy(ids_hbm, ids_ref, sems.at[len(copies)])
    for copy in copies:
        copy.start()
    ids_copy.start()
    for step, copy in enumerate(copies):
        copy.wait()
        last = step == len(copies) - 1
        if last:
            ids_copy.wait()
        for block in range(stops[step] // LANES, full + 1 if last else stops[step + 1] // LANES):
            if block < full:
                tile = hidden_ref[block * LANES : (block + 1) * LANES, :]
            else:
                ids = jnp.broadcast_to(
                    ids_ref[...].astype(jnp.float32).astype(jnp.bfloat16),
                    ((full + 1) * LANES - units, rows),
                )
                tile = jnp.concatenate([hidden_ref[full * LANES :, :], ids], axis=0)
            turned = tile.T
            at = slice(block * LANES, (block + 1) * LANES)
            own_ref[:, at] = turned
            for first, piece_ref in zip(starts, piece_refs):
                piece_ref[:, at] = turned[first : first + piece_ref.shape[0]]


def load_kernel(w_hbm, s_hbm, token_ref, *refs):
    *panel_refs, spread_ref, s_ref, w_sems, s_sem = refs
    units = w_hbm.shape[0]
    copies = [
        pltpu.make_async_copy(
            w_hbm.at[:, pl.ds(panel * PANEL, PANEL)],
            panel_ref.at[pl.ds(0, units), :],
            w_sems.at[panel],
        )
        for panel, panel_ref in enumerate(panel_refs)
    ]
    s_copy = pltpu.make_async_copy(s_hbm, s_ref, s_sem)
    s_copy.start()
    for copy in copies:
        copy.start()
    token_ref[...] = jnp.zeros_like(token_ref)
    for ref in (spread_ref, *panel_refs):
        ref[units:, :] = jnp.zeros_like(ref[units:, :])
    s_copy.wait()
    for at in range(0, units, DEPTH):
        to = min(at + DEPTH, units)
        spread_ref[at:to, :] = s_ref[:, at:to].T
    for copy in copies:
        copy.wait()


def part_rows(rows, value, cols, send_ref, keep_ref):
    keep_first = lax.rem(lax.axis_index("req"), 2) == lax.rem(lax.axis_index("tensor"), 2)
    value = value.astype(send_ref.dtype)
    for at in range(0, send_ref.shape[0], rows):
        first, second = value[2 * at : 2 * at + rows], value[2 * at + rows : 2 * at + 2 * rows]
        send_ref[at : at + rows, cols] = jnp.where(keep_first, second, first)
        keep_ref[at : at + rows, cols] = jnp.where(keep_first, first, second)


def product_kernel(adapters, units, cuts, nears, _, own_ref, other_ref, direct_ref, *refs):
    passed_refs, refs = refs[:cuts], refs[cuts:]
    *panel_refs, spread_ref, send_ref, keep_ref = refs
    rows = direct_ref.shape[0]
    width = send_ref.shape[1] - LANES
    wide = spread_ref.shape[1]
    rank = wide // adapters

    def piece():
        passed = jnp.concatenate([ref[...] for ref in passed_refs], axis=1)
        whole = [direct_ref[...], passed]
        for at in nears:
            whole += [ref[at : at + rows, :] for ref in (own_ref, other_ref)]
        return jnp.concatenate(whole * max(1, FULL // (rows * len(whole))), axis=0)

    every = jnp.dot(piece(), spread_ref[...], preferred_element_type=jnp.float32)
    ids = piece()[:, units : units + 1].astype(jnp.float32)
    column = lax.broadcasted_iota(jnp.int32, every.shape, 1) // rank
    picked = jnp.where(column.astype(jnp.float32) == ids, every, 0.0)
    tile = picked[:, :LANES]
    for lane in range(LANES, wide, LANES):
        tile = tile + picked[:, lane : lane + LANES]
    tile = tile + pltpu.roll(tile, rank, 1)
    lane = lax.broadcasted_iota(jnp.int32, tile.shape, 1)
    tile = jnp.where(lane < rank, tile, ids)
    part_rows(rows, tile, slice(width, width + LANES), send_ref, keep_ref)

    for panel, panel_ref in enumerate(panel_refs):
        value = jnp.dot(
            piece(), panel_ref[...], preferred_element_type=jnp.float32
        )
        part_rows(rows, value, slice(panel * PANEL, (panel + 1) * PANEL), send_ref, keep_ref)


def add_kernel(near_at, near_a, near_b, far_a, far_b, send_ref, keep_ref):
    rows = send_ref.shape[0]
    keep_near = lax.axis_index("tensor") // 2 == lax.axis_index("req") // 2

    def total(first_ref, second_ref, at):
        cut = slice(at, at + rows)
        value = first_ref[cut].astype(jnp.float32) + second_ref[cut].astype(jnp.float32)
        return value.astype(send_ref.dtype)

    near, far = total(near_a, near_b, near_at), total(far_a, far_b, 0)
    send_ref[...] = jnp.where(keep_near, far, near)
    keep_ref[...] = jnp.where(keep_near, near, far)


def last_kernel(n_tensor, adapters, expand_ref, *refs):
    out_ref = refs[-1]
    count = (len(refs) - 1) // 2
    kept, got = refs[:count], refs[count:-1]
    wide, width = expand_ref.shape
    rank = wide // adapters

    def whole(cols):
        parts = [
            first[:, cols].astype(jnp.float32) + second[:, cols].astype(jnp.float32)
            for first, second in zip(kept, got)
        ]
        return jnp.concatenate(parts, axis=0)

    small = whole(slice(width, width + LANES))
    ids = small[:, rank : rank + 1] * (1.0 / n_tensor)
    lane = lax.broadcasted_iota(jnp.int32, small.shape, 1)
    shrink = jnp.where(lane < rank, small, 0.0)
    shrink = shrink + pltpu.roll(shrink, rank, 1)
    spread = jnp.concatenate([shrink] * (wide // LANES), axis=1)
    column = lax.broadcasted_iota(jnp.int32, spread.shape, 1) // rank
    placed = jnp.where(column.astype(jnp.float32) == ids, spread, 0.0).astype(jnp.bfloat16)
    for at in range(0, width, PANEL):
        cols = slice(at, at + PANEL)
        adapter = jnp.dot(placed, expand_ref[:, cols], preferred_element_type=jnp.float32)
        out_ref[:, cols] = (whole(cols) + adapter).astype(out_ref.dtype)


def paired(n_tensor, n_req, hidden, weight, shrink, expand, ids):
    rows, units = hidden.shape
    width = weight.shape[1]
    adapters, rank = shrink.shape[1:]
    wide = adapters * rank
    room = (units // LANES + 1) * LANES
    payload = width + LANES
    bf16 = jnp.bfloat16
    counts = [rows * part // 128 for part in PIECES]
    starts = [sum(counts[:at]) for at in range(len(counts))]
    quick = pl.CostEstimate(flops=1, bytes_accessed=1, transcendentals=0)

    def params(mib):
        return pltpu.CompilerParams(vmem_limit_bytes=mib * MIB)

    def struct(count, lanes):
        return jax.ShapeDtypeStruct((count, lanes), bf16)

    own, *pieces = pl.pallas_call(
        functools.partial(turn_kernel, starts),
        out_shape=[struct(rows, room)] + [struct(count, room) for count in counts],
        in_specs=[in_hbm(), in_hbm()],
        out_specs=[in_vmem()] * (1 + len(counts)),
        scratch_shapes=[
            pltpu.VMEM((units, rows), bf16),
            pltpu.VMEM((1, rows), jnp.int32),
            pltpu.SemaphoreType.DMA((units // LANES // TURN + 2,)),
        ],
        compiler_params=params(4),
        name="turn",
    )(left(hidden.T), left(ids.reshape(1, rows)))

    across = [(i, i ^ 2) for i in range(n_req)]
    beside = [(i, i ^ 1) for i in range(n_req)]
    next_z = [(i, i ^ 1) for i in range(n_tensor)]
    far_z = [(i, i ^ 2) for i in range(n_tensor)]

    direct = [lax.ppermute(pieces[0], "req", across)]
    other = lax.ppermute(own, "req", beside)

    shrink_rows = shrink.transpose(1, 2, 0).reshape(wide, units)
    token, *both = pl.pallas_call(
        load_kernel,
        out_shape=[jax.ShapeDtypeStruct((8, LANES), jnp.float32)]
        + [pltpu.VMEM((room, PANEL), bf16)] * (width // PANEL)
        + [pltpu.VMEM((room, wide), bf16)],
        in_specs=[in_hbm(), in_hbm()],
        out_specs=[in_vmem()] * (2 + width // PANEL),
        scratch_shapes=[
            pltpu.VMEM((wide, units), bf16),
            pltpu.SemaphoreType.DMA((width // PANEL,)),
            pltpu.SemaphoreType.DMA,
        ],
        compiler_params=params(10),
        cost_estimate=quick,
        name="load",
    )(left(weight), left(shrink_rows))

    def product(step, passed, token):
        nears = [starts[step]] if step + 1 < len(counts) else []
        nears += [starts[-1]] if step == 0 else []
        return pl.pallas_call(
            functools.partial(product_kernel, adapters, units, len(passed), nears),
            out_shape=[struct((1 + len(nears)) * counts[step], payload)] * 2,
            in_specs=[in_vmem()] * (4 + len(passed) + len(both)),
            out_specs=[in_vmem()] * 2,
            compiler_params=params(4),
            cost_estimate=quick,
            name="product",
        )(token, own, other, direct[step], *passed, *both)

    def add(step):
        last = step + 1 == len(counts)
        near_at = counts[step] * (2 if last else 1)
        return pl.pallas_call(
            functools.partial(add_kernel, near_at),
            out_shape=[struct(counts[step], payload)] * 2,
            in_specs=[in_vmem()] * 4,
            out_specs=[in_vmem()] * 2,
            compiler_params=params(4),
            cost_estimate=quick,
            name="add",
        )(*parts[0 if last else step], *parts[step])

    def over_core(part, cuts):
        tiles = room // LANES
        ends = [tiles * cut // cuts * LANES for cut in range(cuts + 1)]
        return [
            lax.ppermute(part[:, at:to], "req", beside) for at, to in zip(ends, ends[1:])
        ]

    after = lax.optimization_barrier
    steps = len(counts)
    direct[0], token = after((direct[0], token))
    parts, kept, gots = [], [], []

    def add_part(step):
        send, keep = add(step)
        kept.append(keep)
        return send

    for step in range(steps):
        passed = over_core(direct[step], CUTS[step])
        if step + 1 < steps:
            direct.append(lax.ppermute(pieces[step + 1], "req", across))
        send, keep = product(step, passed, token)
        hop = gots[step - 2 :] if step > 1 else []
        if step + 1 < steps:
            got = lax.ppermute(send, "tensor", next_z)
            direct[step + 1], keep, parts, hop = after((direct[step + 1], keep, parts, hop))
        else:
            got = lax.ppermute(send, "tensor", next_z)
        if step > 1 and step + 1 < steps:
            gots[step - 2 :] = hop
        if step > 0:
            send = add_part(step - 1)
            if step + 1 < steps:
                direct[step + 1], kept[-1] = after((direct[step + 1], kept[-1]))
            gots.append(lax.ppermute(send, "tensor", far_z))
        parts.append((keep, got))
    parts[-1], gots[-2] = after((parts[-1], gots[-2]))
    gots.append(lax.ppermute(add_part(steps - 1), "tensor", far_z))

    return pl.pallas_call(
        functools.partial(last_kernel, n_tensor, adapters),
        out_shape=struct(rows, width),
        in_specs=[in_vmem()] * (1 + 2 * steps),
        out_specs=in_vmem(),
        compiler_params=params(8),
        name="last",
    )(expand.reshape(wide, width), *kept, *gots)


def gathered(hidden, weight, shrink, expand, ids):
    rows, units = hidden.shape
    adapters, rank = shrink.shape[1:]
    width = weight.shape[1]
    columns = jnp.arange(adapters, dtype=jnp.int32)[None, :]
    onehot = (ids[:, None] == columns).astype(jnp.float32)
    every = jnp.dot(
        hidden, shrink.reshape(units, adapters * rank), preferred_element_type=jnp.float32
    )
    part = jnp.sum(every.reshape(rows, adapters, rank) * onehot[:, :, None], axis=1)
    all_ids = lax.all_gather(ids, "req", axis=0, tiled=True)
    base = jnp.dot(
        lax.all_gather(hidden, "req", axis=0, tiled=True),
        weight,
        preferred_element_type=jnp.float32,
    )
    base = lax.psum_scatter(
        base.astype(jnp.bfloat16), "tensor", scatter_dimension=0, tiled=True
    ).astype(jnp.float32)
    shrunk = lax.all_gather(
        lax.psum(part.astype(jnp.bfloat16), "tensor"), "req", axis=0, tiled=True
    )
    mine = base.shape[0]
    first = lax.axis_index("tensor") * mine
    shrunk = lax.dynamic_slice_in_dim(shrunk, first, mine, 0)
    mask = lax.dynamic_slice_in_dim(all_ids, first, mine, 0)[:, None] == columns
    placed = (shrunk[:, None, :] * mask.astype(jnp.bfloat16)[:, :, None]).reshape(
        mine, adapters * rank
    )
    adapter = jnp.dot(
        placed, expand.reshape(adapters * rank, width), preferred_element_type=jnp.float32
    )
    return (base + adapter).astype(jnp.bfloat16)


def solution(mesh):
    n_tensor, n_req = mesh.shape["tensor"], mesh.shape["req"]
    if n_tensor == 4 and n_req == 4:
        on_device = functools.partial(paired, n_tensor, n_req)
    else:
        on_device = gathered
    placed = (
        P(("rep", "req"), "tensor"),
        P("tensor", "req"),
        P("tensor", None, None),
        P(None, None, "req"),
        P(("rep", "req")),
    )
    return jax.shard_map(
        on_device,
        mesh=mesh,
        in_specs=placed,
        out_specs=P(("rep", "tensor"), "req"),
        check_vma=False,
    )
```
